32 devices in a mesh: ctx: 8 (over y, x, core), exp: 4 (over z).
Axes of the slice: x: 2, y: 2, z: 4, core: 2. Of those that a mesh axis runs over, the one named last changes fastest.
Arguments:
- queries: bfloat16 [4, 2048, 2048], P(None, 'ctx', 'exp'), may hold values from -12 to 12
- rotated_key_heads: bfloat16 [4, 2048, 256], P(None, 'ctx'), may hold values from -12 to 12
- value_head_rows: bfloat16 [4, 2048, 256], P(None, 'ctx'), may hold values from -6 to 6
- out_proj: bfloat16 [2048, 2048], P('exp'), may hold values from -0.59765625 to 0.59765625
- norm_gain: float32 [2048], replicated, may hold values from 0.5 to 1.5
- expert_ids: int32 [8192, 1], P(('ctx', 'exp')), may hold values from 0 to 3; in each aligned block of 256 rows (0 to 255, 256 to 511, ...) at most 128 rows name the same one
- gate_weights: float32 [8192, 1], P(('ctx', 'exp')), may hold values from 0.25 to 1
- expert_gate: bfloat16 [4, 2048, 768], P('exp'), may hold values from -0.125 to 0.125
- expert_up: bfloat16 [4, 2048, 768], P('exp'), may hold values from -0.125 to 0.125
- expert_down: bfloat16 [4, 768, 2048], P('exp'), may hold values from -0.21875 to 0.21875
- grad_out: bfloat16 [8192, 2048], P(('ctx', 'exp')), may hold values from -0.59765625 to 0.59765625
Outputs:
- layer_out: bfloat16 [8192, 2048], P(('ctx', 'exp'))
- grad_hidden: bfloat16 [8192, 2048], P(('ctx', 'exp'))
- grad_gate: float32 [4, 2048, 768], P('exp', 'ctx')
- grad_up: float32 [4, 2048, 768], P('exp', 'ctx')
- grad_down: float32 [4, 768, 2048], P('exp', None, 'ctx')
The draws below stay inside these ranges and needn't reach their ends.
Inputs may be any that keep to these rules, and one draw needn't show every extreme that they name: `expert_ids`: in the rows of one device no expert is named more than 128 times, and the experts named in one row differ from each other.
All inputs are finite; a program needn't handle non-finite values.
Results may differ from the reference program's by a relative error of at most 0.035.
Values may be sent and summed in bfloat16 or wider, within the bound.
No kernel may reach another device: no remote copies, remote signals or barrier semaphores. Data moves between devices by JAX's collectives and lax.ppermute only.
A program may use at most 128 MiB of HBM per device.

```python
import math
import jax
import jax.numpy as jnp
import numpy as np
from jax import lax

D = 2048
LOCAL_QUERY_HEADS = 16
LOCAL_KEY_HEADS = 2
HEAD_SIZE = 128
FF = 768
TOPK = 1
SEQUENCE_COUNT = 4
BLK = 256
SEQUENCE_LENGTH = 2048
TOKENS = 8192
TOK_DEV = 256
EXPERTS = 4
CAP = 128
N_CTX = 8
N_EXP = 4


def draw_queries(key, part):
    key = jax.random.fold_in(key, 3)
    value_entries = jnp.clip(jax.random.normal(key, (SEQUENCE_COUNT, SEQUENCE_LENGTH, LOCAL_QUERY_HEADS * HEAD_SIZE), jnp.float32), -6.0, 6.0)
    return value_entries.astype(jnp.bfloat16)


def draw_rotated_key_heads(key, part):
    key = jax.random.fold_in(key, 5)
    value_entries = jnp.clip(jax.random.normal(key, (SEQUENCE_COUNT, SEQUENCE_LENGTH, LOCAL_KEY_HEADS * HEAD_SIZE), jnp.float32), -6.0, 6.0)
    return value_entries.astype(jnp.bfloat16)


def strengthened(entries, key, source, target, parts, factor):
    owner, partner = [(jnp.arange(entries.shape[axis_at]) // (entries.shape[axis_at] // parts)).reshape([-1 if axis == axis_at else 1 for axis in range(entries.ndim)]) for axis_at in (source, target)]
    chosen = jax.random.permutation(key, parts)[partner]
    strong = (owner == chosen) | (owner == (partner + parts // 2) % parts)
    return jnp.where(strong, factor * entries, entries)


def block_levels(own_key, dims, pieces, low, top_value):
    factor_of, own = 1.0, jax.random.fold_in(own_key, 6)
    for axis_at, parts in pieces:
        heights = jnp.exp(jax.random.uniform(jax.random.fold_in(own, axis_at), (parts,), jnp.float32, low / len(pieces), top_value / len(pieces)))
        factor_of = factor_of * jnp.repeat(heights, dims[axis_at] // parts).reshape([-1 if axis == axis_at else 1 for axis in range(len(dims))])
    return factor_of


def assign_block(rng, own, number, rows, count, top, bound, slope):
    sequence = jax.random.permutation(rng, count)
    heavy_load, ordinary = portions_of(count, rows * top, bound, slope, True), portions_of(count, rows * top, bound, slope, False)
    places = jnp.arange(count)

    def named(tallies, offset_by):
        used = int((tallies > 0).sum())
        fixed = max(1, used // 4)
        moved = fixed + (places - fixed + offset_by * (used - fixed)) % max(1, count - fixed)
        return jnp.zeros((count,), jnp.int32).at[sequence[jnp.where(places < fixed, places, moved)]].set(jnp.asarray(tallies, jnp.int32))

    tallies = jnp.where(number % 4 == 0, named(heavy_load, number // 4), named(ordinary, number - number // 4 - 1))
    mixed = jax.random.permutation(jax.random.fold_in(own, 3), count)
    giver, sink = mixed[0:count // 2 * 2:2], mixed[1:count // 2 * 2:2]
    margin = jnp.minimum(tallies[giver] - 1, bound - tallies[sink]) // 2
    margin = jnp.where((giver == sequence[0]) | (sink == sequence[0]) | (tallies[sink] == 0), 0, jnp.maximum(margin, 0))
    moved = jax.random.randint(jax.random.fold_in(own, 4), (count // 2,), 0, 1 << 20) % (margin + 1)
    tallies = tallies.at[giver].add(-moved).at[sink].add(moved)
    items = jnp.searchsorted(jnp.cumsum(tallies), jnp.arange(rows * top), side="right").astype(jnp.int32)
    table = items.reshape(top, rows).T
    table = table[jax.random.permutation(jax.random.fold_in(own, 1), rows)]
    offset_by = jax.random.randint(jax.random.fold_in(own, 2), (rows, 1), 0, top)
    return jnp.take_along_axis(table, (jnp.arange(top)[None, :] + offset_by) % top, axis=1)


def portions_of(count, total, most, slope, full):
    weights = [(1 << 20) // math.isqrt(rank ** slope) + 1 for rank in range(1, count + 1)]
    largest = most if full else min(most, max(-(-total // count), total * weights[0] // sum(weights)))
    least = 1 if total - largest >= count - 1 else 0
    counts, spare = [largest] + [least] * (count - 1), total - largest - least * (count - 1)
    while spare > 0:
        movable = [i for i in range(1, count) if counts[i] < largest] or [i for i in range(1, count) if counts[i] < most]
        pool, remaining = sum([weights[i] for i in movable]), spare
        for i in movable:
            addition = min(most - counts[i], max(1, remaining * weights[i] // pool), spare)
            counts[i] = counts[i] + addition
            spare = spare - addition
    return np.array(counts)


def gaussian(own_key, dims, width, bound, cuts=(), held_as=jnp.bfloat16):
    level = block_levels(own_key, dims, cuts, -0.22, 0.18) if cuts else 1.0
    values = jax.random.normal(own_key, dims, jnp.float32) * width * level
    return jnp.minimum(jnp.maximum(values, -bound), bound).astype(held_as)


def bell_draw_with(key, dims, width, limit, shards, heavy, kind=jnp.bfloat16):
    drawn = width * jax.random.normal(key, dims, jnp.float32)
    if shards:
        drawn = drawn * block_levels(key, dims, shards, -0.22, 0.18)
    return jnp.clip(strengthened(drawn, jax.random.fold_in(key, 3), *heavy), -limit, limit).astype(kind)


def setup_inputs(seed: int = 0) -> dict:
    splits = jax.random.split(jax.random.key(seed), 12)
    queries = draw_queries(jax.random.fold_in(splits[11], 71), 0)
    rotated_key_heads = draw_rotated_key_heads(jax.random.fold_in(splits[11], 71), 0)
    value_head_rows = gaussian(splits[2], (SEQUENCE_COUNT, SEQUENCE_LENGTH, LOCAL_KEY_HEADS * HEAD_SIZE), 1.0, 6.0, ((1, 8),))
    out_proj = gaussian(splits[3], (LOCAL_QUERY_HEADS * HEAD_SIZE, D), 0.1, 0.59765625, ((0, 4),))
    norm_gain = jnp.clip(1.0 + 0.1 * jax.random.normal(splits[4], (D,), jnp.float32), 0.5, 1.5)
    expert_ids_keys = jax.random.split(jax.random.fold_in(splits[5], 1), TOKENS // TOK_DEV)
    expert_ids_turns = jax.random.permutation(jax.random.fold_in(splits[5], 3), TOKENS // TOK_DEV)
    expert_ids = jax.vmap(lambda own, number: assign_block(jax.random.fold_in(splits[5], 2), own, number, TOK_DEV, EXPERTS, TOPK, CAP, 2))(expert_ids_keys, expert_ids_turns).reshape((TOKENS, TOPK))
    gate_weights = jnp.clip(0.25 + 0.75 * jax.random.uniform(splits[6], (TOKENS, TOPK), jnp.float32) ** block_levels(splits[6], (TOKENS, TOPK), ((0, 32),), -0.2, 0.2), 0.25, 1.0)
    expert_gate = gaussian(splits[7], (EXPERTS, D, FF), D ** -0.5, 0.125, ((0, 4),))
    expert_up = gaussian(splits[8], (EXPERTS, D, FF), D ** -0.5, 0.125, ((0, 4),))
    expert_down = gaussian(splits[9], (EXPERTS, FF, D), FF ** -0.5, 0.21875, ((0, 4),))
    grad_out = bell_draw_with(splits[10], (TOKENS, D), 0.1, 0.59765625, ((0, 32),), (0, 1, 32, 2.75))
    return {"queries": queries, "rotated_key_heads": rotated_key_heads, "value_head_rows": value_head_rows, "out_proj": out_proj, "norm_gain": norm_gain, "expert_ids": expert_ids, "gate_weights": gate_weights, "expert_gate": expert_gate, "expert_up": expert_up, "expert_down": expert_down, "grad_out": grad_out}


epsilon = 1e-06
masked_score = -1e+30

def attend_head(trio):
    query_rows, key_rows, value_rows = trio
    positions = jnp.arange(query_rows.shape[0], dtype=jnp.int32)
    allowed = positions[None, :] <= positions[:, None]
    scores = jnp.dot(query_rows, key_rows.T, preferred_element_type=jnp.float32) * (1.0 / math.sqrt(HEAD_SIZE))
    scores = jnp.where(allowed, scores, masked_score)
    row_best = lax.optimization_barrier(jnp.max(scores, axis=1, keepdims=True))
    weights = jnp.where(allowed, jnp.exp(scores - row_best), 0.0)
    totals = lax.optimization_barrier(jnp.sum(weights, axis=1, keepdims=True))
    blended = jnp.dot(weights.astype(jnp.bfloat16), value_rows, preferred_element_type=jnp.float32)
    return (blended / totals).astype(jnp.bfloat16)

def block_tables(block_ids, block_gates):
    flat_ids = block_ids.reshape(-1).astype(jnp.int32)
    chosen = (flat_ids[:, None] == jnp.arange(EXPERTS, dtype=jnp.int32)[None, :]).astype(jnp.int32)
    earlier = jnp.cumsum(chosen, axis=0) - chosen
    target = flat_ids * CAP + lax.optimization_barrier(jnp.sum(earlier * chosen, axis=1))
    placed = (jnp.arange(EXPERTS * CAP, dtype=jnp.int32)[:, None] == target[None, :]).reshape(EXPERTS * CAP, TOK_DEV, TOPK)
    selector = jnp.any(placed, axis=2).astype(jnp.bfloat16)
    weighting = lax.optimization_barrier(jnp.sum(jnp.where(placed, block_gates[None, :, :], 0.0), axis=2))
    return (selector, weighting)

def round_sum(partials):
    rounded = lax.optimization_barrier(partials.astype(jnp.bfloat16))
    return lax.optimization_barrier(jnp.sum(rounded.astype(jnp.float32), axis=0))

def expert_pass(item):
    arrived, cotangent, gate_mat, up_mat, down_mat = item
    arrived_f = arrived.astype(jnp.float32)
    gate_f = gate_mat.astype(jnp.float32)
    up_f = up_mat.astype(jnp.float32)
    down_f = down_mat.astype(jnp.float32)
    gate_act = jnp.einsum('csd,df->csf', arrived_f, gate_f)
    up_act = jnp.einsum('csd,df->csf', arrived_f, up_f)
    sigma = jax.nn.sigmoid(gate_act)
    gated = gate_act * sigma
    hidden_units = (gated * up_act).astype(jnp.bfloat16)
    result = jnp.einsum('csf,fd->csd', hidden_units.astype(jnp.float32), down_f).astype(jnp.bfloat16)
    cotangent_f = cotangent.astype(jnp.float32)
    back_units = jnp.einsum('csd,fd->csf', cotangent_f, down_f)
    back_gate = (back_units * up_act * sigma * (1.0 + gate_act * (1.0 - sigma))).astype(jnp.bfloat16)
    back_up = (back_units * gated).astype(jnp.bfloat16)
    back_in = (jnp.einsum('csf,df->csd', back_gate.astype(jnp.float32), gate_f) + jnp.einsum('csf,df->csd', back_up.astype(jnp.float32), up_f)).astype(jnp.bfloat16)
    grad_gate_part = round_sum(jnp.einsum('csd,csf->cdf', arrived_f, back_gate.astype(jnp.float32)))
    grad_up_part = round_sum(jnp.einsum('csd,csf->cdf', arrived_f, back_up.astype(jnp.float32)))
    grad_down_part = round_sum(jnp.einsum('csf,csd->cfd', hidden_units.astype(jnp.float32), cotangent_f))
    return (result, back_in, grad_gate_part, grad_up_part, grad_down_part)

def reference(queries, rotated_key_heads, value_head_rows, out_proj, norm_gain, expert_ids, gate_weights, expert_gate, expert_up, expert_down, grad_out):
    query_group_width = LOCAL_QUERY_HEADS // LOCAL_KEY_HEADS
    query_all = queries.reshape(SEQUENCE_COUNT, SEQUENCE_LENGTH, LOCAL_QUERY_HEADS, HEAD_SIZE).transpose(0, 2, 1, 3).reshape(SEQUENCE_COUNT * LOCAL_QUERY_HEADS, SEQUENCE_LENGTH, HEAD_SIZE)
    gathered_keys = jnp.repeat(rotated_key_heads.reshape(SEQUENCE_COUNT, SEQUENCE_LENGTH, LOCAL_KEY_HEADS, HEAD_SIZE).transpose(0, 2, 1, 3), query_group_width, axis=1).reshape(SEQUENCE_COUNT * LOCAL_QUERY_HEADS, SEQUENCE_LENGTH, HEAD_SIZE)
    gathered_values = jnp.repeat(value_head_rows.reshape(SEQUENCE_COUNT, SEQUENCE_LENGTH, LOCAL_KEY_HEADS, HEAD_SIZE).transpose(0, 2, 1, 3), query_group_width, axis=1).reshape(SEQUENCE_COUNT * LOCAL_QUERY_HEADS, SEQUENCE_LENGTH, HEAD_SIZE)
    attended = lax.map(attend_head, (query_all, gathered_keys, gathered_values))
    attended = attended.reshape(SEQUENCE_COUNT, LOCAL_QUERY_HEADS, SEQUENCE_LENGTH, HEAD_SIZE).transpose(0, 2, 1, 3).reshape(SEQUENCE_COUNT * SEQUENCE_LENGTH, LOCAL_QUERY_HEADS * HEAD_SIZE)
    group_cols = LOCAL_QUERY_HEADS // N_EXP * HEAD_SIZE
    hidden_sum = jnp.zeros((SEQUENCE_COUNT * SEQUENCE_LENGTH, D), jnp.float32)
    for group_index in range(N_EXP):
        part_term = jnp.dot(attended[:, group_index * group_cols:(group_index + 1) * group_cols], out_proj[group_index * group_cols:(group_index + 1) * group_cols], preferred_element_type=jnp.float32)
        rounded = lax.optimization_barrier(part_term.astype(jnp.bfloat16))
        hidden_sum = hidden_sum + rounded.astype(jnp.float32)
    hidden = hidden_sum.astype(jnp.bfloat16).reshape(SEQUENCE_COUNT, N_CTX, BLK, D).transpose(1, 0, 2, 3).reshape(TOKENS, D)
    hidden_f = hidden.astype(jnp.float32)
    inv_rms = lax.rsqrt(lax.optimization_barrier(jnp.mean(hidden_f * hidden_f, axis=1, keepdims=True)) + epsilon)
    unit = hidden_f * inv_rms
    normed = (unit * norm_gain).astype(jnp.bfloat16)
    block_count = TOKENS // TOK_DEV
    selector, weighting = jax.vmap(block_tables)(expert_ids.reshape(block_count, TOK_DEV, TOPK), gate_weights.reshape(block_count, TOK_DEV, TOPK))
    send_rows = jnp.einsum('bst,btd->bsd', selector.astype(jnp.float32), normed.reshape(block_count, TOK_DEV, D).astype(jnp.float32)).astype(jnp.bfloat16)
    send_grads = jnp.einsum('bst,btd->bsd', weighting, grad_out.reshape(block_count, TOK_DEV, D).astype(jnp.float32), precision=lax.Precision.HIGHEST).astype(jnp.bfloat16)
    per_expert_rows = send_rows.reshape(N_CTX, N_EXP, EXPERTS, CAP, D).transpose(2, 0, 1, 3, 4).reshape(EXPERTS, N_CTX, N_EXP * CAP, D)
    per_expert_grads = send_grads.reshape(N_CTX, N_EXP, EXPERTS, CAP, D).transpose(2, 0, 1, 3, 4).reshape(EXPERTS, N_CTX, N_EXP * CAP, D)
    result, back_in, grad_gate, grad_up, grad_down = lax.map(expert_pass, (per_expert_rows, per_expert_grads, expert_gate, expert_up, expert_down))
    result = result.reshape(EXPERTS, N_CTX, N_EXP, CAP, D).transpose(1, 2, 0, 3, 4).reshape(block_count, EXPERTS * CAP, D)
    back_in = back_in.reshape(EXPERTS, N_CTX, N_EXP, CAP, D).transpose(1, 2, 0, 3, 4).reshape(block_count, EXPERTS * CAP, D)
    expert_sum = jnp.einsum('bst,bsd->btd', weighting, result.astype(jnp.float32), precision=lax.Precision.HIGHEST).reshape(TOKENS, D)
    layer_out = (hidden_f + expert_sum).astype(jnp.bfloat16)
    back_normed = jnp.einsum('bst,bsd->btd', selector.astype(jnp.float32), back_in.astype(jnp.float32)).reshape(TOKENS, D)
    scaled_back = back_normed * norm_gain
    grad_hidden = (grad_out.astype(jnp.float32) + inv_rms * (scaled_back - unit * lax.optimization_barrier(jnp.mean(scaled_back * unit, axis=1, keepdims=True)))).astype(jnp.bfloat16)
    return (layer_out, grad_hidden, grad_gate, grad_up, grad_down)
```

```python
import functools
import math

import jax
import jax.numpy as jnp
from jax import lax
from jax.experimental import pallas as pl
from jax.experimental.pallas import tpu as pltpu
from jax.sharding import PartitionSpec as P

LOCAL_QUERY_HEADS = 16
LOCAL_KEY_HEADS = 2
HEAD_SIZE = 128
PIECE = 256
PARTS = 2

epsilon = 1e-06
masked_score = -1e30
F32 = jnp.float32
BF16 = jnp.bfloat16
MIB = 1 << 20


def dot(a, b, contract=((1,), (0,))):
    return lax.dot_general(a, b, (contract, ((), ())), preferred_element_type=F32)


def iota(shape, dim):
    return lax.broadcasted_iota(jnp.int32, shape, dim)


def slots_row(ids_row, capacity):
    n = ids_row.shape[1]
    names = iota((16, n), 0).astype(F32)
    chosen = names == ids_row
    before = (iota((n, n), 0) < iota((n, n), 1)).astype(F32).astype(BF16)
    earlier = dot(jnp.where(chosen, 1.0, 0.0).astype(BF16), before)
    return jnp.sum(jnp.where(chosen, earlier + names * capacity, 0.0), axis=0, keepdims=True)


def slots_column(ids_column, capacity):
    n = ids_column.shape[0]
    names = iota((n, 128), 1).astype(F32)
    chosen = names == ids_column
    before = (iota((n, n), 1) < iota((n, n), 0)).astype(F32).astype(BF16)
    earlier = dot(before, jnp.where(chosen, 1.0, 0.0).astype(BF16))
    return jnp.sum(jnp.where(chosen, earlier + names * capacity, 0.0), axis=1, keepdims=True)


def one_hot(matches):
    return jnp.where(matches, 1.0, 0.0).astype(BF16)


def attend_kernel(experts, capacity, heads, ctx_ref, q_ref, k_ref, v_ref, ids_ref, *rest):
    out_refs, att_scr = rest[:PARTS], rest[PARTS]
    ctx = ctx_ref[0]
    block = q_ref.shape[1]
    rows = heads * block
    factor = math.log2(math.e) / math.sqrt(HEAD_SIZE)
    q = jnp.concatenate(
        [q_ref[0, :, h * HEAD_SIZE : (h + 1) * HEAD_SIZE] for h in range(heads)], axis=0
    )

    def scores(m):
        return dot(q, k_ref[m, 0], ((1,), (1,))) * factor

    q_pos = lax.rem(iota((rows, block), 0), block)
    s = jnp.where(iota((rows, block), 1) <= q_pos, scores(0), masked_score)
    best = jnp.max(s, axis=1, keepdims=True)
    p = jnp.exp2(s - best)
    total = jnp.sum(p, axis=1, keepdims=True)
    acc = dot(p.astype(BF16), v_ref[0, 0])

    def fold(j, state):
        best, total, acc = state
        m = jnp.bitwise_xor(j, ctx)
        s = scores(m)
        new_best = jnp.maximum(best, jnp.max(s, axis=1, keepdims=True))
        p = jnp.exp2(s - new_best)
        scale = jnp.exp2(best - new_best)
        total = total * scale + jnp.sum(p, axis=1, keepdims=True)
        acc = acc * scale + dot(p.astype(BF16), v_ref[m, 0])
        return new_best, total, acc

    best, total, acc = lax.fori_loop(0, ctx, fold, (best, total, acc))
    att = (acc / total).astype(BF16)
    for h in range(heads):
        att_scr[:, h * HEAD_SIZE : (h + 1) * HEAD_SIZE] = att[h * block : (h + 1) * block]

    n = ids_ref.shape[2]
    part = capacity // PARTS
    for b in range(block // n):
        target = slots_row(ids_ref[b], capacity)
        pick = one_hot(iota((experts * capacity, n), 0).astype(F32) == target)
        picked = dot(pick, att_scr[b * n : (b + 1) * n, :]).astype(BF16)
        for e in range(experts):
            for c in range(PARTS):
                first = e * capacity + c * part
                out_refs[c][e, b] = picked[first : first + part]


def attend(ctx, queries, keys, values, ids, experts, capacity):
    seqs, block, width = queries.shape
    n_ctx = keys.shape[0]
    blocks, _, n = ids.shape
    per_seq = block // n
    heads = width // HEAD_SIZE
    part = capacity // PARTS
    return pl.pallas_call(
        functools.partial(attend_kernel, experts, capacity, heads),
        grid_spec=pltpu.PrefetchScalarGridSpec(
            num_scalar_prefetch=1,
            grid=(seqs,),
            in_specs=[
                pl.BlockSpec((1, block, width), lambda s, c: (s, 0, 0)),
                pl.BlockSpec((n_ctx, 1, block, HEAD_SIZE), lambda s, c: (0, s, 0, 0)),
                pl.BlockSpec((n_ctx, 1, block, HEAD_SIZE), lambda s, c: (0, s, 0, 0)),
                pl.BlockSpec((per_seq, 1, n), lambda s, c: (s, 0, 0)),
            ],
            out_specs=[
                pl.BlockSpec((experts, per_seq, part, width), lambda s, c: (0, s, 0, 0))
                for _ in range(PARTS)
            ],
            scratch_shapes=[pltpu.VMEM((block, width), BF16)],
        ),
        out_shape=[
            jax.ShapeDtypeStruct((experts, blocks, part, width), BF16) for _ in range(PARTS)
        ],
        compiler_params=pltpu.CompilerParams(vmem_limit_bytes=48 * MIB),
        cost_estimate=pl.CostEstimate(
            flops=4 * seqs * block * block * n_ctx * width // 2,
            bytes_accessed=8 * MIB,
            transcendentals=seqs * heads * block * block * n_ctx,
        ),
        name="attend",
    )(ctx, queries, keys, values, ids)


def place_kernel(experts, capacity, ids_ref, rows_ref, out_ref):
    n = rows_ref.shape[0]
    target = slots_row(ids_ref[...], capacity)
    pick = one_hot(iota((experts * capacity, n), 0).astype(F32) == target)
    picked = dot(pick, rows_ref[...]).astype(BF16)
    for e in range(experts):
        out_ref[e] = picked[e * capacity : (e + 1) * capacity]


def place(ids_row, rows, experts, capacity):
    n, width = rows.shape
    cols = min(width, 512)
    return pl.pallas_call(
        functools.partial(place_kernel, experts, capacity),
        grid=(width // cols,),
        in_specs=[
            pl.BlockSpec((1, n), lambda i: (0, 0)),
            pl.BlockSpec((n, cols), lambda i: (0, i)),
        ],
        out_specs=pl.BlockSpec((experts, capacity, cols), lambda i: (0, 0, i)),
        out_shape=jax.ShapeDtypeStruct((experts, capacity, width), BF16),
        compiler_params=pltpu.CompilerParams(vmem_limit_bytes=32 * MIB),
        name="place",
    )(ids_row, rows)


def restore_kernel(experts, capacity, ids_ref, *refs):
    parts, out_ref = refs[:-1], refs[-1]
    n = out_ref.shape[0]
    part = capacity // len(parts)
    target = slots_column(ids_ref[...], capacity)
    expert = jnp.floor(target / capacity)
    local = target - expert * capacity
    lane = iota((n, experts * part), 1)
    total = jnp.zeros(out_ref.shape, F32)
    for c, ref in enumerate(parts):
        where_to = jnp.where(
            (local >= c * part) & (local < (c + 1) * part),
            expert * part + local - c * part,
            -1.0,
        )
        pick = one_hot(lane.astype(F32) == where_to)
        total += dot(pick, ref[...].reshape(experts * part, -1))
    out_ref[...] = total.astype(BF16)


def restore(ids_column, parts, capacity):
    experts, part, width = parts[0].shape
    n = ids_column.shape[0]
    cols = min(width, 512)
    return pl.pallas_call(
        functools.partial(restore_kernel, experts, capacity),
        grid=(width // cols,),
        in_specs=[pl.BlockSpec((n, 1), lambda i: (0, 0))]
        + [pl.BlockSpec((experts, part, cols), lambda i: (0, 0, i)) for _ in parts],
        out_specs=pl.BlockSpec((n, cols), lambda i: (0, i)),
        out_shape=jax.ShapeDtypeStruct((n, width), BF16),
        compiler_params=pltpu.CompilerParams(vmem_limit_bytes=32 * MIB),
        name="restore",
    )(ids_column, *parts)


def expert_kernel(
    pieces,
    tiles,
    capacity,
    part_index,
    place_ref,
    att_ref,
    wa_ref,
    wb_ref,
    gain_ref,
    ids_ref,
    weight_ref,
    grad_ref,
    gate_ref,
    up_ref,
    down_ref,
    layer_ref,
    grad_hidden_ref,
    normed_ref,
    back_ref,
    units_ref,
    back_gate_ref,
    back_up_ref,
    hidden_scr,
    inv_scr,
    weight_scr,
    result_scr,
    back_in_scr,
):
    step = pl.program_id(0)
    sources, blocks, part, att_cols = att_ref.shape
    rows = blocks * part
    width = hidden_scr.shape[1]
    piece = width // pieces

    @pl.when(step < pieces)
    def _():
        total = jnp.zeros((rows, piece), F32)
        half = wa_ref.shape[1]
        for z in range(sources):
            first = z * att_cols
            source = wa_ref if first < half else wb_ref
            first = first % half
            total += dot(
                att_ref[z].reshape(rows, att_cols), source[0, first : first + att_cols, :]
            )
        column = jnp.bitwise_xor(step, place_ref[0]) * piece
        hidden_scr[:, pl.ds(pl.multiple_of(column, piece), piece)] = total.astype(BF16)

    @pl.when(step == pieces)
    def _():
        n = ids_ref.shape[2]
        owner = place_ref[1]
        weights = []
        for s in range(blocks):
            target = slots_row(ids_ref[s], capacity)
            slot = iota((part, n), 0) + (owner * capacity + part_index * part)
            weights.append(
                jnp.sum(
                    jnp.where(slot.astype(F32) == target, weight_ref[s], 0.0),
                    axis=1,
                    keepdims=True,
                )
            )
        weight = jnp.concatenate(weights, axis=0)
        weight_scr[...] = weight
        hidden = hidden_scr[...].astype(F32)
        inv = lax.rsqrt(jnp.mean(hidden * hidden, axis=1, keepdims=True) + epsilon)
        inv_scr[...] = inv
        normed_ref[...] = (hidden * inv * gain_ref[...]).astype(BF16)
        grads = grad_ref[...].reshape(rows, width).astype(F32)
        back_ref[...] = (weight * grads).astype(BF16)

    @pl.when(step >= pieces)
    def _():
        normed = normed_ref[...]
        back = back_ref[...]
        gate, up, down = gate_ref[0], up_ref[0], down_ref[0]
        gate_act = dot(normed, gate)
        up_act = dot(normed, up)
        back_units = dot(back, down, ((1,), (1,)))
        sigma = 1.0 / (1.0 + jnp.exp(-gate_act))
        gated = gate_act * sigma
        units = (gated * up_act).astype(BF16)
        back_gate = (back_units * up_act * sigma * (1.0 + gate_act * (1.0 - sigma))).astype(BF16)
        back_up = (back_units * gated).astype(BF16)
        units_ref[...] = units
        back_gate_ref[...] = back_gate
        back_up_ref[...] = back_up
        result = dot(units, down)
        back_in = dot(back_gate, gate, ((1,), (1,))) + dot(back_up, up, ((1,), (1,)))

        @pl.when(step == pieces)
        def _():
            result_scr[...] = result
            back_in_scr[...] = back_in

        @pl.when(step > pieces)
        def _():
            result_scr[...] += result
            back_in_scr[...] += back_in

    @pl.when(step == pieces + tiles - 1)
    def _():
        hidden = hidden_scr[...].astype(F32)
        inv = inv_scr[...]
        result = result_scr[...].astype(BF16).astype(F32)
        layer = hidden + weight_scr[...] * result
        layer_ref[...] = layer.astype(BF16).reshape(layer_ref.shape)
        scaled = back_in_scr[...].astype(BF16).astype(F32) * gain_ref[...]
        unit = hidden * inv
        mean = jnp.mean(scaled * unit, axis=1, keepdims=True)
        grads = grad_ref[...].reshape(rows, width).astype(F32)
        grad_hidden = grads + inv * (scaled - unit * mean)
        grad_hidden_ref[...] = grad_hidden.astype(BF16).reshape(grad_hidden_ref.shape)


def expert_part(place_of, att, wa, wb, gain, ids, weights, grads, gate, up, down, capacity, index):
    sources, blocks, part, att_cols = att.shape
    pieces, half, piece = wa.shape
    width = grads.shape[2]
    ff = gate.shape[2]
    tile = 256
    tiles = ff // tile
    rows = blocks * part
    n = ids.shape[2]
    whole = lambda *shape: pl.BlockSpec(shape, lambda i, p: (0,) * len(shape))
    tile_at = lambda i: jnp.maximum(i - pieces, 0)
    out = lambda *shape: jax.ShapeDtypeStruct(shape, BF16)
    return pl.pallas_call(
        functools.partial(expert_kernel, pieces, tiles, capacity, index),
        grid_spec=pltpu.PrefetchScalarGridSpec(
            num_scalar_prefetch=1,
            grid=(pieces + tiles,),
            in_specs=[
                whole(sources, blocks, part, att_cols),
                pl.BlockSpec((1, half, piece), lambda i, p: (jnp.minimum(i, pieces - 1), 0, 0)),
                pl.BlockSpec((1, half, piece), lambda i, p: (jnp.minimum(i, pieces - 1), 0, 0)),
                whole(1, width),
                whole(blocks, 1, n),
                whole(blocks, 1, n),
                pl.BlockSpec((blocks, part, width), lambda i, p: (0, index, 0)),
                pl.BlockSpec((1, width, tile), lambda i, p: (0, 0, tile_at(i))),
                pl.BlockSpec((1, width, tile), lambda i, p: (0, 0, tile_at(i))),
                pl.BlockSpec((1, tile, width), lambda i, p: (0, tile_at(i), 0)),
            ],
            out_specs=[
                whole(blocks, part, width),
                whole(blocks, part, width),
                whole(rows, width),
                whole(rows, width),
                pl.BlockSpec((rows, tile), lambda i, p: (0, tile_at(i))),
                pl.BlockSpec((rows, tile), lambda i, p: (0, tile_at(i))),
                pl.BlockSpec((rows, tile), lambda i, p: (0, tile_at(i))),
            ],
            scratch_shapes=[
                pltpu.VMEM((rows, width), BF16),
                pltpu.VMEM((rows, 1), F32),
                pltpu.VMEM((rows, 1), F32),
                pltpu.VMEM((rows, width), F32),
                pltpu.VMEM((rows, width), F32),
            ],
        ),
        out_shape=[
            out(blocks, part, width),
            out(blocks, part, width),
            out(rows, width),
            out(rows, width),
            out(rows, ff),
            out(rows, ff),
            out(rows, ff),
        ],
        compiler_params=pltpu.CompilerParams(vmem_limit_bytes=56 * MIB),
        cost_estimate=pl.CostEstimate(
            flops=2 * rows * width * (width + 6 * ff),
            bytes_accessed=2 * (width * width + 3 * width * ff + 8 * rows * width),
            transcendentals=rows * ff,
        ),
        name="expert",
    )(place_of, att, wa, wb, gain, ids, weights, grads, gate, up, down)


def weight_kernel(count, *refs):
    normed, back, units, back_gate, back_up = [refs[i * count : (i + 1) * count] for i in range(5)]
    gate_ref, up_ref, down_ref = refs[5 * count :]
    first = ((0,), (0,))
    gate = up = down = 0.0
    for c in range(count):
        gate += dot(normed[c][...], back_gate[c][...], first)
        up += dot(normed[c][...], back_up[c][...], first)
        down += dot(units[c][...], back[c][...], first)
    gate_ref[...] = gate.astype(BF16)
    up_ref[...] = up.astype(BF16)
    down_ref[0] = down.astype(BF16)


def weight_parts(normed, back, units, back_gate, back_up):
    count = len(normed)
    rows, width = normed[0].shape
    ff = units[0].shape[1]
    cols = PIECE
    thin = [pl.BlockSpec((rows, cols), lambda i: (0, i))] * count
    full = [pl.BlockSpec((rows, ff), lambda i: (0, 0))] * count
    return pl.pallas_call(
        functools.partial(weight_kernel, count),
        grid=(width // cols,),
        in_specs=thin + thin + full + full + full,
        out_specs=[
            pl.BlockSpec((cols, ff), lambda i: (i, 0)),
            pl.BlockSpec((cols, ff), lambda i: (i, 0)),
            pl.BlockSpec((1, ff, cols), lambda i: (i, 0, 0)),
        ],
        out_shape=[
            jax.ShapeDtypeStruct((width, ff), BF16),
            jax.ShapeDtypeStruct((width, ff), BF16),
            jax.ShapeDtypeStruct((width // cols, ff, cols), BF16),
        ],
        compiler_params=pltpu.CompilerParams(vmem_limit_bytes=40 * MIB),
        cost_estimate=pl.CostEstimate(
            flops=6 * count * rows * width * ff,
            bytes_accessed=2 * (3 * width * ff + 2 * count * rows * (width + 2 * ff)),
            transcendentals=0,
        ),
        name="weight_grads",
    )(*normed, *back, *units, *back_gate, *back_up)


def partner(axis_name, value, bit):
    count = lax.axis_size(axis_name)
    return lax.ppermute(value, axis_name, [(i, i ^ (1 << bit)) for i in range(count)])


def doubled(value, bits, order):
    shape = value.shape
    held = value.reshape((1,) * bits + shape)
    for bit in order:
        other = partner("ctx", held, bit)
        held = jnp.concatenate([held, other], axis=bits - 1 - bit)
    return held.reshape((1 << bits,) + shape)


def halved(value, bits, order, ctx):
    shape = value.shape[1:]
    held = value.reshape((2,) * bits + shape)
    for place_in_order, bit in enumerate(order):
        axis = bits - 1 - bit
        mine = (ctx >> bit) & 1
        gone = lax.dynamic_slice_in_dim(held, 1 - mine, 1, axis)
        kept = lax.dynamic_slice_in_dim(held, mine, 1, axis)
        held = kept.astype(F32) + partner("ctx", gone, bit).astype(F32)
        if place_in_order < bits - 1:
            held = held.astype(BF16)
    return held.reshape(shape)


def on_device(
    queries,
    rotated_key_heads,
    value_head_rows,
    out_proj,
    norm_gain,
    expert_ids,
    gate_weights,
    expert_gate,
    expert_up,
    expert_down,
    grad_out,
):
    seq_count, block_len, heads_width = queries.shape
    heads_dev = heads_width // HEAD_SIZE
    group = LOCAL_QUERY_HEADS // LOCAL_KEY_HEADS
    exp_count = lax.axis_size("exp")
    ctx_count = lax.axis_size("ctx")
    owner = lax.axis_index("exp")
    ctx = lax.axis_index("ctx")
    bits = ctx_count.bit_length() - 1
    n, _ = expert_ids.shape
    width = grad_out.shape[1]
    experts = exp_count * expert_gate.shape[0]
    capacity = min(n, 2 * n // experts)

    ids_f = expert_ids.astype(F32)
    info = jnp.stack([ids_f[:, 0], gate_weights[:, 0]])
    info = lax.all_to_all(
        jnp.broadcast_to(info[None], (exp_count, 2, n)), "exp", 0, 0, tiled=True
    )
    ids_all, weights_all = info[:, 0:1, :], info[:, 1:2, :]

    grads = place(ids_f.reshape(1, n), grad_out, experts, capacity)
    grads = lax.all_to_all(grads, "exp", 0, 0, tiled=True)

    first_column = (owner * heads_dev // group) * HEAD_SIZE
    low, high = list(range(1, bits)) + [0], list(range(bits - 1, 0, -1)) + [0]
    keys = lax.dynamic_slice_in_dim(rotated_key_heads, first_column, HEAD_SIZE, 2)
    values = lax.dynamic_slice_in_dim(value_head_rows, first_column, HEAD_SIZE, 2)
    keys = doubled(keys, bits, low)
    values = doubled(values, bits, high)

    pieces = min(ctx_count, width // PIECE)
    piece_bits = pieces.bit_length() - 1
    piece = width // pieces
    piece_index = ctx % pieces
    mine = lax.dynamic_slice_in_dim(out_proj, piece_index * piece, piece, 1)
    mine = lax.all_gather(mine, "exp", axis=0, tiled=True)
    half = mine.shape[0] // 2
    wa = doubled(mine[:half], piece_bits, [b for b in low if b < piece_bits])
    wb = doubled(mine[half:], piece_bits, [b for b in high if b < piece_bits])

    attended = attend(
        ctx.reshape(1).astype(jnp.int32), queries, keys, values, ids_all, experts, capacity
    )
    place_of = jnp.stack([piece_index, owner]).astype(jnp.int32)
    outs = []
    for index, sent in enumerate(attended):
        arrived = lax.all_to_all(sent, "exp", 0, 0, tiled=True)
        outs.append(
            expert_part(
                place_of,
                arrived,
                wa,
                wb,
                norm_gain.reshape(1, width),
                ids_all,
                weights_all,
                grads,
                expert_gate,
                expert_up,
                expert_down,
                capacity,
                index,
            )
        )
    layer, grad_hidden, normed, back, units, back_gate, back_up = zip(*outs)
    layer = [lax.all_to_all(x, "exp", 0, 0, tiled=True) for x in layer]
    grad_hidden = [lax.all_to_all(x, "exp", 0, 0, tiled=True) for x in grad_hidden]
    part_gate, part_up, part_down = weight_parts(normed, back, units, back_gate, back_up)

    ff = part_gate.shape[1]
    rows_dev = width // ctx_count
    part_gate = part_gate.reshape(ctx_count, rows_dev, ff)
    part_up = part_up.reshape(ctx_count, rows_dev, ff)
    if rows_dev != PIECE:
        part_down = part_down.reshape(width // PIECE, ff, PIECE // rows_dev, rows_dev)
        part_down = part_down.transpose(0, 2, 1, 3).reshape(ctx_count, ff, rows_dev)
    core_low, core_high = [0] + low[:-1], [0] + high[:-1]
    grad_gate = halved(part_gate, bits, core_low, ctx)[None]
    grad_up = halved(part_up, bits, core_high, ctx)[None]
    grad_down = halved(part_down, bits, core_low, ctx)[None]

    layer_out = restore(ids_f, layer, capacity)
    grad_hidden = restore(ids_f, grad_hidden, capacity)
    return (layer_out, grad_hidden, grad_gate, grad_up, grad_down)


def solution(mesh):
    in_specs = (
        P(None, "ctx", "exp"),
        P(None, "ctx", None),
        P(None, "ctx", None),
        P("exp", None),
        P(),
        P(("ctx", "exp"), None),
        P(("ctx", "exp"), None),
        P("exp", None, None),
        P("exp", None, None),
        P("exp", None, None),
        P(("ctx", "exp"), None),
    )
    out_specs = (
        P(("ctx", "exp"), None),
        P(("ctx", "exp"), None),
        P("exp", "ctx", None),
        P("exp", "ctx", None),
        P("exp", None, "ctx"),
    )
    return jax.shard_map(
        on_device, mesh=mesh, in_specs=in_specs, out_specs=out_specs, check_vma=False
    )
```

```python
import functools
import math

import jax
import jax.numpy as jnp
from jax import lax
from jax.experimental import pallas as pl
from jax.experimental.pallas import tpu as pltpu
from jax.sharding import PartitionSpec as P

LOCAL_QUERY_HEADS = 16
LOCAL_KEY_HEADS = 2
HEAD_SIZE = 128
PIECE = 256
PARTS = 2

epsilon = 1e-06
masked_score = -1e30
F32 = jnp.float32
BF16 = jnp.bfloat16
VMEM_LIMIT = 60 << 20


def dot(a, b, contract=((1,), (0,))):
    return lax.dot_general(a, b, (contract, ((), ())), preferred_element_type=F32)


def iota(shape, dim):
    return lax.broadcasted_iota(jnp.int32, shape, dim)


def slots_row(ids_row, capacity):
    n = ids_row.shape[1]
    names = iota((16, n), 0).astype(F32)
    chosen = names == ids_row
    before = (iota((n, n), 0) < iota((n, n), 1)).astype(F32).astype(BF16)
    earlier = dot(jnp.where(chosen, 1.0, 0.0).astype(BF16), before)
    return jnp.sum(jnp.where(chosen, earlier + names * capacity, 0.0), axis=0, keepdims=True)


def slots_column(ids_column, capacity):
    n = ids_column.shape[0]
    names = iota((n, 128), 1).astype(F32)
    chosen = names == ids_column
    before = (iota((n, n), 1) < iota((n, n), 0)).astype(F32).astype(BF16)
    earlier = dot(before, jnp.where(chosen, 1.0, 0.0).astype(BF16))
    return jnp.sum(jnp.where(chosen, earlier + names * capacity, 0.0), axis=1, keepdims=True)


def one_hot(matches):
    return jnp.where(matches, 1.0, 0.0).astype(BF16)


def shifted_slots(position, owner, experts, capacity):
    expert = lax.rem(position // capacity + owner, experts)
    return (expert * capacity + lax.rem(position, capacity)).astype(F32)


def kernel_params():
    return pltpu.CompilerParams(vmem_limit_bytes=VMEM_LIMIT)


def whole(*shape):
    return pl.BlockSpec(shape, lambda *_: (0,) * len(shape))


def smem():
    return pl.BlockSpec(memory_space=pltpu.SMEM)


def attend_kernel(experts, capacity, heads, n_ctx, where_ref, q_ref, ids_ref, *refs):
    k_refs, refs = refs[:n_ctx], refs[n_ctx:]
    v_refs, refs = refs[:n_ctx], refs[n_ctx:]
    out_refs, refs = refs[: experts * PARTS], refs[experts * PARTS :]
    k_scr, v_scr, best_scr, acc_scr, att_scr = refs
    ctx, owner = where_ref[0], where_ref[1]
    seq = pl.program_id(0)
    block = q_ref.shape[1]
    tile = 2 * block
    factor = math.log2(math.e) / math.sqrt(HEAD_SIZE)

    @pl.when(seq == 0)
    def _():
        v_scr[:, :, HEAD_SIZE:] = jnp.ones((n_ctx, block, HEAD_SIZE), BF16)

    for m in range(n_ctx):
        index = jnp.bitwise_xor(ctx, m)
        k_scr[index] = k_refs[m][0]
        v_scr[index, :, :HEAD_SIZE] = v_refs[m][0]

    def fold(t, last):
        key_tile = k_scr[pl.ds(2 * t, 2)].reshape(tile, HEAD_SIZE)
        value_tile = v_scr[pl.ds(2 * t, 2)].reshape(tile, 2 * HEAD_SIZE)
        for h in range(heads):
            q = q_ref[0, :, h * HEAD_SIZE : (h + 1) * HEAD_SIZE]
            s = dot(q, key_tile, ((1,), (1,)))
            if last:
                key_pos = iota((block, tile), 1) + t * tile
                query_pos = iota((block, tile), 0) + ctx * block
                s = jnp.where(key_pos <= query_pos, s, masked_score)
            best = jnp.max(s, axis=1, keepdims=True)
            if not last:
                old = best_scr[h]
                best = jnp.maximum(old, best)
            p = jnp.exp2((s - best) * factor)
            blended = dot(p.astype(BF16), value_tile)
            if last:
                acc_scr[h] = blended
            else:
                acc_scr[h] = acc_scr[h] * jnp.exp2((old - best) * factor) + blended
            best_scr[h] = best

    fold(ctx // 2, True)

    @pl.loop(0, ctx // 2)
    def _(t):
        fold(t, False)

    for h in range(heads):
        acc = acc_scr[h]
        att = acc[:, :HEAD_SIZE] / acc[:, HEAD_SIZE:]
        att_scr[:, h * HEAD_SIZE : (h + 1) * HEAD_SIZE] = att.astype(BF16)

    n = ids_ref.shape[2]
    part = capacity // PARTS
    per_seq = block // n
    position = iota((experts * capacity, n), 0)
    slots = shifted_slots(position, owner, experts, capacity)
    for b in range(per_seq):
        source = seq * per_seq + b
        target = slots_row(ids_ref[lax.rem(owner - source + experts, experts)], capacity)
        picked = dot(one_hot(slots == target), att_scr[b * n : (b + 1) * n, :]).astype(BF16)
        for d in range(experts):
            rank = lax.rem(owner + d - source + experts, experts)
            for c in range(PARTS):
                first = d * capacity + c * part
                out_refs[c * experts + d][rank] = picked[first : first + part]


def attend(where, queries, keys, values, ids, capacity):
    seqs, block, width = queries.shape
    n_ctx = len(keys)
    experts, _, n = ids.shape
    heads = width // HEAD_SIZE
    part = capacity // PARTS
    by_seq = pl.BlockSpec((1, block, HEAD_SIZE), lambda s: (s, 0, 0))
    outs = pl.pallas_call(
        functools.partial(attend_kernel, experts, capacity, heads, n_ctx),
        grid=(seqs,),
        in_specs=[
            smem(),
            pl.BlockSpec((1, block, width), lambda s: (s, 0, 0)),
            whole(experts, 1, n),
        ]
        + [by_seq] * (2 * n_ctx),
        out_specs=[whole(experts, part, width)] * (PARTS * experts),
        scratch_shapes=[
            pltpu.VMEM((n_ctx, block, HEAD_SIZE), BF16),
            pltpu.VMEM((n_ctx, block, 2 * HEAD_SIZE), BF16),
            pltpu.VMEM((heads, block, 1), F32),
            pltpu.VMEM((heads, block, 2 * HEAD_SIZE), F32),
            pltpu.VMEM((block, width), BF16),
        ],
        out_shape=[jax.ShapeDtypeStruct((experts, part, width), BF16)] * (PARTS * experts),
        compiler_params=kernel_params(),
        cost_estimate=pl.CostEstimate(
            flops=4 * seqs * block * block * n_ctx * width,
            bytes_accessed=8 << 20,
            transcendentals=seqs * heads * block * block * n_ctx,
        ),
        name="attend",
    )(where, queries, ids, *keys, *values)
    return [outs[c * experts : (c + 1) * experts] for c in range(PARTS)]


def place_kernel(experts, capacity, where_ref, ids_ref, rows_ref, *refs):
    out_refs, pick_scr = refs[:-1], refs[-1]

    @pl.when(pl.program_id(0) == 0)
    def _():
        position = iota(pick_scr.shape, 0)
        slots = shifted_slots(position, where_ref[1], experts, capacity)
        pick_scr[...] = one_hot(slots == slots_row(ids_ref[...], capacity))

    picked = dot(pick_scr[...], rows_ref[...]).astype(BF16)
    for d, ref in enumerate(out_refs):
        ref[...] = picked[d * capacity : (d + 1) * capacity]


def place(where, ids_row, rows, experts, capacity):
    n, width = rows.shape
    cols = min(width, 1024)
    return pl.pallas_call(
        functools.partial(place_kernel, experts, capacity),
        grid=(width // cols,),
        in_specs=[smem(), whole(1, n), pl.BlockSpec((n, cols), lambda i: (0, i))],
        out_specs=[pl.BlockSpec((capacity, cols), lambda i: (0, i))] * experts,
        out_shape=[jax.ShapeDtypeStruct((capacity, width), BF16)] * experts,
        scratch_shapes=[pltpu.VMEM((experts * capacity, n), BF16)],
        compiler_params=kernel_params(),
        name="place",
    )(where, ids_row, rows)


def restore_kernel(experts, capacity, tiles, where_ref, ids_ref, *refs):
    parts, refs = refs[: experts * PARTS], refs[experts * PARTS :]
    layer_ref, grad_ref, pick_scr = refs
    step = pl.program_id(0)

    @pl.when(step == 0)
    def _():
        slots = shifted_slots(iota(pick_scr.shape, 1), where_ref[1], experts, capacity)
        pick_scr[...] = one_hot(slots == slots_column(ids_ref[...], capacity))

    rows = jnp.concatenate([ref[...] for ref in parts], axis=0)
    out = dot(pick_scr[...], rows).astype(BF16)

    @pl.when(step < tiles)
    def _():
        layer_ref[...] = out

    @pl.when(step >= tiles)
    def _():
        grad_ref[...] = out


def restore(where, ids_column, parts, experts, capacity):
    n = ids_column.shape[0]
    part, both = parts[0][0].shape
    width = both // 2
    cols = min(width, 1024)
    tiles = width // cols
    return pl.pallas_call(
        functools.partial(restore_kernel, experts, capacity, tiles),
        grid=(2 * tiles,),
        in_specs=[smem(), whole(n, 1)]
        + [pl.BlockSpec((part, cols), lambda i: (0, i))] * (experts * PARTS),
        out_specs=[
            pl.BlockSpec((n, cols), lambda i: (0, jnp.minimum(i, tiles - 1))),
            pl.BlockSpec((n, cols), lambda i: (0, jnp.maximum(i - tiles, 0))),
        ],
        out_shape=[jax.ShapeDtypeStruct((n, width), BF16)] * 2,
        scratch_shapes=[pltpu.VMEM((n, experts * capacity), BF16)],
        compiler_params=kernel_params(),
        name="restore",
    )(where, ids_column, *[parts[c][d] for d in range(experts) for c in range(PARTS)])


def expert_kernel(pieces, experts, capacity, part_index, where_ref, *refs):
    att_refs, refs = refs[:experts], refs[experts:]
    grad_refs, refs = refs[:experts], refs[experts:]
    wa_refs, refs = refs[:pieces], refs[pieces:]
    wb_refs, refs = refs[:pieces], refs[pieces:]
    gate_hbm, up_hbm, down_hbm, gain_ref, ids_ref, weight_ref = refs[:6]
    refs = refs[6:]
    out_refs, refs = refs[:experts], refs[experts:]
    normed_ref, back_ref, units_ref, back_gate_ref, back_up_ref = refs[:5]
    w_scr, gate_scr, up_scr, down_scr, hidden_scr, back_in_scr, sems = refs[5:]
    part, width = grad_refs[0].shape
    rows = experts * part
    att_cols = att_refs[0].shape[2]
    half, piece = wa_refs[0].shape
    ff = units_ref.shape[1]
    piece_index, owner = where_ref[2], where_ref[1]

    copies = []
    for m in range(pieces):
        copies.append(
            (
                pltpu.make_async_copy(wa_refs[m], w_scr.at[m, pl.ds(0, half)], sems.at[2 * m]),
                pltpu.make_async_copy(
                    wb_refs[m], w_scr.at[m, pl.ds(half, half)], sems.at[2 * m + 1]
                ),
            )
        )
    first = 2 * pieces
    weight_copies = (
        pltpu.make_async_copy(gate_hbm.at[0], gate_scr, sems.at[first]),
        pltpu.make_async_copy(up_hbm.at[0], up_scr, sems.at[first + 1]),
        pltpu.make_async_copy(down_hbm.at[0], down_scr, sems.at[first + 2]),
    )
    for pair in copies:
        for copy in pair:
            copy.start()
    for copy in weight_copies:
        copy.start()

    n = ids_ref.shape[2]
    weights = []
    for s in range(experts):
        target = slots_row(ids_ref[s], capacity)
        slot = iota((part, n), 0) + (owner * capacity + part_index * part)
        weights.append(
            jnp.sum(
                jnp.where(slot.astype(F32) == target, weight_ref[s], 0.0), axis=1, keepdims=True
            )
        )
        grads = grad_refs[s][...].astype(F32)
        back_ref[s * part : (s + 1) * part, :] = (weights[s] * grads).astype(BF16)

    for m in range(pieces):
        for copy in copies[m]:
            copy.wait()
        total = jnp.zeros((rows, piece), F32)
        for d in range(experts):
            source = lax.rem(owner - d + experts, experts)
            at = pl.multiple_of(source * att_cols, att_cols)
            total += dot(
                att_refs[d][...].reshape(rows, att_cols), w_scr[m, pl.ds(at, att_cols), :]
            )
        column = pl.multiple_of(jnp.bitwise_xor(piece_index, m) * piece, piece)
        hidden_scr[:, pl.ds(column, piece)] = total.astype(BF16)

    squares = jnp.zeros((rows, 1), F32)
    for t in range(0, width, PIECE):
        hidden = hidden_scr[:, t : t + PIECE].astype(F32)
        squares += jnp.sum(hidden * hidden, axis=1, keepdims=True)
    inv = lax.rsqrt(squares / width + epsilon)
    for t in range(0, width, PIECE):
        hidden = hidden_scr[:, t : t + PIECE].astype(F32)
        normed_ref[:, t : t + PIECE] = (hidden * inv * gain_ref[:, t : t + PIECE]).astype(BF16)

    for copy in weight_copies:
        copy.wait()
    for f in range(0, ff, 256):
        gate_act = dot(normed_ref[...], gate_scr[:, f : f + 256])
        up_act = dot(normed_ref[...], up_scr[:, f : f + 256])
        back_units = dot(back_ref[...], down_scr[f : f + 256, :], ((1,), (1,)))
        sigma = 1.0 / (1.0 + jnp.exp(-gate_act))
        gated = gate_act * sigma
        units_ref[:, f : f + 256] = (gated * up_act).astype(BF16)
        back_gate = back_units * up_act * sigma * (1.0 + gate_act * (1.0 - sigma))
        back_gate_ref[:, f : f + 256] = back_gate.astype(BF16)
        back_up_ref[:, f : f + 256] = (back_units * gated).astype(BF16)

    weight = jnp.concatenate(weights, axis=0)
    moment = jnp.zeros((rows, 1), F32)
    for t in range(0, width, PIECE):
        hidden = hidden_scr[:, t : t + PIECE].astype(F32)
        result = dot(units_ref[...], down_scr[:, t : t + PIECE]).astype(BF16).astype(F32)
        layer = (hidden + weight * result).astype(BF16)
        for s in range(experts):
            out_refs[s][:, t : t + PIECE] = layer[s * part : (s + 1) * part]
        back_in = dot(back_gate_ref[...], gate_scr[t : t + PIECE, :], ((1,), (1,)))
        back_in += dot(back_up_ref[...], up_scr[t : t + PIECE, :], ((1,), (1,)))
        back_in = back_in.astype(BF16)
        back_in_scr[:, t : t + PIECE] = back_in
        scaled = back_in.astype(F32) * gain_ref[:, t : t + PIECE]
        moment += jnp.sum(scaled * (hidden * inv), axis=1, keepdims=True)
    moment = moment / width
    for t in range(0, width, PIECE):
        unit = hidden_scr[:, t : t + PIECE].astype(F32) * inv
        scaled = back_in_scr[:, t : t + PIECE].astype(F32) * gain_ref[:, t : t + PIECE]
        change = inv * (scaled - unit * moment)
        for s in range(experts):
            grads = grad_refs[s][:, t : t + PIECE].astype(F32)
            out_refs[s][:, width + t : width + t + PIECE] = (
                grads + change[s * part : (s + 1) * part]
            ).astype(BF16)


def expert_part(where, att, grads, wa, wb, gate, up, down, gain, ids, weights, capacity, index):
    experts, part, att_cols = att[0].shape
    pieces = len(wa)
    half, piece = wa[0].shape
    width = grads[0].shape[1]
    ff = gate.shape[2]
    rows = experts * part
    n = ids.shape[2]
    out = lambda *shape: jax.ShapeDtypeStruct(shape, BF16)
    in_hbm = pl.BlockSpec(memory_space=pl.ANY)
    outs = pl.pallas_call(
        functools.partial(expert_kernel, pieces, experts, capacity, index),
        grid=(1,),
        in_specs=[smem()]
        + [whole(experts, part, att_cols)] * experts
        + [pl.BlockSpec((part, width), lambda i: (index, 0))] * experts
        + [in_hbm] * (2 * pieces + 3)
        + [whole(1, width), whole(experts, 1, n), whole(experts, 1, n)],
        out_specs=[whole(part, 2 * width)] * experts
        + [whole(rows, width)] * 2
        + [whole(rows, ff)] * 3,
        scratch_shapes=[
            pltpu.VMEM((pieces, 2 * half, piece), BF16),
            pltpu.VMEM((width, ff), BF16),
            pltpu.VMEM((width, ff), BF16),
            pltpu.VMEM((ff, width), BF16),
            pltpu.VMEM((rows, width), BF16),
            pltpu.VMEM((rows, width), BF16),
            pltpu.SemaphoreType.DMA((2 * pieces + 3,)),
        ],
        out_shape=[out(part, 2 * width)] * experts + [out(rows, width)] * 2 + [out(rows, ff)] * 3,
        compiler_params=kernel_params(),
        cost_estimate=pl.CostEstimate(
            flops=2 * rows * width * (width + 6 * ff),
            bytes_accessed=2 * (width * width + 3 * width * ff + 8 * rows * width),
            transcendentals=rows * ff,
        ),
        name="expert",
    )(where, *att, *grads, *wa, *wb, gate, up, down, gain, ids, weights)
    return outs[:experts], outs[experts:]


def weight_kernel(count, lead, *refs):
    normed, back, units, back_gate, back_up = [refs[i * count : (i + 1) * count] for i in range(5)]
    outs = refs[5 * count :]
    first = ((0,), (0,))
    gate = up = down = 0.0
    for c in range(count):
        gate += dot(normed[c][...], back_gate[c][...], first)
        up += dot(normed[c][...], back_up[c][...], first)
        down += dot(units[c][...], back[c][...], first)

    def put(gate_ref, up_ref, down_ref):
        gate_ref[0] = gate.astype(BF16)
        up_ref[0] = up.astype(BF16)
        down_ref[0] = down.astype(BF16)

    if len(outs) == 3:
        put(*outs)
        return

    @pl.when(pl.program_id(0) < lead)
    def _():
        put(*outs[:3])

    @pl.when(pl.program_id(0) >= lead)
    def _():
        put(*outs[3:])


def weight_parts(where, normed, back, units, back_gate, back_up, exchange):
    count = len(normed)
    rows, width = normed[0].shape
    ff = units[0].shape[1]
    cols = PIECE
    blocks = width // cols
    lead = blocks // 2 if exchange else blocks

    def block_of(i, where_ref):
        if not exchange:
            return i
        mask = jnp.where(i < lead, 2 * i + 1, 2 * (i - lead))
        return jnp.bitwise_xor(where_ref[0], mask)

    thin = [pl.BlockSpec((rows, cols), lambda i, w: (0, block_of(i, w)))] * count
    full = [pl.BlockSpec((rows, ff), lambda i, w: (0, 0))] * count
    early = lambda i, w: (jnp.minimum(i, lead - 1), 0, 0)
    late = lambda i, w: (jnp.maximum(i - lead, 0), 0, 0)
    shapes = [(cols, ff), (cols, ff), (ff, cols)]
    groups = [early, late] if exchange else [early]
    kernel = lambda where_ref, *refs: weight_kernel(count, lead, *refs)
    outs = pl.pallas_call(
        kernel,
        grid_spec=pltpu.PrefetchScalarGridSpec(
            num_scalar_prefetch=1,
            grid=(blocks,),
            in_specs=thin + thin + full + full + full,
            out_specs=[pl.BlockSpec((1,) + shape, at) for at in groups for shape in shapes],
        ),
        out_shape=[jax.ShapeDtypeStruct((lead,) + shape, BF16) for _ in groups for shape in shapes],
        compiler_params=kernel_params(),
        cost_estimate=pl.CostEstimate(
            flops=6 * count * rows * width * ff,
            bytes_accessed=2 * (3 * width * ff + 2 * count * rows * (width + 2 * ff)),
            transcendentals=0,
        ),
        name="weight_grads",
    )(where, *normed, *back, *units, *back_gate, *back_up)
    return outs[:3], outs[3:]


def partner(value, bit):
    count = lax.axis_size("ctx")
    return lax.ppermute(value, "ctx", [(i, i ^ (1 << bit)) for i in range(count)])


def shift(value, by):
    count = lax.axis_size("exp")
    return lax.ppermute(value, "exp", [(i, (i + by) % count) for i in range(count)])


def spread(value, order):
    held = {0: value}
    for bit in order:
        for m in list(held):
            held[m | 1 << bit] = partner(held[m], bit)
    return [held[m] for m in sorted(held)]


def halved(value, bits, order, ctx):
    shape = value.shape[1:]
    held = value.reshape((2,) * bits + shape)
    for place_in_order, bit in enumerate(order):
        axis = bits - 1 - bit
        mine = (ctx >> bit) & 1
        gone = lax.dynamic_slice_in_dim(held, 1 - mine, 1, axis)
        kept = lax.dynamic_slice_in_dim(held, mine, 1, axis)
        held = kept.astype(F32) + partner(gone, bit).astype(F32)
        if place_in_order < bits - 1:
            held = held.astype(BF16)
    return held.reshape(shape)


def halved_relative(gone, kept, bits, order):
    shape = kept.shape[1:]
    arrived = partner(gone, 0).astype(F32).reshape((2,) * (bits - 1) + shape)
    held = kept.astype(F32).reshape((2,) * (bits - 1) + shape)
    for bit in order:
        axis = bits - 1 - bit
        take = lambda x, i: lax.slice_in_dim(x, i, i + 1, axis=axis)
        gone = (take(held, 1) + take(arrived, 1)).astype(BF16)
        held = (take(held, 0) + take(arrived, 0)).astype(BF16).astype(F32)
        arrived = partner(gone, bit).astype(F32)
    return (held + arrived).reshape(shape)


def on_device(
    queries,
    rotated_key_heads,
    value_head_rows,
    out_proj,
    norm_gain,
    expert_ids,
    gate_weights,
    expert_gate,
    expert_up,
    expert_down,
    grad_out,
):
    heads_dev = queries.shape[2] // HEAD_SIZE
    group = LOCAL_QUERY_HEADS // LOCAL_KEY_HEADS
    exp_count = lax.axis_size("exp")
    ctx_count = lax.axis_size("ctx")
    owner = lax.axis_index("exp")
    ctx = lax.axis_index("ctx")
    bits = ctx_count.bit_length() - 1
    n, _ = expert_ids.shape
    width = grad_out.shape[1]
    experts = exp_count
    capacity = min(n, 2 * n // experts)
    pieces = min(ctx_count, width // PIECE)
    piece_bits = pieces.bit_length() - 1
    piece = width // pieces
    piece_index = ctx % pieces
    where = jnp.stack([ctx, owner, piece_index]).astype(jnp.int32)

    first_column = (owner * heads_dev // group) * HEAD_SIZE
    low, high = list(range(1, bits)) + [0], list(range(bits - 1, 0, -1)) + [0]
    keys = lax.dynamic_slice_in_dim(rotated_key_heads, first_column, HEAD_SIZE, 2)
    values = lax.dynamic_slice_in_dim(value_head_rows, first_column, HEAD_SIZE, 2)
    keys = spread(keys, low)
    values = spread(values, high)

    ids_f = expert_ids.astype(F32)
    info = jnp.stack([ids_f[:, 0], gate_weights[:, 0]])
    info = jnp.stack([info] + [shift(info, d) for d in range(1, experts)])
    ids_all, weights_all = info[:, 0:1, :], info[:, 1:2, :]

    grads = place(where, ids_f.reshape(1, n), grad_out, experts, capacity)
    grads = [grads[0]] + [shift(grads[d], d) for d in range(1, experts)]

    mine = lax.dynamic_slice_in_dim(out_proj, piece_index * piece, piece, 1)
    mine = lax.all_gather(mine, "exp", axis=0, tiled=True)
    half = mine.shape[0] // 2
    mine, keys, values = lax.optimization_barrier((mine, keys, values))
    wa = spread(mine[:half], [b for b in low if b < piece_bits])
    wb = spread(mine[half:], [b for b in high if b < piece_bits])

    attended = attend(where, queries, keys, values, ids_all, capacity)
    returned, kept = [], []
    for index, sent in enumerate(attended):
        arrived = [sent[0]] + [shift(sent[d], d) for d in range(1, experts)]
        rows, saved = expert_part(
            where,
            arrived,
            grads,
            wa,
            wb,
            expert_gate,
            expert_up,
            expert_down,
            norm_gain.reshape(1, width),
            ids_all,
            weights_all,
            capacity,
            index,
        )
        returned.append([rows[0]] + [shift(rows[d], -d) for d in range(1, experts)])
        kept.append(saved)

    rows_dev = width // ctx_count
    exchange = rows_dev == PIECE
    gone, stay = weight_parts(where, *zip(*kept), exchange)
    if exchange:
        orders = low[:-1], high[:-1], low[:-1]
        grad_gate, grad_up, grad_down = [
            halved_relative(g, s, bits, order)[None] for g, s, order in zip(gone, stay, orders)
        ]
    else:
        ff = expert_gate.shape[2]
        part_gate, part_up = [x.reshape(ctx_count, rows_dev, ff) for x in gone[:2]]
        part_down = gone[2].reshape(width // PIECE, ff, PIECE // rows_dev, rows_dev)
        part_down = part_down.transpose(0, 2, 1, 3).reshape(ctx_count, ff, rows_dev)
        core_low, core_high = [0] + low[:-1], [0] + high[:-1]
        grad_gate = halved(part_gate, bits, core_low, ctx)[None]
        grad_up = halved(part_up, bits, core_high, ctx)[None]
        grad_down = halved(part_down, bits, core_low, ctx)[None]

    layer_out, grad_hidden = restore(where, ids_f, returned, experts, capacity)
    return (layer_out, grad_hidden, grad_gate, grad_up, grad_down)


def solution(mesh):
    in_specs = (
        P(None, "ctx", "exp"),
        P(None, "ctx", None),
        P(None, "ctx", None),
        P("exp", None),
        P(),
        P(("ctx", "exp"), None),
        P(("ctx", "exp"), None),
        P("exp", None, None),
        P("exp", None, None),
        P("exp", None, None),
        P(("ctx", "exp"), None),
    )
    out_specs = (
        P(("ctx", "exp"), None),
        P(("ctx", "exp"), None),
        P("exp", "ctx", None),
        P("exp", "ctx", None),
        P("exp", None, "ctx"),
    )
    return jax.shard_map(
        on_device, mesh=mesh, in_specs=in_specs, out_specs=out_specs, check_vma=False
    )
```

```python
import functools
import math

import jax
import jax.numpy as jnp
from jax import lax
from jax.experimental import pallas as pl
from jax.experimental.pallas import tpu as pltpu
from jax.sharding import PartitionSpec as P

LOCAL_QUERY_HEADS = 16
LOCAL_KEY_HEADS = 2
HEAD_SIZE = 128
PIECE = 256
PARTS = 2

epsilon = 1e-06
masked_score = -1e30
F32 = jnp.float32
BF16 = jnp.bfloat16
VMEM_LIMIT = 60 << 20


def dot(a, b, contract=((1,), (0,))):
    return lax.dot_general(a, b, (contract, ((), ())), preferred_element_type=F32)


def iota(shape, dim):
    return lax.broadcasted_iota(jnp.int32, shape, dim)


def slots_row(ids_row, capacity):
    n = ids_row.shape[1]
    names = iota((16, n), 0).astype(F32)
    chosen = names == ids_row
    before = (iota((n, n), 0) < iota((n, n), 1)).astype(F32).astype(BF16)
    earlier = dot(jnp.where(chosen, 1.0, 0.0).astype(BF16), before)
    return jnp.sum(jnp.where(chosen, earlier + names * capacity, 0.0), axis=0, keepdims=True)


def slots_column(ids_column, capacity):
    n = ids_column.shape[0]
    names = iota((n, 128), 1).astype(F32)
    chosen = names == ids_column
    before = (iota((n, n), 1) < iota((n, n), 0)).astype(F32).astype(BF16)
    earlier = dot(before, jnp.where(chosen, 1.0, 0.0).astype(BF16))
    return jnp.sum(jnp.where(chosen, earlier + names * capacity, 0.0), axis=1, keepdims=True)


def one_hot(matches):
    return jnp.where(matches, 1.0, 0.0).astype(BF16)


def shifted_slots(position, owner, experts, capacity):
    expert = lax.rem(position // capacity + owner, experts)
    return (expert * capacity + lax.rem(position, capacity)).astype(F32)


def kernel_params():
    return pltpu.CompilerParams(vmem_limit_bytes=VMEM_LIMIT)


def brief():
    return pl.CostEstimate(flops=1000, bytes_accessed=1000, transcendentals=0)


def whole(*shape):
    return pl.BlockSpec(shape, lambda *_: (0,) * len(shape))


def smem():
    return pl.BlockSpec(memory_space=pltpu.SMEM)


def attend_kernel(experts, capacity, heads, n_ctx, where_ref, q_ref, ids_ref, *refs):
    kv_refs, refs = refs[:n_ctx], refs[n_ctx:]
    out_refs, refs = refs[: experts * PARTS], refs[experts * PARTS :]
    k_scr, v_scr, best_scr, acc_scr, att_scr = refs
    ctx, owner = where_ref[0], where_ref[1]
    seq = pl.program_id(0)
    block = q_ref.shape[1]
    tile = 2 * block
    factor = math.log2(math.e) / math.sqrt(HEAD_SIZE)

    @pl.when(seq == 0)
    def _():
        v_scr[:, :, HEAD_SIZE:] = jnp.ones((n_ctx, block, HEAD_SIZE), BF16)

    for m in range(n_ctx):
        index = jnp.bitwise_xor(ctx, m)
        k_scr[index] = kv_refs[m][0, :, :HEAD_SIZE]
        v_scr[index, :, :HEAD_SIZE] = kv_refs[m][0, :, HEAD_SIZE:]

    def fold(t, last):
        key_tile = k_scr[pl.ds(2 * t, 2)].reshape(tile, HEAD_SIZE)
        value_tile = v_scr[pl.ds(2 * t, 2)].reshape(tile, 2 * HEAD_SIZE)
        for h in range(heads):
            q = q_ref[0, :, h * HEAD_SIZE : (h + 1) * HEAD_SIZE]
            s = dot(q, key_tile, ((1,), (1,)))
            if last:
                key_pos = iota((block, tile), 1) + t * tile
                query_pos = iota((block, tile), 0) + ctx * block
                s = jnp.where(key_pos <= query_pos, s, masked_score)
            best = jnp.max(s, axis=1, keepdims=True)
            if not last:
                old = best_scr[h]
                best = jnp.maximum(old, best)
            p = jnp.exp2((s - best) * factor)
            blended = dot(p.astype(BF16), value_tile)
            if last:
                acc_scr[h] = blended
            else:
                acc_scr[h] = acc_scr[h] * jnp.exp2((old - best) * factor) + blended
            best_scr[h] = best

    fold(ctx // 2, True)

    @pl.loop(0, ctx // 2)
    def _(t):
        fold(t, False)

    for h in range(heads):
        acc = acc_scr[h]
        att = acc[:, :HEAD_SIZE] / acc[:, HEAD_SIZE:]
        att_scr[:, h * HEAD_SIZE : (h + 1) * HEAD_SIZE] = att.astype(BF16)

    n = ids_ref.shape[2]
    part = capacity // PARTS
    per_seq = block // n
    position = iota((experts * capacity, n), 0)
    slots = shifted_slots(position, owner, experts, capacity)
    for b in range(per_seq):
        source = seq * per_seq + b
        target = slots_row(ids_ref[lax.rem(owner - source + experts, experts)], capacity)
        picked = dot(one_hot(slots == target), att_scr[b * n : (b + 1) * n, :]).astype(BF16)
        for d in range(experts):
            rank = lax.rem(owner + d - source + experts, experts)
            for c in range(PARTS):
                first = d * capacity + c * part
                out_refs[c * experts + d][rank] = picked[first : first + part]


def attend(where, queries, key_values, ids, capacity):
    seqs, block, width = queries.shape
    n_ctx = len(key_values)
    experts, _, n = ids.shape
    heads = width // HEAD_SIZE
    part = capacity // PARTS
    by_seq = pl.BlockSpec((1, block, 2 * HEAD_SIZE), lambda s: (s, 0, 0))
    outs = pl.pallas_call(
        functools.partial(attend_kernel, experts, capacity, heads, n_ctx),
        grid=(seqs,),
        in_specs=[
            smem(),
            pl.BlockSpec((1, block, width), lambda s: (s, 0, 0)),
            whole(experts, 1, n),
        ]
        + [by_seq] * n_ctx,
        out_specs=[whole(experts, part, width)] * (PARTS * experts),
        scratch_shapes=[
            pltpu.VMEM((n_ctx, block, HEAD_SIZE), BF16),
            pltpu.VMEM((n_ctx, block, 2 * HEAD_SIZE), BF16),
            pltpu.VMEM((heads, block, 1), F32),
            pltpu.VMEM((heads, block, 2 * HEAD_SIZE), F32),
            pltpu.VMEM((block, width), BF16),
        ],
        out_shape=[jax.ShapeDtypeStruct((experts, part, width), BF16)] * (PARTS * experts),
        compiler_params=kernel_params(),
        cost_estimate=brief(),
        name="attend",
    )(where, queries, ids, *key_values)
    return [outs[c * experts : (c + 1) * experts] for c in range(PARTS)]


def place_kernel(experts, capacity, where_ref, ids_ref, rows_ref, *refs):
    out_refs, pick_scr = refs[:-1], refs[-1]

    @pl.when(pl.program_id(0) == 0)
    def _():
        position = iota(pick_scr.shape, 0)
        slots = shifted_slots(position, where_ref[1], experts, capacity)
        pick_scr[...] = one_hot(slots == slots_row(ids_ref[...], capacity))

    picked = dot(pick_scr[...], rows_ref[...]).astype(BF16)
    for d, ref in enumerate(out_refs):
        ref[...] = picked[d * capacity : (d + 1) * capacity]


def place(where, ids_row, rows, experts, capacity):
    n, width = rows.shape
    cols = min(width, 1024)
    return pl.pallas_call(
        functools.partial(place_kernel, experts, capacity),
        grid=(width // cols,),
        in_specs=[smem(), whole(1, n), pl.BlockSpec((n, cols), lambda i: (0, i))],
        out_specs=[pl.BlockSpec((capacity, cols), lambda i: (0, i))] * experts,
        out_shape=[jax.ShapeDtypeStruct((capacity, width), BF16)] * experts,
        scratch_shapes=[pltpu.VMEM((experts * capacity, n), BF16)],
        compiler_params=kernel_params(),
        cost_estimate=brief(),
        name="place",
    )(where, ids_row, rows)


def restore_kernel(experts, capacity, tiles, where_ref, ids_ref, *refs):
    parts, refs = refs[: experts * PARTS], refs[experts * PARTS :]
    layer_ref, grad_ref, pick_scr = refs
    step = pl.program_id(0)

    @pl.when(step == 0)
    def _():
        slots = shifted_slots(iota(pick_scr.shape, 1), where_ref[1], experts, capacity)
        pick_scr[...] = one_hot(slots == slots_column(ids_ref[...], capacity))

    rows = jnp.concatenate([ref[...] for ref in parts], axis=0)
    out = dot(pick_scr[...], rows).astype(BF16)

    @pl.when(step < tiles)
    def _():
        layer_ref[...] = out

    @pl.when(step >= tiles)
    def _():
        grad_ref[...] = out


def restore(where, ids_column, parts, experts, capacity):
    n = ids_column.shape[0]
    part, both = parts[0][0].shape
    width = both // 2
    cols = min(width, 1024)
    tiles = width // cols
    return pl.pallas_call(
        functools.partial(restore_kernel, experts, capacity, tiles),
        grid=(2 * tiles,),
        in_specs=[smem(), whole(n, 1)]
        + [pl.BlockSpec((part, cols), lambda i: (0, i))] * (experts * PARTS),
        out_specs=[
            pl.BlockSpec((n, cols), lambda i: (0, jnp.minimum(i, tiles - 1))),
            pl.BlockSpec((n, cols), lambda i: (0, jnp.maximum(i - tiles, 0))),
        ],
        out_shape=[jax.ShapeDtypeStruct((n, width), BF16)] * 2,
        scratch_shapes=[pltpu.VMEM((n, experts * capacity), BF16)],
        compiler_params=kernel_params(),
        cost_estimate=brief(),
        name="restore",
    )(where, ids_column, *[parts[c][d] for d in range(experts) for c in range(PARTS)])


def expert_kernel(pieces, experts, capacity, part_index, where_ref, *refs):
    att_refs, refs = refs[:experts], refs[experts:]
    grad_refs, refs = refs[:experts], refs[experts:]
    w_refs, refs = refs[:pieces], refs[pieces:]
    gate_hbm, up_hbm, down_hbm, gain_ref, ids_ref, weight_ref = refs[:6]
    refs = refs[6:]
    out_refs, refs = refs[:experts], refs[experts:]
    normed_ref, back_ref, units_ref, back_gate_ref, back_up_ref = refs[:5]
    w_scr, gate_scr, up_scr, down_scr, hidden_scr, back_in_scr, sems = refs[5:]
    part, width = grad_refs[0].shape
    rows = experts * part
    att_cols = att_refs[0].shape[2]
    piece = w_refs[0].shape[1]
    ff = units_ref.shape[1]
    piece_index, owner = where_ref[2], where_ref[1]

    copies = [
        pltpu.make_async_copy(w_refs[m], w_scr.at[m], sems.at[m]) for m in range(pieces)
    ]
    first = pieces
    weight_copies = (
        pltpu.make_async_copy(gate_hbm.at[0], gate_scr, sems.at[first]),
        pltpu.make_async_copy(up_hbm.at[0], up_scr, sems.at[first + 1]),
        pltpu.make_async_copy(down_hbm.at[0], down_scr, sems.at[first + 2]),
    )
    for copy in copies:
        copy.start()
    for copy in weight_copies:
        copy.start()

    n = ids_ref.shape[2]
    weights = []
    for s in range(experts):
        target = slots_row(ids_ref[s], capacity)
        slot = iota((part, n), 0) + (owner * capacity + part_index * part)
        weights.append(
            jnp.sum(
                jnp.where(slot.astype(F32) == target, weight_ref[s], 0.0), axis=1, keepdims=True
            )
        )
        grads = grad_refs[s][...].astype(F32)
        back_ref[s * part : (s + 1) * part, :] = (weights[s] * grads).astype(BF16)

    for m in range(pieces):
        copies[m].wait()
        total = jnp.zeros((rows, piece), F32)
        for d in range(experts):
            source = lax.rem(owner - d + experts, experts)
            at = pl.multiple_of(source * att_cols, att_cols)
            total += dot(
                att_refs[d][...].reshape(rows, att_cols), w_scr[m, pl.ds(at, att_cols), :]
            )
        column = pl.multiple_of(jnp.bitwise_xor(piece_index, m) * piece, piece)
        hidden_scr[:, pl.ds(column, piece)] = total.astype(BF16)

    squares = jnp.zeros((rows, 1), F32)
    for t in range(0, width, PIECE):
        hidden = hidden_scr[:, t : t + PIECE].astype(F32)
        squares += jnp.sum(hidden * hidden, axis=1, keepdims=True)
    inv = lax.rsqrt(squares / width + epsilon)
    for t in range(0, width, PIECE):
        hidden = hidden_scr[:, t : t + PIECE].astype(F32)
        normed_ref[:, t : t + PIECE] = (hidden * inv * gain_ref[:, t : t + PIECE]).astype(BF16)

    for copy in weight_copies:
        copy.wait()
    for f in range(0, ff, 256):
        gate_act = dot(normed_ref[...], gate_scr[:, f : f + 256])
        up_act = dot(normed_ref[...], up_scr[:, f : f + 256])
        back_units = dot(back_ref[...], down_scr[f : f + 256, :], ((1,), (1,)))
        sigma = 1.0 / (1.0 + jnp.exp(-gate_act))
        gated = gate_act * sigma
        units_ref[:, f : f + 256] = (gated * up_act).astype(BF16)
        back_gate = back_units * up_act * sigma * (1.0 + gate_act * (1.0 - sigma))
        back_gate_ref[:, f : f + 256] = back_gate.astype(BF16)
        back_up_ref[:, f : f + 256] = (back_units * gated).astype(BF16)

    weight = jnp.concatenate(weights, axis=0)
    moment = jnp.zeros((rows, 1), F32)
    for t in range(0, width, PIECE):
        hidden = hidden_scr[:, t : t + PIECE].astype(F32)
        result = dot(units_ref[...], down_scr[:, t : t + PIECE]).astype(BF16).astype(F32)
        layer = (hidden + weight * result).astype(BF16)
        for s in range(experts):
            out_refs[s][:, t : t + PIECE] = layer[s * part : (s + 1) * part]
        back_in = dot(back_gate_ref[...], gate_scr[t : t + PIECE, :], ((1,), (1,)))
        back_in += dot(back_up_ref[...], up_scr[t : t + PIECE, :], ((1,), (1,)))
        back_in = back_in.astype(BF16)
        back_in_scr[:, t : t + PIECE] = back_in
        scaled = back_in.astype(F32) * gain_ref[:, t : t + PIECE]
        moment += jnp.sum(scaled * (hidden * inv), axis=1, keepdims=True)
    moment = moment / width
    for t in range(0, width, PIECE):
        unit = hidden_scr[:, t : t + PIECE].astype(F32) * inv
        scaled = back_in_scr[:, t : t + PIECE].astype(F32) * gain_ref[:, t : t + PIECE]
        change = inv * (scaled - unit * moment)
        for s in range(experts):
            grads = grad_refs[s][:, t : t + PIECE].astype(F32)
            out_refs[s][:, width + t : width + t + PIECE] = (
                grads + change[s * part : (s + 1) * part]
            ).astype(BF16)


def expert_part(where, att, grads, projection, gate, up, down, gain, ids, weights, capacity, index):
    experts, part, att_cols = att[0].shape
    pieces = len(projection)
    depth, piece = projection[0].shape
    width = grads[0].shape[1]
    ff = gate.shape[2]
    rows = experts * part
    n = ids.shape[2]
    out = lambda *shape: jax.ShapeDtypeStruct(shape, BF16)
    in_hbm = pl.BlockSpec(memory_space=pl.ANY)
    outs = pl.pallas_call(
        functools.partial(expert_kernel, pieces, experts, capacity, index),
        grid=(1,),
        in_specs=[smem()]
        + [whole(experts, part, att_cols)] * experts
        + [pl.BlockSpec((part, width), lambda i: (index, 0))] * experts
        + [in_hbm] * (pieces + 3)
        + [whole(1, width), whole(experts, 1, n), whole(experts, 1, n)],
        out_specs=[whole(part, 2 * width)] * experts
        + [whole(rows, width)] * 2
        + [whole(rows, ff)] * 3,
        scratch_shapes=[
            pltpu.VMEM((pieces, depth, piece), BF16),
            pltpu.VMEM((width, ff), BF16),
            pltpu.VMEM((width, ff), BF16),
            pltpu.VMEM((ff, width), BF16),
            pltpu.VMEM((rows, width), BF16),
            pltpu.VMEM((rows, width), BF16),
            pltpu.SemaphoreType.DMA((pieces + 3,)),
        ],
        out_shape=[out(part, 2 * width)] * experts + [out(rows, width)] * 2 + [out(rows, ff)] * 3,
        compiler_params=kernel_params(),
        cost_estimate=brief(),
        name="expert",
    )(where, *att, *grads, *projection, gate, up, down, gain, ids, weights)
    return outs[:experts], outs[experts:]


def weight_kernel(count, *refs):
    normed, back, units, back_gate, back_up = [refs[i * count : (i + 1) * count] for i in range(5)]
    outs = refs[5 * count :]
    first = ((0,), (0,))

    def total(left, right):
        return sum(dot(a[...], b[...], first) for a, b in zip(left, right)).astype(BF16)

    gate, up, down = total(normed, back_gate), total(normed, back_up), total(units, back)
    if len(outs) == 3:
        outs[0][0], outs[1][0], outs[2][0] = gate, up, down
        return
    packed = outs[0]
    packed[0, 0] = gate
    packed[0, 1] = up
    cols = down.shape[1]
    for t in range(0, down.shape[0], cols):
        packed[0, 2, :, t : t + cols] = down[t : t + cols]


def weight_blocks(where, normed, back, units, back_gate, back_up, first=None):
    count = len(normed)
    rows, width = normed[0].shape
    ff = units[0].shape[1]
    cols = PIECE
    packed = first is not None
    blocks = width // cols // 2 if packed else width // cols

    def block_of(i, where_ref):
        return jnp.bitwise_xor(where_ref[0], 2 * i + first) if packed else i

    thin = [pl.BlockSpec((rows, cols), lambda i, w: (0, block_of(i, w)))] * count
    full = [pl.BlockSpec((rows, ff), lambda i, w: (0, 0))] * count
    shapes = [(3, cols, ff)] if packed else [(cols, ff), (cols, ff), (ff, cols)]
    return pl.pallas_call(
        lambda where_ref, *refs: weight_kernel(count, *refs),
        grid_spec=pltpu.PrefetchScalarGridSpec(
            num_scalar_prefetch=1,
            grid=(blocks,),
            in_specs=thin + thin + full + full + full,
            out_specs=[
                pl.BlockSpec((1,) + shape, lambda i, w, zeros=(0,) * len(shape): (i,) + zeros)
                for shape in shapes
            ],
        ),
        out_shape=[jax.ShapeDtypeStruct((blocks,) + shape, BF16) for shape in shapes],
        compiler_params=kernel_params(),
        cost_estimate=brief(),
        name="weight_grads",
    )(where, *normed, *back, *units, *back_gate, *back_up)


def partner(value, mask):
    count = lax.axis_size("ctx")
    return lax.ppermute(value, "ctx", [(i, i ^ mask) for i in range(count)])


def shift(value, by):
    count = lax.axis_size("exp")
    return lax.ppermute(value, "exp", [(i, (i + by) % count) for i in range(count)])


def from_chips(value, count):
    return [value] + [partner(value, m) for m in range(2, count, 2)]


def with_cores(held):
    return [x for value in held for x in (value, partner(value, 1))]


def halved(value, bits, order, ctx):
    shape = value.shape[1:]
    held = value.reshape((2,) * bits + shape)
    for place_in_order, bit in enumerate(order):
        axis = bits - 1 - bit
        mine = (ctx >> bit) & 1
        gone = lax.dynamic_slice_in_dim(held, 1 - mine, 1, axis)
        kept = lax.dynamic_slice_in_dim(held, mine, 1, axis)
        held = kept.astype(F32) + partner(gone, 1 << bit).astype(F32)
        if place_in_order < bits - 1:
            held = held.astype(BF16)
    return held.reshape(shape)


def on_device(
    queries,
    rotated_key_heads,
    value_head_rows,
    out_proj,
    norm_gain,
    expert_ids,
    gate_weights,
    expert_gate,
    expert_up,
    expert_down,
    grad_out,
):
    heads_dev = queries.shape[2] // HEAD_SIZE
    group = LOCAL_QUERY_HEADS // LOCAL_KEY_HEADS
    exp_count = lax.axis_size("exp")
    ctx_count = lax.axis_size("ctx")
    owner = lax.axis_index("exp")
    ctx = lax.axis_index("ctx")
    bits = ctx_count.bit_length() - 1
    n, _ = expert_ids.shape
    width = grad_out.shape[1]
    experts = exp_count
    capacity = min(n, 2 * n // experts)
    pieces = min(ctx_count, width // PIECE)
    piece = width // pieces
    piece_index = ctx % pieces
    where = jnp.stack([ctx, owner, piece_index]).astype(jnp.int32)

    first_column = (owner * heads_dev // group) * HEAD_SIZE
    keys = lax.dynamic_slice_in_dim(rotated_key_heads, first_column, HEAD_SIZE, 2)
    values = lax.dynamic_slice_in_dim(value_head_rows, first_column, HEAD_SIZE, 2)
    key_values = jnp.concatenate([keys, values], axis=2)
    key_values = with_cores(from_chips(key_values, ctx_count))

    ids_f = expert_ids.astype(F32)
    info = jnp.stack([ids_f[:, 0], gate_weights[:, 0]])
    info = jnp.stack([info] + [shift(info, d) for d in range(1, experts)])
    ids_all, weights_all = info[:, 0:1, :], info[:, 1:2, :]

    grads = place(where, ids_f.reshape(1, n), grad_out, experts, capacity)
    grads = [grads[0]] + [shift(grads[d], d) for d in range(1, experts)]

    mine = lax.dynamic_slice_in_dim(out_proj, piece_index * piece, piece, 1)
    mine = lax.all_gather(mine, "exp", axis=0, tiled=True)
    mine, key_values = lax.optimization_barrier((mine, key_values))
    projection = from_chips(mine, pieces)

    attended = attend(where, queries, key_values, ids_all, capacity)
    arrived = [[sent[0]] + [shift(sent[d], d) for d in range(1, experts)] for sent in attended[:1]]
    projection, later = lax.optimization_barrier((projection, attended[1:]))
    projection = with_cores(projection)
    arrived += [[sent[0]] + [shift(sent[d], d) for d in range(1, experts)] for sent in later]

    rows, kept = [], []
    for index, att in enumerate(arrived):
        out, saved = expert_part(
            where,
            att,
            grads,
            projection,
            expert_gate,
            expert_up,
            expert_down,
            norm_gain.reshape(1, width),
            ids_all,
            weights_all,
            capacity,
            index,
        )
        rows.append(out)
        kept.append(saved)
    returned = [[rows[0][0]] + [shift(rows[0][d], -d) for d in range(1, experts)]]

    rows_dev = width // ctx_count
    ff = expert_gate.shape[2]
    if rows_dev == PIECE:
        (gone,) = weight_blocks(where, *zip(*kept), first=1)
        near = partner(gone, 1)
        (stay,) = weight_blocks(where, *zip(*kept), first=0)
        pair = [(stay[j].astype(F32) + near[j].astype(F32)) for j in range(ctx_count // 2)]
        far = [x.astype(BF16) for x in pair[1:]]
        far, later = lax.optimization_barrier((far, rows[1:]))
        far = [partner(x, 2 * j + 2) for j, x in enumerate(far)]
        total = sum([x.astype(F32) for x in far], pair[0])
        grad_gate, grad_up = total[0][None], total[1][None]
        grad_down = total[2].reshape(PIECE, ff // PIECE, PIECE).transpose(1, 0, 2)
        grad_down = grad_down.reshape(1, ff, PIECE)
    else:
        gone = weight_blocks(where, *zip(*kept))
        later = rows[1:]
        part_gate, part_up = [x.reshape(ctx_count, rows_dev, ff) for x in gone[:2]]
        part_down = gone[2].reshape(width // PIECE, ff, PIECE // rows_dev, rows_dev)
        part_down = part_down.transpose(0, 2, 1, 3).reshape(ctx_count, ff, rows_dev)
        order = list(range(bits))
        grad_gate, grad_up, grad_down = [
            halved(x, bits, order, ctx)[None] for x in (part_gate, part_up, part_down)
        ]
    returned += [[out[0]] + [shift(out[d], -d) for d in range(1, experts)] for out in later]
    returned, grad_gate, grad_up, grad_down = lax.optimization_barrier(
        (returned, grad_gate, grad_up, grad_down)
    )

    layer_out, grad_hidden = restore(where, ids_f, returned, experts, capacity)
    return (layer_out, grad_hidden, grad_gate, grad_up, grad_down)


def solution(mesh):
    in_specs = (
        P(None, "ctx", "exp"),
        P(None, "ctx", None),
        P(None, "ctx", None),
        P("exp", None),
        P(),
        P(("ctx", "exp"), None),
        P(("ctx", "exp"), None),
        P("exp", None, None),
        P("exp", None, None),
        P("exp", None, None),
        P(("ctx", "exp"), None),
    )
    out_specs = (
        P(("ctx", "exp"), None),
        P(("ctx", "exp"), None),
        P("exp", "ctx", None),
        P("exp", "ctx", None),
        P("exp", None, "ctx"),
    )
    return jax.shard_map(
        on_device, mesh=mesh, in_specs=in_specs, out_specs=out_specs, check_vma=False
    )
```

```python
import functools
import math

import jax
import jax.numpy as jnp
from jax import lax
from jax.experimental import pallas as pl
from jax.experimental.pallas import tpu as pltpu
from jax.sharding import PartitionSpec as P

LOCAL_QUERY_HEADS = 16
LOCAL_KEY_HEADS = 2
HEAD_SIZE = 128
PIECE = 256
PARTS = 2
SENT_STACKED = (False, True)
BACK_STACKED = (True, False)

epsilon = 1e-06
masked_score = -1e30
F32 = jnp.float32
BF16 = jnp.bfloat16
VMEM_LIMIT = 60 << 20


def dot(a, b, contract=((1,), (0,))):
    return lax.dot_general(a, b, (contract, ((), ())), preferred_element_type=F32)


def iota(shape, dim):
    return lax.broadcasted_iota(jnp.int32, shape, dim)


def slots_row(ids_row, capacity):
    n = ids_row.shape[1]
    names = iota((16, n), 0).astype(F32)
    chosen = names == ids_row
    before = (iota((n, n), 0) < iota((n, n), 1)).astype(F32).astype(BF16)
    earlier = dot(jnp.where(chosen, 1.0, 0.0).astype(BF16), before)
    return jnp.sum(jnp.where(chosen, earlier + names * capacity, 0.0), axis=0, keepdims=True)


def slots_column(ids_column, capacity):
    n = ids_column.shape[0]
    names = iota((n, 128), 1).astype(F32)
    chosen = names == ids_column
    before = (iota((n, n), 1) < iota((n, n), 0)).astype(F32).astype(BF16)
    earlier = dot(before, jnp.where(chosen, 1.0, 0.0).astype(BF16))
    return jnp.sum(jnp.where(chosen, earlier + names * capacity, 0.0), axis=1, keepdims=True)


def one_hot(matches):
    return jnp.where(matches, 1.0, 0.0).astype(BF16)


def shifted_slots(position, owner, experts, capacity):
    expert = jnp.bitwise_xor(position // capacity, owner)
    return (expert * capacity + lax.rem(position, capacity)).astype(F32)


def kernel_params():
    return pltpu.CompilerParams(vmem_limit_bytes=VMEM_LIMIT)


def entry(refs, d, owner):
    return refs[0].at[jnp.bitwise_xor(owner, d)] if len(refs) == 1 else refs[d]


def arrays(stacked, experts, shape):
    return [(experts,) + shape] if stacked else [shape] * experts


def brief():
    return pl.CostEstimate(flops=1000, bytes_accessed=1000, transcendentals=0)


def whole(*shape):
    return pl.BlockSpec(shape, lambda *_: (0,) * len(shape))


def smem():
    return pl.BlockSpec(memory_space=pltpu.SMEM)


def attend_kernel(experts, capacity, heads, n_ctx, where_ref, q_ref, ids_ref, *refs):
    count = n_ctx // 2 + 2
    own, own_core, *chips, cores = refs[:count]
    refs = refs[count:]
    blocks = [own, own_core]
    for j, chip in enumerate(chips):
        blocks += [chip, cores.at[j]]
    out_refs = []
    for stacked in SENT_STACKED:
        count = 1 if stacked else experts
        out_refs.append(refs[:count])
        refs = refs[count:]
    k_scr, v_scr, best_scr, acc_scr, att_scr = refs
    ctx, owner = where_ref[0], where_ref[1]
    seq = pl.program_id(0)
    block = q_ref.shape[1]
    tile = 2 * block
    factor = math.log2(math.e) / math.sqrt(HEAD_SIZE)

    @pl.when(seq == 0)
    def _():
        v_scr[:, :, HEAD_SIZE:] = jnp.ones((n_ctx, block, HEAD_SIZE), BF16)

    for m in range(n_ctx):
        index = jnp.bitwise_xor(ctx, m)
        k_scr[index] = blocks[m][0, :, :HEAD_SIZE]
        v_scr[index, :, :HEAD_SIZE] = blocks[m][0, :, HEAD_SIZE:]

    def fold(t, last):
        key_tile = k_scr[pl.ds(2 * t, 2)].reshape(tile, HEAD_SIZE)
        value_tile = v_scr[pl.ds(2 * t, 2)].reshape(tile, 2 * HEAD_SIZE)
        for h in range(heads):
            q = q_ref[0, :, h * HEAD_SIZE : (h + 1) * HEAD_SIZE]
            s = dot(q, key_tile, ((1,), (1,)))
            if last:
                key_pos = iota((block, tile), 1) + t * tile
                query_pos = iota((block, tile), 0) + ctx * block
                s = jnp.where(key_pos <= query_pos, s, masked_score)
            best = jnp.max(s, axis=1, keepdims=True)
            if not last:
                old = best_scr[h]
                best = jnp.maximum(old, best)
            p = jnp.exp2((s - best) * factor)
            blended = dot(p.astype(BF16), value_tile)
            if last:
                acc_scr[h] = blended
            else:
                acc_scr[h] = acc_scr[h] * jnp.exp2((old - best) * factor) + blended
            best_scr[h] = best

    fold(ctx // 2, True)

    @pl.loop(0, ctx // 2)
    def _(t):
        fold(t, False)

    for h in range(heads):
        acc = acc_scr[h]
        att = acc[:, :HEAD_SIZE] / acc[:, HEAD_SIZE:]
        att_scr[:, h * HEAD_SIZE : (h + 1) * HEAD_SIZE] = att.astype(BF16)

    n = ids_ref.shape[2]
    part = capacity // PARTS
    per_seq = block // n
    position = iota((experts * capacity, n), 0)
    slots = shifted_slots(position, owner, experts, capacity)
    for b in range(per_seq):
        source = seq * per_seq + b
        target = slots_row(ids_ref[source], capacity)
        picked = dot(one_hot(slots == target), att_scr[b * n : (b + 1) * n, :]).astype(BF16)
        for d in range(experts):
            rank = jnp.bitwise_xor(jnp.bitwise_xor(owner, d), source)
            for c in range(PARTS):
                first = d * capacity + c * part
                entry(out_refs[c], d, owner)[rank] = picked[first : first + part]


def attend(where, queries, key_values, ids, capacity):
    seqs, block, width = queries.shape
    n_ctx = 2 * (len(key_values) - 2)
    experts, _, n = ids.shape
    heads = width // HEAD_SIZE
    part = capacity // PARTS
    by_seq = pl.BlockSpec((1, block, 2 * HEAD_SIZE), lambda s: (s, 0, 0))
    shapes = []
    for stacked in SENT_STACKED:
        shapes += arrays(stacked, experts, (experts, part, width))
    outs = pl.pallas_call(
        functools.partial(attend_kernel, experts, capacity, heads, n_ctx),
        grid=(seqs,),
        in_specs=[
            smem(),
            pl.BlockSpec((1, block, width), lambda s: (s, 0, 0)),
            whole(experts, 1, n),
        ]
        + [by_seq] * (len(key_values) - 1)
        + [pl.BlockSpec((n_ctx // 2 - 1, 1, block, 2 * HEAD_SIZE), lambda s: (0, s, 0, 0))],
        out_specs=[whole(*shape) for shape in shapes],
        scratch_shapes=[
            pltpu.VMEM((n_ctx, block, HEAD_SIZE), BF16),
            pltpu.VMEM((n_ctx, block, 2 * HEAD_SIZE), BF16),
            pltpu.VMEM((heads, block, 1), F32),
            pltpu.VMEM((heads, block, 2 * HEAD_SIZE), F32),
            pltpu.VMEM((block, width), BF16),
        ],
        out_shape=[jax.ShapeDtypeStruct(shape, BF16) for shape in shapes],
        compiler_params=kernel_params(),
        cost_estimate=brief(),
        name="attend",
    )(where, queries, ids, *key_values)
    sent = []
    for stacked in SENT_STACKED:
        count = 1 if stacked else experts
        sent.append(list(outs[:count]))
        outs = outs[count:]
    return sent


def place_kernel(capacity, ids_ref, rows_ref, out_ref, pick_scr):
    @pl.when(pl.program_id(0) == 0)
    def _():
        position = iota(pick_scr.shape, 0)
        pick_scr[...] = one_hot(position.astype(F32) == slots_row(ids_ref[...], capacity))

    out_ref[...] = dot(pick_scr[...], rows_ref[...]).astype(BF16).reshape(out_ref.shape)


def place(ids_row, rows, experts, capacity):
    n, width = rows.shape
    cols = min(width, 1024)
    return pl.pallas_call(
        functools.partial(place_kernel, capacity),
        grid=(width // cols,),
        in_specs=[whole(1, n), pl.BlockSpec((n, cols), lambda i: (0, i))],
        out_specs=pl.BlockSpec((experts, capacity, cols), lambda i: (0, 0, i)),
        out_shape=jax.ShapeDtypeStruct((experts, capacity, width), BF16),
        scratch_shapes=[pltpu.VMEM((experts * capacity, n), BF16)],
        compiler_params=kernel_params(),
        cost_estimate=brief(),
        name="place",
    )(ids_row, rows)


def restore_kernel(experts, capacity, tiles, where_ref, ids_ref, *refs):
    *refs, layer_ref, grad_ref, pick_scr = refs
    parts = []
    for stacked in BACK_STACKED:
        count = 1 if stacked else experts
        parts.append(refs[:count])
        refs = refs[count:]
    owner = where_ref[1]
    step = pl.program_id(0)

    @pl.when(step == 0)
    def _():
        slots = shifted_slots(iota(pick_scr.shape, 1), owner, experts, capacity)
        pick_scr[...] = one_hot(slots == slots_column(ids_ref[...], capacity))

    rows = [entry(parts[c], d, owner)[...] for d in range(experts) for c in range(PARTS)]
    rows = jnp.concatenate(rows, axis=0)
    out = dot(pick_scr[...], rows).astype(BF16)

    @pl.when(step < tiles)
    def _():
        layer_ref[...] = out

    @pl.when(step >= tiles)
    def _():
        grad_ref[...] = out


def restore(where, ids_column, parts, experts, capacity):
    n = ids_column.shape[0]
    part, both = parts[0][0].shape[-2:]
    width = both // 2
    cols = min(width, 1024)
    tiles = width // cols
    flat = [x for values in parts for x in values]
    return pl.pallas_call(
        functools.partial(restore_kernel, experts, capacity, tiles),
        grid=(2 * tiles,),
        in_specs=[smem(), whole(n, 1)]
        + [
            pl.BlockSpec(x.shape[:-1] + (cols,), lambda i, zeros=(0,) * (x.ndim - 1): zeros + (i,))
            for x in flat
        ],
        out_specs=[
            pl.BlockSpec((n, cols), lambda i: (0, jnp.minimum(i, tiles - 1))),
            pl.BlockSpec((n, cols), lambda i: (0, jnp.maximum(i - tiles, 0))),
        ],
        out_shape=[jax.ShapeDtypeStruct((n, width), BF16)] * 2,
        scratch_shapes=[pltpu.VMEM((n, experts * capacity), BF16)],
        compiler_params=kernel_params(),
        cost_estimate=brief(),
        name="restore",
    )(where, ids_column, *flat)


def expert_kernel(pieces, experts, capacity, part_index, where_ref, *refs):
    count = 1 if SENT_STACKED[part_index] else experts
    att_refs, refs = refs[:count], refs[count:]
    grad_ref, own_ref, refs = refs[0], refs[1], refs[2:]
    count = pieces // 2 + 2
    w_refs, refs = refs[:count], refs[count:]
    gate_hbm, up_hbm, down_hbm, gain_ref, ids_ref, weight_ref = refs[:6]
    refs = refs[6:]
    count = 1 if BACK_STACKED[part_index] else experts
    out_refs, refs = refs[:count], refs[count:]
    normed_ref, back_ref, units_ref, back_gate_ref, back_up_ref = refs[:5]
    w_scr, gate_scr, up_scr, down_scr, hidden_scr, back_in_scr, sems = refs[5:]
    _, part, width = grad_ref.shape
    rows = experts * part
    att_cols = att_refs[0].shape[-1]
    piece = w_scr.shape[3]
    ff = units_ref.shape[1]
    piece_index, owner = where_ref[2], where_ref[1]
    sources = [jnp.bitwise_xor(owner, d) for d in range(experts)]

    own, own_core, *chips, cores = w_refs
    blocks = [own, own_core]
    for j, chip in enumerate(chips):
        blocks += [chip, cores.at[j]]
    copies = [
        pltpu.make_async_copy(block, w_scr.at[m], sems.at[m]) for m, block in enumerate(blocks)
    ]
    first = pieces
    weight_copies = (
        pltpu.make_async_copy(gate_hbm.at[0], gate_scr, sems.at[first]),
        pltpu.make_async_copy(up_hbm.at[0], up_scr, sems.at[first + 1]),
        pltpu.make_async_copy(down_hbm.at[0], down_scr, sems.at[first + 2]),
    )
    for copy in copies:
        copy.start()
    for copy in weight_copies:
        copy.start()

    n = ids_ref.shape[2]
    weights = []
    for s, source in enumerate(sources):
        target = slots_row(ids_ref[source], capacity)
        slot = iota((part, n), 0) + (owner * capacity + part_index * part)
        weights.append(
            jnp.sum(
                jnp.where(slot.astype(F32) == target, weight_ref[source], 0.0),
                axis=1,
                keepdims=True,
            )
        )
        grads = grad_ref[source].astype(F32)
        back_ref[s * part : (s + 1) * part, :] = (weights[s] * grads).astype(BF16)

    for m in range(pieces):
        copies[m].wait()
        column = pl.multiple_of(jnp.bitwise_xor(piece_index, m) * piece, piece)
        total = jnp.zeros((rows, piece), F32)
        for d in range(experts):
            block = own_ref[:, pl.ds(column, piece)] if d == 0 else w_scr[m, d - 1]
            total += dot(entry(att_refs, d, owner)[...].reshape(rows, att_cols), block)
        hidden_scr[:, pl.ds(column, piece)] = total.astype(BF16)

    squares = jnp.zeros((rows, 1), F32)
    for t in range(0, width, PIECE):
        hidden = hidden_scr[:, t : t + PIECE].astype(F32)
        squares += jnp.sum(hidden * hidden, axis=1, keepdims=True)
    inv = lax.rsqrt(squares / width + epsilon)
    for t in range(0, width, PIECE):
        hidden = hidden_scr[:, t : t + PIECE].astype(F32)
        normed_ref[:, t : t + PIECE] = (hidden * inv * gain_ref[:, t : t + PIECE]).astype(BF16)

    for copy in weight_copies:
        copy.wait()
    for f in range(0, ff, 256):
        gate_act = dot(normed_ref[...], gate_scr[:, f : f + 256])
        up_act = dot(normed_ref[...], up_scr[:, f : f + 256])
        back_units = dot(back_ref[...], down_scr[f : f + 256, :], ((1,), (1,)))
        sigma = 1.0 / (1.0 + jnp.exp(-gate_act))
        gated = gate_act * sigma
        units_ref[:, f : f + 256] = (gated * up_act).astype(BF16)
        back_gate = back_units * up_act * sigma * (1.0 + gate_act * (1.0 - sigma))
        back_gate_ref[:, f : f + 256] = back_gate.astype(BF16)
        back_up_ref[:, f : f + 256] = (back_units * gated).astype(BF16)

    weight = jnp.concatenate(weights, axis=0)
    moment = jnp.zeros((rows, 1), F32)
    for t in range(0, width, PIECE):
        hidden = hidden_scr[:, t : t + PIECE].astype(F32)
        result = dot(units_ref[...], down_scr[:, t : t + PIECE]).astype(BF16).astype(F32)
        layer = (hidden + weight * result).astype(BF16)
        for s in range(experts):
            entry(out_refs, s, owner)[:, t : t + PIECE] = layer[s * part : (s + 1) * part]
        back_in = dot(back_gate_ref[...], gate_scr[t : t + PIECE, :], ((1,), (1,)))
        back_in += dot(back_up_ref[...], up_scr[t : t + PIECE, :], ((1,), (1,)))
        back_in = back_in.astype(BF16)
        back_in_scr[:, t : t + PIECE] = back_in
        scaled = back_in.astype(F32) * gain_ref[:, t : t + PIECE]
        moment += jnp.sum(scaled * (hidden * inv), axis=1, keepdims=True)
    moment = moment / width
    for t in range(0, width, PIECE):
        unit = hidden_scr[:, t : t + PIECE].astype(F32) * inv
        scaled = back_in_scr[:, t : t + PIECE].astype(F32) * gain_ref[:, t : t + PIECE]
        change = inv * (scaled - unit * moment)
        for s in range(experts):
            grads = grad_ref[sources[s], :, t : t + PIECE].astype(F32)
            entry(out_refs, s, owner)[:, width + t : width + t + PIECE] = (
                grads + change[s * part : (s + 1) * part]
            ).astype(BF16)


def expert_part(
    where, att, grads, own, projection, gate, up, down, gain, ids, weights, capacity, index
):
    experts, part, att_cols = att[0].shape[-3:]
    pieces = 2 * (len(projection) - 2)
    piece = projection[0].shape[-1]
    width = grads.shape[2]
    ff = gate.shape[2]
    rows = experts * part
    n = ids.shape[2]
    out = lambda *shape: jax.ShapeDtypeStruct(shape, BF16)
    back = arrays(BACK_STACKED[index], experts, (part, 2 * width))
    in_hbm = pl.BlockSpec(memory_space=pl.ANY)
    outs = pl.pallas_call(
        functools.partial(expert_kernel, pieces, experts, capacity, index),
        grid=(1,),
        in_specs=[smem()]
        + [whole(*x.shape) for x in att]
        + [pl.BlockSpec((experts, part, width), lambda i: (0, index, 0))]
        + [whole(*own.shape)]
        + [in_hbm] * (len(projection) + 3)
        + [whole(1, width), whole(experts, 1, n), whole(experts, 1, n)],
        out_specs=[whole(*shape) for shape in back]
        + [whole(rows, width)] * 2
        + [whole(rows, ff)] * 3,
        scratch_shapes=[
            pltpu.VMEM((pieces, experts - 1, att_cols, piece), BF16),
            pltpu.VMEM((width, ff), BF16),
            pltpu.VMEM((width, ff), BF16),
            pltpu.VMEM((ff, width), BF16),
            pltpu.VMEM((rows, width), BF16),
            pltpu.VMEM((rows, width), BF16),
            pltpu.SemaphoreType.DMA((pieces + 3,)),
        ],
        out_shape=[out(*shape) for shape in back] + [out(rows, width)] * 2 + [out(rows, ff)] * 3,
        compiler_params=kernel_params(),
        cost_estimate=brief(),
        name="expert",
    )(where, *att, grads, own, *projection, gate, up, down, gain, ids, weights)
    return outs[: len(back)], outs[len(back) :]


def weight_kernel(count, *refs):
    normed, back, units, back_gate, back_up = [refs[i * count : (i + 1) * count] for i in range(5)]
    outs = refs[5 * count :]
    first = ((0,), (0,))

    def total(left, right):
        return sum(dot(a[...], b[...], first) for a, b in zip(left, right)).astype(BF16)

    gate, up, down = total(normed, back_gate), total(normed, back_up), total(units, back)
    if len(outs) == 3:
        outs[0][0], outs[1][0], outs[2][0] = gate, up, down
        return
    packed = outs[0]
    packed[0, 0] = gate
    packed[0, 1] = up
    cols = down.shape[1]
    for t in range(0, down.shape[0], cols):
        packed[0, 2, :, t : t + cols] = down[t : t + cols]


def weight_blocks(where, normed, back, units, back_gate, back_up, first=None):
    count = len(normed)
    rows, width = normed[0].shape
    ff = units[0].shape[1]
    cols = PIECE
    packed = first is not None
    blocks = width // cols // 2 if packed else width // cols

    def block_of(i, where_ref):
        return jnp.bitwise_xor(where_ref[0], 2 * i + first) if packed else i

    thin = [pl.BlockSpec((rows, cols), lambda i, w: (0, block_of(i, w)))] * count
    full = [pl.BlockSpec((rows, ff), lambda i, w: (0, 0))] * count
    shapes = [(3, cols, ff)] if packed else [(cols, ff), (cols, ff), (ff, cols)]
    return pl.pallas_call(
        lambda where_ref, *refs: weight_kernel(count, *refs),
        grid_spec=pltpu.PrefetchScalarGridSpec(
            num_scalar_prefetch=1,
            grid=(blocks,),
            in_specs=thin + thin + full + full + full,
            out_specs=[
                pl.BlockSpec((1,) + shape, lambda i, w, zeros=(0,) * len(shape): (i,) + zeros)
                for shape in shapes
            ],
        ),
        out_shape=[jax.ShapeDtypeStruct((blocks,) + shape, BF16) for shape in shapes],
        compiler_params=kernel_params(),
        cost_estimate=brief(),
        name="weight_grads",
    )(where, *normed, *back, *units, *back_gate, *back_up)


def partner(value, mask):
    count = lax.axis_size("ctx")
    return lax.ppermute(value, "ctx", [(i, i ^ mask) for i in range(count)])


def to_owner(value, mask):
    count = lax.axis_size("exp")
    return lax.ppermute(value, "exp", [(i, i ^ mask) for i in range(count)])


def to_owners(values):
    if len(values) == 1:
        return [lax.all_to_all(values[0], "exp", 0, 0, tiled=True)]
    return [values[0]] + [to_owner(values[d], d) for d in range(len(values) - 1, 0, -1)][::-1]


def from_chips(value, count):
    return [partner(value, m) for m in range(2, count, 2)]


def with_cores(value, own_core, chips):
    return [value, own_core, *chips, partner(jnp.stack(chips), 1)]


def halved(value, bits, order, ctx):
    shape = value.shape[1:]
    held = value.reshape((2,) * bits + shape)
    for place_in_order, bit in enumerate(order):
        axis = bits - 1 - bit
        mine = (ctx >> bit) & 1
        gone = lax.dynamic_slice_in_dim(held, 1 - mine, 1, axis)
        kept = lax.dynamic_slice_in_dim(held, mine, 1, axis)
        held = kept.astype(F32) + partner(gone, 1 << bit).astype(F32)
        if place_in_order < bits - 1:
            held = held.astype(BF16)
    return held.reshape(shape)


def on_device(
    queries,
    rotated_key_heads,
    value_head_rows,
    out_proj,
    norm_gain,
    expert_ids,
    gate_weights,
    expert_gate,
    expert_up,
    expert_down,
    grad_out,
):
    heads_dev = queries.shape[2] // HEAD_SIZE
    group = LOCAL_QUERY_HEADS // LOCAL_KEY_HEADS
    exp_count = lax.axis_size("exp")
    ctx_count = lax.axis_size("ctx")
    owner = lax.axis_index("exp")
    ctx = lax.axis_index("ctx")
    bits = ctx_count.bit_length() - 1
    n, _ = expert_ids.shape
    width = grad_out.shape[1]
    experts = exp_count
    capacity = min(n, 2 * n // experts)
    pieces = min(ctx_count, width // PIECE)
    piece = width // pieces
    piece_index = ctx % pieces
    where = jnp.stack([ctx, owner, piece_index]).astype(jnp.int32)

    ids_f = expert_ids.astype(F32)
    info = jnp.stack([ids_f[:, 0], gate_weights[:, 0]])
    info = lax.all_gather(info, "exp")
    ids_all, weights_all = info[:, 0:1, :], info[:, 1:2, :]

    grads = place(ids_f.reshape(1, n), grad_out, experts, capacity)

    first_column = (owner * heads_dev // group) * HEAD_SIZE
    keys = lax.dynamic_slice_in_dim(rotated_key_heads, first_column, HEAD_SIZE, 2)
    values = lax.dynamic_slice_in_dim(value_head_rows, first_column, HEAD_SIZE, 2)
    own = jnp.concatenate([keys, values], axis=2)
    grads = lax.all_to_all(grads, "exp", 0, 0, tiled=True)
    chips = from_chips(own, ctx_count)

    mine = lax.dynamic_slice_in_dim(out_proj, piece_index * piece, piece, 1)
    mine = lax.all_gather(mine, "exp", axis=0)
    mine, chips = lax.optimization_barrier((mine, chips))
    key_values = with_cores(own, partner(own, 1), chips)
    mine = jnp.concatenate(
        [lax.dynamic_slice_in_dim(mine, owner ^ d, 1, 0) for d in range(1, exp_count)]
    )
    own_core = partner(mine, 1)
    chips = from_chips(mine, pieces)

    attended = attend(where, queries, key_values, ids_all, capacity)
    attended[0], grads = lax.optimization_barrier((attended[0], grads))
    arrived = [to_owners(attended[0])]
    chips, attended[1] = lax.optimization_barrier((chips, attended[1]))
    projection = with_cores(mine, own_core, chips)
    arrived[0], later = lax.optimization_barrier((arrived[0], attended[1]))
    arrived.append(to_owners(later))

    rows, kept = [], []
    for index, att in enumerate(arrived):
        out, saved = expert_part(
            where,
            att,
            grads,
            out_proj,
            projection,
            expert_gate,
            expert_up,
            expert_down,
            norm_gain.reshape(1, width),
            ids_all,
            weights_all,
            capacity,
            index,
        )
        rows.append(out)
        kept.append(saved)
    returned = [to_owners(rows[0])]

    rows_dev = width // ctx_count
    ff = expert_gate.shape[2]
    if rows_dev == PIECE:
        (gone,) = weight_blocks(where, *zip(*kept), first=1)
        near = partner(gone, 1)
        (stay,) = weight_blocks(where, *zip(*kept), first=0)
        pair = [(stay[j].astype(F32) + near[j].astype(F32)).astype(BF16) for j in range(len(stay))]
        far = [partner(x, 2 * j + 2) for j, x in enumerate(pair[1:])]
        total = sum([x.astype(F32) for x in far], pair[0].astype(F32))
        grad_gate, grad_up = total[0][None], total[1][None]
        grad_down = total[2].reshape(PIECE, ff // PIECE, PIECE).transpose(1, 0, 2)
        grad_down = grad_down.reshape(1, ff, PIECE)
    else:
        gone = weight_blocks(where, *zip(*kept))
        part_gate, part_up = [x.reshape(ctx_count, rows_dev, ff) for x in gone[:2]]
        part_down = gone[2].reshape(width // PIECE, ff, PIECE // rows_dev, rows_dev)
        part_down = part_down.transpose(0, 2, 1, 3).reshape(ctx_count, ff, rows_dev)
        order = list(range(bits))
        grad_gate, grad_up, grad_down = [
            halved(x, bits, order, ctx)[None] for x in (part_gate, part_up, part_down)
        ]
    returned += [to_owners(out) for out in rows[1:]]
    returned, grad_gate, grad_up, grad_down = lax.optimization_barrier(
        (returned, grad_gate, grad_up, grad_down)
    )

    layer_out, grad_hidden = restore(where, ids_f, returned, experts, capacity)
    return (layer_out, grad_hidden, grad_gate, grad_up, grad_down)


def solution(mesh):
    in_specs = (
        P(None, "ctx", "exp"),
        P(None, "ctx", None),
        P(None, "ctx", None),
        P("exp", None),
        P(),
        P(("ctx", "exp"), None),
        P(("ctx", "exp"), None),
        P("exp", None, None),
        P("exp", None, None),
        P("exp", None, None),
        P(("ctx", "exp"), None),
    )
    out_specs = (
        P(("ctx", "exp"), None),
        P(("ctx", "exp"), None),
        P("exp", "ctx", None),
        P("exp", "ctx", None),
        P("exp", None, "ctx"),
    )
    return jax.shard_map(
        on_device, mesh=mesh, in_specs=in_specs, out_specs=out_specs, check_vma=False
    )
```

```python
import functools
import math

import jax
import jax.numpy as jnp
from jax import lax
from jax.experimental import pallas as pl
from jax.experimental.pallas import tpu as pltpu
from jax.sharding import PartitionSpec as P

LOCAL_QUERY_HEADS = 16
LOCAL_KEY_HEADS = 2
HEAD_SIZE = 128
PIECE = 256
PARTS = 2

epsilon = 1e-06
masked_score = -1e30
F32 = jnp.float32
BF16 = jnp.bfloat16
VMEM_LIMIT = 60 << 20


def dot(a, b, contract=((1,), (0,))):
    return lax.dot_general(a, b, (contract, ((), ())), preferred_element_type=F32)


def iota(shape, dim):
    return lax.broadcasted_iota(jnp.int32, shape, dim)


def slots_row(ids_row, capacity):
    n = ids_row.shape[1]
    names = iota((16, n), 0).astype(F32)
    chosen = names == ids_row
    before = (iota((n, n), 0) < iota((n, n), 1)).astype(F32).astype(BF16)
    earlier = dot(jnp.where(chosen, 1.0, 0.0).astype(BF16), before)
    return jnp.sum(jnp.where(chosen, earlier + names * capacity, 0.0), axis=0, keepdims=True)


def slots_column(ids_column, capacity):
    n = ids_column.shape[0]
    names = iota((n, 128), 1).astype(F32)
    chosen = names == ids_column
    before = (iota((n, n), 1) < iota((n, n), 0)).astype(F32).astype(BF16)
    earlier = dot(before, jnp.where(chosen, 1.0, 0.0).astype(BF16))
    return jnp.sum(jnp.where(chosen, earlier + names * capacity, 0.0), axis=1, keepdims=True)


def one_hot(matches):
    return jnp.where(matches, 1.0, 0.0).astype(BF16)


def shifted_slots(position, owner, experts, capacity):
    expert = jnp.bitwise_xor(position // capacity, owner)
    return (expert * capacity + lax.rem(position, capacity)).astype(F32)


def kernel_params():
    return pltpu.CompilerParams(vmem_limit_bytes=VMEM_LIMIT)


def brief():
    return pl.CostEstimate(flops=1000, bytes_accessed=1000, transcendentals=0)


def whole(*shape):
    return pl.BlockSpec(shape, lambda *_: (0,) * len(shape))


def smem():
    return pl.BlockSpec(memory_space=pltpu.SMEM)


def attend_kernel(experts, capacity, heads, n_ctx, where_ref, q_ref, ids_ref, *refs):
    count = n_ctx // 2 + 1
    *chips, cores = refs[:count]
    refs = refs[count:]
    blocks = []
    for j, chip in enumerate(chips):
        blocks += [chip, cores.at[j]]
    out_refs, refs = refs[: experts * PARTS], refs[experts * PARTS :]
    k_scr, v_scr, best_scr, acc_scr, att_scr = refs
    ctx, owner = where_ref[0], where_ref[1]
    seq = pl.program_id(0)
    block = q_ref.shape[1]
    tile = 2 * block
    factor = math.log2(math.e) / math.sqrt(HEAD_SIZE)

    @pl.when(seq == 0)
    def _():
        v_scr[:, :, HEAD_SIZE:] = jnp.ones((n_ctx, block, HEAD_SIZE), BF16)

    for m in range(n_ctx):
        index = jnp.bitwise_xor(ctx, m)
        k_scr[index] = blocks[m][0, :, :HEAD_SIZE]
        v_scr[index, :, :HEAD_SIZE] = blocks[m][0, :, HEAD_SIZE:]

    def fold(t, last):
        key_tile = k_scr[pl.ds(2 * t, 2)].reshape(tile, HEAD_SIZE)
        value_tile = v_scr[pl.ds(2 * t, 2)].reshape(tile, 2 * HEAD_SIZE)
        for h in range(heads):
            q = q_ref[0, :, h * HEAD_SIZE : (h + 1) * HEAD_SIZE]
            s = dot(q, key_tile, ((1,), (1,)))
            if last:
                key_pos = iota((block, tile), 1) + t * tile
                query_pos = iota((block, tile), 0) + ctx * block
                s = jnp.where(key_pos <= query_pos, s, masked_score)
            best = jnp.max(s, axis=1, keepdims=True)
            if not last:
                old = best_scr[h]
                best = jnp.maximum(old, best)
            p = jnp.exp2((s - best) * factor)
            blended = dot(p.astype(BF16), value_tile)
            if last:
                acc_scr[h] = blended
            else:
                acc_scr[h] = acc_scr[h] * jnp.exp2((old - best) * factor) + blended
            best_scr[h] = best

    fold(ctx // 2, True)

    @pl.loop(0, ctx // 2)
    def _(t):
        fold(t, False)

    for h in range(heads):
        acc = acc_scr[h]
        att = acc[:, :HEAD_SIZE] / acc[:, HEAD_SIZE:]
        att_scr[:, h * HEAD_SIZE : (h + 1) * HEAD_SIZE] = att.astype(BF16)

    n = ids_ref.shape[2]
    part = capacity // PARTS
    per_seq = block // n
    position = iota((experts * capacity, n), 0)
    slots = shifted_slots(position, owner, experts, capacity)
    for b in range(per_seq):
        source = seq * per_seq + b
        target = slots_row(ids_ref[source], capacity)
        picked = dot(one_hot(slots == target), att_scr[b * n : (b + 1) * n, :]).astype(BF16)
        for d in range(experts):
            rank = jnp.bitwise_xor(jnp.bitwise_xor(owner, d), source)
            for c in range(PARTS):
                first = d * capacity + c * part
                out_refs[c * experts + d][rank] = picked[first : first + part]


def attend(where, queries, key_values, ids, capacity):
    seqs, block, width = queries.shape
    n_ctx = 2 * (len(key_values) - 1)
    experts, _, n = ids.shape
    heads = width // HEAD_SIZE
    part = capacity // PARTS
    by_seq = pl.BlockSpec((1, block, 2 * HEAD_SIZE), lambda s: (s, 0, 0))
    outs = pl.pallas_call(
        functools.partial(attend_kernel, experts, capacity, heads, n_ctx),
        grid=(seqs,),
        in_specs=[
            smem(),
            pl.BlockSpec((1, block, width), lambda s: (s, 0, 0)),
            whole(experts, 1, n),
        ]
        + [by_seq] * (len(key_values) - 1)
        + [pl.BlockSpec((n_ctx // 2, 1, block, 2 * HEAD_SIZE), lambda s: (0, s, 0, 0))],
        out_specs=[whole(experts, part, width)] * (PARTS * experts),
        scratch_shapes=[
            pltpu.VMEM((n_ctx, block, HEAD_SIZE), BF16),
            pltpu.VMEM((n_ctx, block, 2 * HEAD_SIZE), BF16),
            pltpu.VMEM((heads, block, 1), F32),
            pltpu.VMEM((heads, block, 2 * HEAD_SIZE), F32),
            pltpu.VMEM((block, width), BF16),
        ],
        out_shape=[jax.ShapeDtypeStruct((experts, part, width), BF16)] * (PARTS * experts),
        compiler_params=kernel_params(),
        cost_estimate=brief(),
        name="attend",
    )(where, queries, ids, *key_values)
    return [outs[c * experts : (c + 1) * experts] for c in range(PARTS)]


def place_kernel(experts, capacity, where_ref, ids_ref, rows_ref, *refs):
    out_refs, pick_scr = refs[:-1], refs[-1]

    @pl.when(pl.program_id(0) == 0)
    def _():
        position = iota(pick_scr.shape, 0)
        slots = shifted_slots(position, where_ref[1], experts, capacity)
        pick_scr[...] = one_hot(slots == slots_row(ids_ref[...], capacity))

    picked = dot(pick_scr[...], rows_ref[...]).astype(BF16)
    for d, ref in enumerate(out_refs):
        ref[...] = picked[d * capacity : (d + 1) * capacity]


def place(where, ids_row, rows, experts, capacity):
    n, width = rows.shape
    cols = min(width, 1024)
    return pl.pallas_call(
        functools.partial(place_kernel, experts, capacity),
        grid=(width // cols,),
        in_specs=[smem(), whole(1, n), pl.BlockSpec((n, cols), lambda i: (0, i))],
        out_specs=[pl.BlockSpec((capacity, cols), lambda i: (0, i))] * experts,
        out_shape=[jax.ShapeDtypeStruct((capacity, width), BF16)] * experts,
        scratch_shapes=[pltpu.VMEM((experts * capacity, n), BF16)],
        compiler_params=kernel_params(),
        cost_estimate=brief(),
        name="place",
    )(where, ids_row, rows)


def restore_kernel(experts, capacity, where_ref, ids_ref, *refs):
    *parts, out_ref, pick_scr = refs

    @pl.when(pl.program_id(0) == 0)
    def _():
        slots = shifted_slots(iota(pick_scr.shape, 1), where_ref[1], experts, capacity)
        pick_scr[...] = one_hot(slots == slots_column(ids_ref[...], capacity))

    rows = jnp.concatenate([ref[...] for ref in parts], axis=0)
    out_ref[...] = dot(pick_scr[...], rows).astype(BF16)


def restore(where, ids_column, parts, experts, capacity):
    n = ids_column.shape[0]
    part, width = parts[0][0].shape
    cols = min(width, 1024)
    return pl.pallas_call(
        functools.partial(restore_kernel, experts, capacity),
        grid=(width // cols,),
        in_specs=[smem(), whole(n, 1)]
        + [pl.BlockSpec((part, cols), lambda i: (0, i))] * (experts * PARTS),
        out_specs=pl.BlockSpec((n, cols), lambda i: (0, i)),
        out_shape=jax.ShapeDtypeStruct((n, width), BF16),
        scratch_shapes=[pltpu.VMEM((n, experts * capacity), BF16)],
        compiler_params=kernel_params(),
        cost_estimate=brief(),
        name="restore",
    )(where, ids_column, *[parts[c][d] for d in range(experts) for c in range(PARTS)])


def expert_kernel(experts, capacity, part_index, swap, where_ref, *refs):
    att_refs, refs = refs[:experts], refs[experts:]
    grad_refs, refs = refs[:experts], refs[experts:]
    own_ref, same_hbm, other_hbm, gate_hbm, up_hbm, down_hbm = refs[:6]
    gain_ref, ids_ref, weight_ref, refs = refs[6], refs[7], refs[8], refs[9:]
    layer_refs, refs = refs[:experts], refs[experts:]
    change_refs, refs = refs[:experts], refs[experts:]
    saved_refs, refs = refs[: 1 + swap], refs[1 + swap :]
    w_scr, gate_scr, up_scr, down_scr, hidden_scr, normed_ref, back_ref, back_in_scr, sems = refs
    part, width = grad_refs[0].shape
    rows = experts * part
    att_cols = att_refs[0].shape[-1]
    pieces, _, _, piece = w_scr.shape
    ff = gate_scr.shape[1]
    core, owner = jnp.bitwise_and(where_ref[0], 1), where_ref[1]
    sources = [jnp.bitwise_xor(owner, d) for d in range(experts)]
    units_at, gate_at, up_at, normed_at = 0, ff, 2 * ff, 3 * ff

    copies = []
    for q in range(pieces // 2):
        for ref in (same_hbm, other_hbm):
            m = len(copies)
            copies.append(pltpu.make_async_copy(ref.at[q], w_scr.at[m], sems.at[m]))
    weight_copies = (
        pltpu.make_async_copy(gate_hbm.at[0], gate_scr, sems.at[pieces]),
        pltpu.make_async_copy(up_hbm.at[0], up_scr, sems.at[pieces + 1]),
        pltpu.make_async_copy(down_hbm.at[0], down_scr, sems.at[pieces + 2]),
    )
    for copy in copies:
        copy.start()
    for copy in weight_copies:
        copy.start()

    n = ids_ref.shape[2]
    weights = []
    for s, source in enumerate(sources):
        target = slots_row(ids_ref[source], capacity)
        slot = iota((part, n), 0) + (owner * capacity + part_index * part)
        weights.append(
            jnp.sum(
                jnp.where(slot.astype(F32) == target, weight_ref[source], 0.0),
                axis=1,
                keepdims=True,
            )
        )
        grads = grad_refs[s][...].astype(F32)
        back_ref[s * part : (s + 1) * part, :] = (weights[s] * grads).astype(BF16)

    for m in range(pieces):
        copies[m].wait()
        index = m + core if m % 2 == 0 else m - core
        column = pl.multiple_of(index * piece, piece)
        total = jnp.zeros((rows, piece), F32)
        for d in range(experts):
            block = own_ref[:, pl.ds(column, piece)] if d == 0 else w_scr[m, d - 1]
            total += dot(att_refs[d][...].reshape(rows, att_cols), block)
        hidden_scr[:, pl.ds(column, piece)] = total.astype(BF16)

    squares = jnp.zeros((rows, 1), F32)
    for t in range(0, width, PIECE):
        hidden = hidden_scr[:, t : t + PIECE].astype(F32)
        squares += jnp.sum(hidden * hidden, axis=1, keepdims=True)
    inv = lax.rsqrt(squares / width + epsilon)
    for t in range(0, width, PIECE):
        hidden = hidden_scr[:, t : t + PIECE].astype(F32)
        normed_ref[:, t : t + PIECE] = (hidden * inv * gain_ref[:, t : t + PIECE]).astype(BF16)

    for copy in weight_copies:
        copy.wait()
    for f in range(0, ff, 256):
        gate_act = dot(normed_ref[...], gate_scr[:, f : f + 256])
        up_act = dot(normed_ref[...], up_scr[:, f : f + 256])
        back_units = dot(back_ref[...], down_scr[f : f + 256, :], ((1,), (1,)))
        sigma = 1.0 / (1.0 + jnp.exp(-gate_act))
        gated = gate_act * sigma
        units = (gated * up_act).astype(BF16)
        back_gate = back_units * up_act * sigma * (1.0 + gate_act * (1.0 - sigma))
        back_gate = back_gate.astype(BF16)
        back_up = (back_units * gated).astype(BF16)
        for ref in saved_refs:
            ref[:, units_at + f : units_at + f + 256] = units
            ref[:, gate_at + f : gate_at + f + 256] = back_gate
            ref[:, up_at + f : up_at + f + 256] = back_up

    saved = saved_refs[0]
    half = width // len(saved_refs)
    for c, ref in enumerate(saved_refs):
        for t in range(half // PIECE):
            if swap:
                block = 2 * t + (core if c == 0 else 1 - core)
                column = pl.multiple_of(block * PIECE, PIECE)
            else:
                column = t * PIECE
            at = normed_at + t * PIECE
            ref[:, at : at + PIECE] = normed_ref[:, pl.ds(column, PIECE)]
            ref[:, at + half : at + half + PIECE] = back_ref[:, pl.ds(column, PIECE)]

    weight = jnp.concatenate(weights, axis=0)
    moment = jnp.zeros((rows, 1), F32)
    for t in range(0, width, PIECE):
        hidden = hidden_scr[:, t : t + PIECE].astype(F32)
        result = dot(saved[:, units_at:gate_at], down_scr[:, t : t + PIECE])
        layer = (hidden + weight * result.astype(BF16).astype(F32)).astype(BF16)
        for s in range(experts):
            layer_refs[s][:, t : t + PIECE] = layer[s * part : (s + 1) * part]
        back_in = dot(saved[:, gate_at:up_at], gate_scr[t : t + PIECE, :], ((1,), (1,)))
        back_in += dot(saved[:, up_at:normed_at], up_scr[t : t + PIECE, :], ((1,), (1,)))
        back_in = back_in.astype(BF16)
        back_in_scr[:, t : t + PIECE] = back_in
        scaled = back_in.astype(F32) * gain_ref[:, t : t + PIECE]
        moment += jnp.sum(scaled * (hidden * inv), axis=1, keepdims=True)
    moment = moment / width
    for t in range(0, width, PIECE):
        unit = hidden_scr[:, t : t + PIECE].astype(F32) * inv
        scaled = back_in_scr[:, t : t + PIECE].astype(F32) * gain_ref[:, t : t + PIECE]
        change = inv * (scaled - unit * moment)
        for s in range(experts):
            grads = grad_refs[s][:, t : t + PIECE].astype(F32)
            change_refs[s][:, t : t + PIECE] = (
                grads + change[s * part : (s + 1) * part]
            ).astype(BF16)


def expert_part(
    where, att, grads, own, same, other, gate, up, down, gain, ids, weights, capacity, index, swap
):
    experts, part, att_cols = att[0].shape
    pieces = 2 * same.shape[0]
    piece = same.shape[-1]
    width = grads[0].shape[1]
    ff = gate.shape[2]
    rows = experts * part
    n = ids.shape[2]
    half = width // 2 if swap else width
    out = lambda *shape: jax.ShapeDtypeStruct(shape, BF16)
    in_hbm = pl.BlockSpec(memory_space=pl.ANY)
    outs = pl.pallas_call(
        functools.partial(expert_kernel, experts, capacity, index, swap),
        grid=(1,),
        in_specs=[smem()]
        + [whole(*x.shape) for x in att]
        + [pl.BlockSpec((part, width), lambda i: (index, 0))] * experts
        + [whole(*own.shape)]
        + [in_hbm] * 5
        + [whole(1, width), whole(experts, 1, n), whole(experts, 1, n)],
        out_specs=[whole(part, width)] * (2 * experts)
        + [whole(rows, 3 * ff + 2 * half)] * (1 + swap),
        scratch_shapes=[
            pltpu.VMEM((pieces, experts - 1, att_cols, piece), BF16),
            pltpu.VMEM((width, ff), BF16),
            pltpu.VMEM((width, ff), BF16),
            pltpu.VMEM((ff, width), BF16),
            pltpu.VMEM((rows, width), BF16),
            pltpu.VMEM((rows, width), BF16),
            pltpu.VMEM((rows, width), BF16),
            pltpu.VMEM((rows, width), BF16),
            pltpu.SemaphoreType.DMA((pieces + 3,)),
        ],
        out_shape=[out(part, width)] * (2 * experts)
        + [out(rows, 3 * ff + 2 * half)] * (1 + swap),
        compiler_params=kernel_params(),
        cost_estimate=brief(),
        name="expert",
    )(where, *att, *grads, own, same, other, gate, up, down, gain, ids, weights)
    return outs[:experts], outs[experts : 2 * experts], outs[2 * experts :]


def weight_kernel(count, *refs):
    units, back_gate, back_up, normed, back = [refs[i * count : (i + 1) * count] for i in range(5)]
    out_ref = refs[5 * count]
    first = ((0,), (0,))

    def total(left, right):
        return sum(dot(a[...], b[...], first) for a, b in zip(left, right)).astype(BF16)

    out_ref[0, 0] = total(normed, back_gate)
    out_ref[0, 1] = total(normed, back_up)
    down = total(units, back)
    cols = down.shape[1]
    for t in range(0, down.shape[0], cols):
        out_ref[0, 2, :, t : t + cols] = down[t : t + cols]


def weight_blocks(saved, blocks, ff):
    count = len(saved)
    rows, total = saved[0].shape
    normed_at = 3 * ff // PIECE
    back_at = normed_at + blocks
    thin = lambda at: [pl.BlockSpec((rows, PIECE), lambda i: (0, at + i))] * count
    full = lambda at: [pl.BlockSpec((rows, ff), lambda i: (0, at))] * count
    return pl.pallas_call(
        functools.partial(weight_kernel, count),
        grid=(blocks,),
        in_specs=full(0) + full(1) + full(2) + thin(normed_at) + thin(back_at),
        out_specs=pl.BlockSpec((1, 3, PIECE, ff), lambda i: (i, 0, 0, 0)),
        out_shape=jax.ShapeDtypeStruct((blocks, 3, PIECE, ff), BF16),
        compiler_params=kernel_params(),
        cost_estimate=brief(),
        name="weight_grads",
    )(*saved * 5)


def partner(value, mask):
    count = lax.axis_size("ctx")
    return lax.ppermute(value, "ctx", [(i, i ^ mask) for i in range(count)])


def to_owner(value, mask):
    count = lax.axis_size("exp")
    return lax.ppermute(value, "exp", [(i, i ^ mask) for i in range(count)])


def to_owners(values):
    return [values[0]] + [to_owner(values[d], d) for d in range(len(values) - 1, 0, -1)][::-1]


def chip_groups(count):
    return [
        list(range(first + core, first + count, 2))
        for first in range(0, lax.axis_size("ctx"), count)
        for core in range(2)
    ]


def after(value, *others):
    return lax.optimization_barrier((value, others))[0]


def halved(value, bits, order, ctx):
    shape = value.shape[1:]
    held = value.reshape((2,) * bits + shape)
    for place_in_order, bit in enumerate(order):
        axis = bits - 1 - bit
        mine = (ctx >> bit) & 1
        gone = lax.dynamic_slice_in_dim(held, 1 - mine, 1, axis)
        kept = lax.dynamic_slice_in_dim(held, mine, 1, axis)
        held = kept.astype(F32) + partner(gone, 1 << bit).astype(F32)
        if place_in_order < bits - 1:
            held = held.astype(BF16)
    return held.reshape(shape)


def on_device(
    queries,
    rotated_key_heads,
    value_head_rows,
    out_proj,
    norm_gain,
    expert_ids,
    gate_weights,
    expert_gate,
    expert_up,
    expert_down,
    grad_out,
):
    heads_dev = queries.shape[2] // HEAD_SIZE
    group = LOCAL_QUERY_HEADS // LOCAL_KEY_HEADS
    exp_count = lax.axis_size("exp")
    ctx_count = lax.axis_size("ctx")
    owner = lax.axis_index("exp")
    ctx = lax.axis_index("ctx")
    bits = ctx_count.bit_length() - 1
    n, _ = expert_ids.shape
    width = grad_out.shape[1]
    experts = exp_count
    capacity = min(n, 2 * n // experts)
    pieces = min(ctx_count, width // PIECE)
    piece = width // pieces
    piece_index = ctx % pieces
    where = jnp.stack([ctx, owner, piece_index]).astype(jnp.int32)

    ids_f = expert_ids.astype(F32)
    info = jnp.stack([ids_f[:, 0], gate_weights[:, 0]])
    info = jnp.broadcast_to(info[None], (exp_count,) + info.shape)
    info = lax.all_to_all(info, "exp", 0, 0, tiled=True)
    ids_all, weights_all = info[:, 0:1, :], info[:, 1:2, :]

    mine = lax.dynamic_slice_in_dim(out_proj, piece_index * piece, piece, 1)
    projection = to_owners([mine] * exp_count)[1:]

    first_column = (owner * heads_dev // group) * HEAD_SIZE
    keys = lax.dynamic_slice_in_dim(rotated_key_heads, first_column, HEAD_SIZE, 2)
    values = lax.dynamic_slice_in_dim(value_head_rows, first_column, HEAD_SIZE, 2)
    own = jnp.concatenate([keys, values], axis=2)
    chips = [own] + [partner(own, m) for m in range(2, ctx_count, 2)]
    key_values = chips + [partner(jnp.stack(chips), 1)]

    grads = place(where, ids_f.reshape(1, n), grad_out, experts, capacity)
    grads = to_owners(after(grads, projection))

    projection = after(jnp.stack(projection), chips)
    projection = jnp.broadcast_to(projection[None], (pieces // 2,) + projection.shape)
    same = lax.all_to_all(
        projection, "ctx", 0, 0, axis_index_groups=chip_groups(pieces), tiled=True
    )

    sent = attend(where, after(queries, grads[1]), key_values, ids_all, capacity)
    arrived = to_owners(after(sent[0], grads))
    later = after(sent[1], arrived, same)
    same = after(same, arrived[1])
    other = partner(same, 1)

    rows_dev = width // ctx_count
    ff = expert_gate.shape[2]
    swap = rows_dev == PIECE

    def run(index, arrived):
        return expert_part(
            where,
            arrived,
            grads,
            out_proj,
            same,
            other,
            expert_gate,
            expert_up,
            expert_down,
            norm_gain.reshape(1, width),
            ids_all,
            weights_all,
            capacity,
            index,
            swap,
        )

    layer_a, change_a, saved_a = run(0, arrived)
    layer_a = to_owners(layer_a)
    layer_b, change_b, saved_b = run(1, to_owners(later))
    if swap:
        saved = [saved_a[0], partner(saved_a[1], 1)]
        saved += [saved_b[0], partner(after(saved_b[1], layer_a), 1)]
        change_a = to_owners(after(change_a, layer_a))
        parts = weight_blocks(saved, width // PIECE // 2, ff)
        layer_b = after(layer_b, parts)
        parts = lax.all_to_all(
            parts, "ctx", 0, 0, axis_index_groups=chip_groups(ctx_count), tiled=True
        )
        total = jnp.sum(parts.astype(F32), axis=0)
        grad_gate, grad_up = total[0][None], total[1][None]
        grad_down = total[2].reshape(PIECE, ff // PIECE, PIECE).transpose(1, 0, 2)
        grad_down = grad_down.reshape(1, ff, PIECE)
    else:
        change_a = to_owners(after(change_a, layer_a))
        blocks = width // PIECE
        parts = weight_blocks(list(saved_a) + list(saved_b), blocks, ff)
        part_down = parts[:, 2].reshape(blocks, PIECE, ff // PIECE, PIECE).transpose(0, 2, 1, 3)
        part_down = part_down.reshape(blocks, ff, PIECE // rows_dev, rows_dev)
        part_down = part_down.transpose(0, 2, 1, 3).reshape(ctx_count, ff, rows_dev)
        order = list(range(bits))
        grad_gate, grad_up, grad_down = [
            halved(x.reshape((ctx_count,) + shape), bits, order, ctx)[None]
            for x, shape in (
                (parts[:, 0], (rows_dev, ff)),
                (parts[:, 1], (rows_dev, ff)),
                (part_down, (ff, rows_dev)),
            )
        ]
    layer_b = to_owners(after(layer_b, change_a))
    change_b = to_owners(after(change_b, layer_b[1:2]))
    layer_out = restore(where, ids_f, [layer_a, layer_b], experts, capacity)
    change_b = after(change_b, layer_out, grad_gate, grad_up, grad_down)
    grad_hidden = restore(where, ids_f, [change_a, change_b], experts, capacity)
    return (layer_out, grad_hidden, grad_gate, grad_up, grad_down)


def solution(mesh):
    in_specs = (
        P(None, "ctx", "exp"),
        P(None, "ctx", None),
        P(None, "ctx", None),
        P("exp", None),
        P(),
        P(("ctx", "exp"), None),
        P(("ctx", "exp"), None),
        P("exp", None, None),
        P("exp", None, None),
        P("exp", None, None),
        P(("ctx", "exp"), None),
    )
    out_specs = (
        P(("ctx", "exp"), None),
        P(("ctx", "exp"), None),
        P("exp", "ctx", None),
        P("exp", "ctx", None),
        P("exp", None, "ctx"),
    )
    return jax.shard_map(
        on_device, mesh=mesh, in_specs=in_specs, out_specs=out_specs, check_vma=False
    )
```

```python
import functools
import math

import jax
import jax.numpy as jnp
from jax import lax
from jax.experimental import pallas as pl
from jax.experimental.pallas import tpu as pltpu
from jax.sharding import PartitionSpec as P

LOCAL_QUERY_HEADS = 16
LOCAL_KEY_HEADS = 2
HEAD_SIZE = 128
PIECE = 256
PARTS = 2

epsilon = 1e-06
masked_score = -1e30
F32 = jnp.float32
BF16 = jnp.bfloat16
VMEM_LIMIT = 60 << 20


def dot(a, b, contract=((1,), (0,))):
    return lax.dot_general(a, b, (contract, ((), ())), preferred_element_type=F32)


def iota(shape, dim):
    return lax.broadcasted_iota(jnp.int32, shape, dim)


def slots_row(ids_row, capacity):
    n = ids_row.shape[1]
    names = iota((16, n), 0).astype(F32)
    chosen = names == ids_row
    before = (iota((n, n), 0) < iota((n, n), 1)).astype(F32).astype(BF16)
    earlier = dot(jnp.where(chosen, 1.0, 0.0).astype(BF16), before)
    return jnp.sum(jnp.where(chosen, earlier + names * capacity, 0.0), axis=0, keepdims=True)


def slots_column(ids_column, capacity):
    n = ids_column.shape[0]
    names = iota((n, 128), 1).astype(F32)
    chosen = names == ids_column
    before = (iota((n, n), 1) < iota((n, n), 0)).astype(F32).astype(BF16)
    earlier = dot(before, jnp.where(chosen, 1.0, 0.0).astype(BF16))
    return jnp.sum(jnp.where(chosen, earlier + names * capacity, 0.0), axis=1, keepdims=True)


def one_hot(matches):
    return jnp.where(matches, 1.0, 0.0).astype(BF16)


def shifted_slots(position, owner, experts, capacity):
    expert = jnp.bitwise_xor(position // capacity, owner)
    return (expert * capacity + lax.rem(position, capacity)).astype(F32)


def kernel_params():
    return pltpu.CompilerParams(vmem_limit_bytes=VMEM_LIMIT)


def brief():
    return pl.CostEstimate(flops=1000, bytes_accessed=1000, transcendentals=0)


def whole(*shape):
    return pl.BlockSpec(shape, lambda *_: (0,) * len(shape))


def smem():
    return pl.BlockSpec(memory_space=pltpu.SMEM)


def attend_kernel(experts, capacity, heads, n_ctx, where_ref, q_ref, ids_ref, *refs):
    count = n_ctx // 2 + 1
    *chips, cores = refs[:count]
    refs = refs[count:]
    blocks = []
    for j, chip in enumerate(chips):
        blocks += [chip, cores.at[j]]
    out_refs, refs = refs[: experts * PARTS], refs[experts * PARTS :]
    k_scr, v_scr, best_scr, acc_scr, att_scr = refs
    ctx, owner = where_ref[0], where_ref[1]
    seq = pl.program_id(0)
    block = q_ref.shape[1]
    tile = 2 * block
    factor = math.log2(math.e) / math.sqrt(HEAD_SIZE)

    @pl.when(seq == 0)
    def _():
        v_scr[:, :, HEAD_SIZE:] = jnp.ones((n_ctx, block, HEAD_SIZE), BF16)

    for m in range(n_ctx):
        index = jnp.bitwise_xor(ctx, m)
        k_scr[index] = blocks[m][0, :, :HEAD_SIZE]
        v_scr[index, :, :HEAD_SIZE] = blocks[m][0, :, HEAD_SIZE:]

    def fold(t, last):
        key_tile = k_scr[pl.ds(2 * t, 2)].reshape(tile, HEAD_SIZE)
        value_tile = v_scr[pl.ds(2 * t, 2)].reshape(tile, 2 * HEAD_SIZE)
        for h in range(heads):
            q = q_ref[0, :, h * HEAD_SIZE : (h + 1) * HEAD_SIZE]
            s = dot(q, key_tile, ((1,), (1,)))
            if last:
                key_pos = iota((block, tile), 1) + t * tile
                query_pos = iota((block, tile), 0) + ctx * block
                s = jnp.where(key_pos <= query_pos, s, masked_score)
            best = jnp.max(s, axis=1, keepdims=True)
            if not last:
                old = best_scr[h]
                best = jnp.maximum(old, best)
            p = jnp.exp2((s - best) * factor)
            blended = dot(p.astype(BF16), value_tile)
            if last:
                acc_scr[h] = blended
            else:
                acc_scr[h] = acc_scr[h] * jnp.exp2((old - best) * factor) + blended
            best_scr[h] = best

    fold(ctx // 2, True)

    @pl.loop(0, ctx // 2)
    def _(t):
        fold(t, False)

    for h in range(heads):
        acc = acc_scr[h]
        att = acc[:, :HEAD_SIZE] / acc[:, HEAD_SIZE:]
        att_scr[:, h * HEAD_SIZE : (h + 1) * HEAD_SIZE] = att.astype(BF16)

    n = ids_ref.shape[2]
    part = capacity // PARTS
    per_seq = block // n
    position = iota((experts * capacity, n), 0)
    slots = shifted_slots(position, owner, experts, capacity)
    for b in range(per_seq):
        source = seq * per_seq + b
        target = slots_row(ids_ref[source], capacity)
        picked = dot(one_hot(slots == target), att_scr[b * n : (b + 1) * n, :]).astype(BF16)
        for d in range(experts):
            rank = jnp.bitwise_xor(jnp.bitwise_xor(owner, d), source)
            for c in range(PARTS):
                first = d * capacity + c * part
                out_refs[c * experts + d][rank] = picked[first : first + part]


def attend(where, queries, key_values, ids, capacity):
    seqs, block, width = queries.shape
    n_ctx = 2 * (len(key_values) - 1)
    experts, _, n = ids.shape
    heads = width // HEAD_SIZE
    part = capacity // PARTS
    by_seq = pl.BlockSpec((1, block, 2 * HEAD_SIZE), lambda s: (s, 0, 0))
    outs = pl.pallas_call(
        functools.partial(attend_kernel, experts, capacity, heads, n_ctx),
        grid=(seqs,),
        in_specs=[
            smem(),
            pl.BlockSpec((1, block, width), lambda s: (s, 0, 0)),
            whole(experts, 1, n),
        ]
        + [by_seq] * (len(key_values) - 1)
        + [pl.BlockSpec((n_ctx // 2, 1, block, 2 * HEAD_SIZE), lambda s: (0, s, 0, 0))],
        out_specs=[whole(experts, part, width)] * (PARTS * experts),
        scratch_shapes=[
            pltpu.VMEM((n_ctx, block, HEAD_SIZE), BF16),
            pltpu.VMEM((n_ctx, block, 2 * HEAD_SIZE), BF16),
            pltpu.VMEM((heads, block, 1), F32),
            pltpu.VMEM((heads, block, 2 * HEAD_SIZE), F32),
            pltpu.VMEM((block, width), BF16),
        ],
        out_shape=[jax.ShapeDtypeStruct((experts, part, width), BF16)] * (PARTS * experts),
        compiler_params=kernel_params(),
        cost_estimate=brief(),
        name="attend",
    )(where, queries, ids, *key_values)
    return [outs[c * experts : (c + 1) * experts] for c in range(PARTS)]


def place_kernel(experts, capacity, where_ref, ids_ref, rows_ref, *refs):
    out_refs, pick_scr = refs[:-1], refs[-1]

    @pl.when(pl.program_id(0) == 0)
    def _():
        position = iota(pick_scr.shape, 0)
        slots = shifted_slots(position, where_ref[1], experts, capacity)
        pick_scr[...] = one_hot(slots == slots_row(ids_ref[...], capacity))

    picked = dot(pick_scr[...], rows_ref[...]).astype(BF16)
    for d, ref in enumerate(out_refs):
        ref[...] = picked[d * capacity : (d + 1) * capacity]


def place(where, ids_row, rows, experts, capacity):
    n, width = rows.shape
    cols = min(width, 1024)
    return pl.pallas_call(
        functools.partial(place_kernel, experts, capacity),
        grid=(width // cols,),
        in_specs=[smem(), whole(1, n), pl.BlockSpec((n, cols), lambda i: (0, i))],
        out_specs=[pl.BlockSpec((capacity, cols), lambda i: (0, i))] * experts,
        out_shape=[jax.ShapeDtypeStruct((capacity, width), BF16)] * experts,
        scratch_shapes=[pltpu.VMEM((experts * capacity, n), BF16)],
        compiler_params=kernel_params(),
        cost_estimate=brief(),
        name="place",
    )(where, ids_row, rows)


def restore_kernel(experts, capacity, where_ref, ids_ref, *refs):
    *parts, out_ref, pick_scr = refs

    @pl.when(pl.program_id(0) == 0)
    def _():
        slots = shifted_slots(iota(pick_scr.shape, 1), where_ref[1], experts, capacity)
        pick_scr[...] = one_hot(slots == slots_column(ids_ref[...], capacity))

    rows = jnp.concatenate([ref[...] for ref in parts], axis=0)
    out_ref[...] = dot(pick_scr[...], rows).astype(BF16)


def restore(where, ids_column, parts, experts, capacity):
    n = ids_column.shape[0]
    part, width = parts[0][0].shape
    cols = min(width, 1024)
    return pl.pallas_call(
        functools.partial(restore_kernel, experts, capacity),
        grid=(width // cols,),
        in_specs=[smem(), whole(n, 1)]
        + [pl.BlockSpec((part, cols), lambda i: (0, i))] * (experts * PARTS),
        out_specs=pl.BlockSpec((n, cols), lambda i: (0, i)),
        out_shape=jax.ShapeDtypeStruct((n, width), BF16),
        scratch_shapes=[pltpu.VMEM((n, experts * capacity), BF16)],
        compiler_params=kernel_params(),
        cost_estimate=brief(),
        name="restore",
    )(where, ids_column, *[parts[c][d] for d in range(experts) for c in range(PARTS)])


def expert_kernel(experts, capacity, part_index, swap, where_ref, *refs):
    att_refs, refs = refs[:experts], refs[experts:]
    grad_refs, refs = refs[:experts], refs[experts:]
    own_ref, same_hbm, other_hbm, gate_hbm, up_hbm, down_hbm = refs[:6]
    gain_ref, ids_ref, weight_ref, refs = refs[6], refs[7], refs[8], refs[9:]
    layer_refs, refs = refs[:experts], refs[experts:]
    change_refs, refs = refs[:experts], refs[experts:]
    saved_refs, refs = refs[: 1 + swap], refs[1 + swap :]
    w_scr, gate_scr, up_scr, down_scr, hidden_scr, normed_ref, back_ref, back_in_scr, sems = refs
    part, width = grad_refs[0].shape
    rows = experts * part
    att_cols = att_refs[0].shape[-1]
    pieces, _, _, piece = w_scr.shape
    ff = gate_scr.shape[1]
    ctx, owner = where_ref[0], where_ref[1]
    core = jnp.bitwise_and(ctx, 1)
    sources = [jnp.bitwise_xor(owner, d) for d in range(experts)]
    units_at, gate_at, up_at, normed_at = 0, ff, 2 * ff, 3 * ff

    copies = []
    for q in range(pieces // 2):
        for ref in (same_hbm, other_hbm):
            m = len(copies)
            copies.append(pltpu.make_async_copy(ref.at[q], w_scr.at[m], sems.at[m]))
    weight_copies = (
        pltpu.make_async_copy(gate_hbm.at[0], gate_scr, sems.at[pieces]),
        pltpu.make_async_copy(up_hbm.at[0], up_scr, sems.at[pieces + 1]),
        pltpu.make_async_copy(down_hbm.at[0], down_scr, sems.at[pieces + 2]),
    )
    for copy in copies:
        copy.start()
    for copy in weight_copies:
        copy.start()

    n = ids_ref.shape[2]
    weights = []
    for s, source in enumerate(sources):
        target = slots_row(ids_ref[source], capacity)
        slot = iota((part, n), 0) + (owner * capacity + part_index * part)
        weights.append(
            jnp.sum(
                jnp.where(slot.astype(F32) == target, weight_ref[source], 0.0),
                axis=1,
                keepdims=True,
            )
        )
        grads = grad_refs[s][...].astype(F32)
        back_ref[s * part : (s + 1) * part, :] = (weights[s] * grads).astype(BF16)

    for m in range(pieces):
        copies[m].wait()
        index = m + core if m % 2 == 0 else m - core
        column = pl.multiple_of(index * piece, piece)
        total = jnp.zeros((rows, piece), F32)
        for d in range(experts):
            block = own_ref[:, pl.ds(column, piece)] if d == 0 else w_scr[m, d - 1]
            total += dot(att_refs[d][...].reshape(rows, att_cols), block)
        hidden_scr[:, pl.ds(column, piece)] = total.astype(BF16)

    squares = jnp.zeros((rows, 1), F32)
    for t in range(0, width, PIECE):
        hidden = hidden_scr[:, t : t + PIECE].astype(F32)
        squares += jnp.sum(hidden * hidden, axis=1, keepdims=True)
    inv = lax.rsqrt(squares / width + epsilon)
    for t in range(0, width, PIECE):
        hidden = hidden_scr[:, t : t + PIECE].astype(F32)
        normed_ref[:, t : t + PIECE] = (hidden * inv * gain_ref[:, t : t + PIECE]).astype(BF16)

    for copy in weight_copies:
        copy.wait()
    for f in range(0, ff, 256):
        gate_act = dot(normed_ref[...], gate_scr[:, f : f + 256])
        up_act = dot(normed_ref[...], up_scr[:, f : f + 256])
        back_units = dot(back_ref[...], down_scr[f : f + 256, :], ((1,), (1,)))
        sigma = 1.0 / (1.0 + jnp.exp(-gate_act))
        gated = gate_act * sigma
        units = (gated * up_act).astype(BF16)
        back_gate = back_units * up_act * sigma * (1.0 + gate_act * (1.0 - sigma))
        back_gate = back_gate.astype(BF16)
        back_up = (back_units * gated).astype(BF16)
        for ref in saved_refs:
            ref[:, units_at + f : units_at + f + 256] = units
            ref[:, gate_at + f : gate_at + f + 256] = back_gate
            ref[:, up_at + f : up_at + f + 256] = back_up

    saved = saved_refs[0]
    half = width // len(saved_refs)
    for c, ref in enumerate(saved_refs):
        for t in range(half // PIECE):
            if swap:
                column = pl.multiple_of(jnp.bitwise_xor(ctx, 2 * t + c) * PIECE, PIECE)
            else:
                column = t * PIECE
            at = normed_at + t * PIECE
            ref[:, at : at + PIECE] = normed_ref[:, pl.ds(column, PIECE)]
            ref[:, at + half : at + half + PIECE] = back_ref[:, pl.ds(column, PIECE)]

    weight = jnp.concatenate(weights, axis=0)
    moment = jnp.zeros((rows, 1), F32)
    for t in range(0, width, PIECE):
        hidden = hidden_scr[:, t : t + PIECE].astype(F32)
        result = dot(saved[:, units_at:gate_at], down_scr[:, t : t + PIECE])
        layer = (hidden + weight * result.astype(BF16).astype(F32)).astype(BF16)
        for s in range(experts):
            layer_refs[s][:, t : t + PIECE] = layer[s * part : (s + 1) * part]
        back_in = dot(saved[:, gate_at:up_at], gate_scr[t : t + PIECE, :], ((1,), (1,)))
        back_in += dot(saved[:, up_at:normed_at], up_scr[t : t + PIECE, :], ((1,), (1,)))
        back_in = back_in.astype(BF16)
        back_in_scr[:, t : t + PIECE] = back_in
        scaled = back_in.astype(F32) * gain_ref[:, t : t + PIECE]
        moment += jnp.sum(scaled * (hidden * inv), axis=1, keepdims=True)
    moment = moment / width
    for t in range(0, width, PIECE):
        unit = hidden_scr[:, t : t + PIECE].astype(F32) * inv
        scaled = back_in_scr[:, t : t + PIECE].astype(F32) * gain_ref[:, t : t + PIECE]
        change = inv * (scaled - unit * moment)
        for s in range(experts):
            grads = grad_refs[s][:, t : t + PIECE].astype(F32)
            change_refs[s][:, t : t + PIECE] = (
                grads + change[s * part : (s + 1) * part]
            ).astype(BF16)


def expert_part(
    where, att, grads, own, same, other, gate, up, down, gain, ids, weights, capacity, index, swap
):
    experts, part, att_cols = att[0].shape
    pieces = 2 * same.shape[0]
    piece = same.shape[-1]
    width = grads[0].shape[1]
    ff = gate.shape[2]
    rows = experts * part
    n = ids.shape[2]
    half = width // 2 if swap else width
    out = lambda *shape: jax.ShapeDtypeStruct(shape, BF16)
    in_hbm = pl.BlockSpec(memory_space=pl.ANY)
    outs = pl.pallas_call(
        functools.partial(expert_kernel, experts, capacity, index, swap),
        grid=(1,),
        in_specs=[smem()]
        + [whole(*x.shape) for x in att]
        + [pl.BlockSpec((part, width), lambda i: (index, 0))] * experts
        + [whole(*own.shape)]
        + [in_hbm] * 5
        + [whole(1, width), whole(experts, 1, n), whole(experts, 1, n)],
        out_specs=[whole(part, width)] * (2 * experts)
        + [whole(rows, 3 * ff + 2 * half)] * (1 + swap),
        scratch_shapes=[
            pltpu.VMEM((pieces, experts - 1, att_cols, piece), BF16),
            pltpu.VMEM((width, ff), BF16),
            pltpu.VMEM((width, ff), BF16),
            pltpu.VMEM((ff, width), BF16),
            pltpu.VMEM((rows, width), BF16),
            pltpu.VMEM((rows, width), BF16),
            pltpu.VMEM((rows, width), BF16),
            pltpu.VMEM((rows, width), BF16),
            pltpu.SemaphoreType.DMA((pieces + 3,)),
        ],
        out_shape=[out(part, width)] * (2 * experts)
        + [out(rows, 3 * ff + 2 * half)] * (1 + swap),
        compiler_params=kernel_params(),
        cost_estimate=brief(),
        name="expert",
    )(where, *att, *grads, own, same, other, gate, up, down, gain, ids, weights)
    return outs[:experts], outs[experts : 2 * experts], outs[2 * experts :]


def weight_kernel(count, *refs):
    units, back_gate, back_up, normed, back = [refs[i * count : (i + 1) * count] for i in range(5)]
    outs = refs[5 * count :]
    first = ((0,), (0,))

    def total(left, right):
        return sum(dot(a[...], b[...], first) for a, b in zip(left, right)).astype(BF16)

    gate, up, down = total(normed, back_gate), total(normed, back_up), total(units, back)
    cols = down.shape[1]
    part = gate.shape[0] // len(outs)
    for c, ref in enumerate(outs):
        rows = slice(c * part, (c + 1) * part)
        ref[0, 0] = gate[rows]
        ref[0, 1] = up[rows]
        for t in range(0, down.shape[0], cols):
            ref[0, 2, :, t : t + cols] = down[t + c * part : t + (c + 1) * part]


def weight_blocks(saved, blocks, ff, split):
    count = len(saved)
    rows, total = saved[0].shape
    normed_at = 3 * ff // PIECE
    back_at = normed_at + blocks
    thin = lambda at: [pl.BlockSpec((rows, PIECE), lambda i: (0, at + i))] * count
    full = lambda at: [pl.BlockSpec((rows, ff), lambda i: (0, at))] * count
    part = PIECE // 2 if split else PIECE
    shuffled = lambda i: (i % 2 * (blocks // 2) + i // 2, 0, 0, 0)
    plain = lambda i: (i, 0, 0, 0)
    orders = [shuffled, plain] if split else [plain]
    return pl.pallas_call(
        functools.partial(weight_kernel, count),
        grid=(blocks,),
        in_specs=full(0) + full(1) + full(2) + thin(normed_at) + thin(back_at),
        out_specs=[pl.BlockSpec((1, 3, part, ff), order) for order in orders],
        out_shape=[jax.ShapeDtypeStruct((blocks, 3, part, ff), BF16) for _ in orders],
        compiler_params=kernel_params(),
        cost_estimate=brief(),
        name="weight_grads",
    )(*saved * 5)


def partner(value, mask):
    count = lax.axis_size("ctx")
    return lax.ppermute(value, "ctx", [(i, i ^ mask) for i in range(count)])


def to_owner(value, mask):
    count = lax.axis_size("exp")
    return lax.ppermute(value, "exp", [(i, i ^ mask) for i in range(count)])


def to_owners(values):
    return [values[0]] + [to_owner(values[d], d) for d in range(len(values) - 1, 0, -1)][::-1]


def chip_groups(count):
    return [
        list(range(first + core, first + count, 2))
        for first in range(0, lax.axis_size("ctx"), count)
        for core in range(2)
    ]


def after(value, *others):
    return lax.optimization_barrier((value, others))[0]


def halved(value, bits, order, ctx):
    shape = value.shape[1:]
    held = value.reshape((2,) * bits + shape)
    for place_in_order, bit in enumerate(order):
        axis = bits - 1 - bit
        mine = (ctx >> bit) & 1
        gone = lax.dynamic_slice_in_dim(held, 1 - mine, 1, axis)
        kept = lax.dynamic_slice_in_dim(held, mine, 1, axis)
        held = kept.astype(F32) + partner(gone, 1 << bit).astype(F32)
        if place_in_order < bits - 1:
            held = held.astype(BF16)
    return held.reshape(shape)


def on_device(
    queries,
    rotated_key_heads,
    value_head_rows,
    out_proj,
    norm_gain,
    expert_ids,
    gate_weights,
    expert_gate,
    expert_up,
    expert_down,
    grad_out,
):
    heads_dev = queries.shape[2] // HEAD_SIZE
    group = LOCAL_QUERY_HEADS // LOCAL_KEY_HEADS
    exp_count = lax.axis_size("exp")
    ctx_count = lax.axis_size("ctx")
    owner = lax.axis_index("exp")
    ctx = lax.axis_index("ctx")
    bits = ctx_count.bit_length() - 1
    n, _ = expert_ids.shape
    width = grad_out.shape[1]
    experts = exp_count
    capacity = min(n, 2 * n // experts)
    pieces = min(ctx_count, width // PIECE)
    piece = width // pieces
    piece_index = ctx % pieces
    where = jnp.stack([ctx, owner, piece_index]).astype(jnp.int32)

    ids_f = expert_ids.astype(F32)
    info = jnp.stack([ids_f[:, 0], gate_weights[:, 0]])
    info = jnp.broadcast_to(info[None], (exp_count,) + info.shape)
    info = lax.all_to_all(info, "exp", 0, 0, tiled=True)
    ids_all, weights_all = info[:, 0:1, :], info[:, 1:2, :]

    mine = lax.dynamic_slice_in_dim(out_proj, piece_index * piece, piece, 1)
    projection = to_owners([mine] * exp_count)[1:]

    first_column = (owner * heads_dev // group) * HEAD_SIZE
    keys = lax.dynamic_slice_in_dim(rotated_key_heads, first_column, HEAD_SIZE, 2)
    values = lax.dynamic_slice_in_dim(value_head_rows, first_column, HEAD_SIZE, 2)
    own = jnp.concatenate([keys, values], axis=2)
    chips = [own] + [partner(own, m) for m in range(2, ctx_count, 2)]

    grads = place(where, ids_f.reshape(1, n), grad_out, experts, capacity)
    grads = to_owners(grads)

    key_values = chips + [partner(after(jnp.stack(chips), grads[1]), 1)]

    projection = after(jnp.stack(projection), chips)
    projection = jnp.broadcast_to(projection[None], (pieces // 2,) + projection.shape)
    same = lax.all_to_all(
        projection, "ctx", 0, 0, axis_index_groups=chip_groups(pieces), tiled=True
    )

    sent = attend(where, queries, key_values, ids_all, capacity)
    arrived = to_owners(after(sent[0], grads))
    later = after(sent[1], arrived[1], same)
    same = after(same, sent[0], grads[2:])
    other = partner(same, 1)

    rows_dev = width // ctx_count
    ff = expert_gate.shape[2]
    swap = rows_dev == PIECE

    def run(index, arrived):
        return expert_part(
            where,
            arrived,
            grads,
            out_proj,
            same,
            other,
            expert_gate,
            expert_up,
            expert_down,
            norm_gain.reshape(1, width),
            ids_all,
            weights_all,
            capacity,
            index,
            swap,
        )

    layer_a, change_a, saved_a = run(0, arrived)
    layer_a = to_owners(layer_a)
    layer_b, change_b, saved_b = run(1, to_owners(later))
    if swap:
        saved = [saved_a[0], partner(saved_a[1], 1)]
        saved += [saved_b[0], partner(after(saved_b[1], layer_a), 1)]
        change_a = to_owners(after(change_a, layer_a[1]))
        parts = weight_blocks(saved, ctx_count // 2, ff, True)
        parts = after(parts, change_a)
        half = ctx_count // 4
        masks = (2, 4), (4, 2)
        near = [partner(x[half:], m[0]) for x, m in zip(parts, masks)]
        layer_b = to_owners(after(layer_b, change_a[1]))
        near = after(near, layer_b[1])
        sums = [x[:half].astype(F32) + y.astype(F32) for x, y in zip(parts, near)]
        gone = [x[1].astype(BF16) for x in sums]
        change_b = after(change_b, gone)
        far = [partner(x, m[1]) for x, m in zip(gone, masks)]
        total = [x[0] + y.astype(F32) for x, y in zip(sums, far)]
        total = jnp.concatenate(total, axis=1)
        grad_gate, grad_up = total[0][None], total[1][None]
        grad_down = total[2].reshape(PIECE, ff // PIECE, PIECE).transpose(1, 0, 2)
        grad_down = grad_down.reshape(1, ff, PIECE)
    else:
        change_a = to_owners(after(change_a, layer_a[1]))
        layer_b = to_owners(after(layer_b, change_a[1]))
        blocks = width // PIECE
        (parts,) = weight_blocks(list(saved_a) + list(saved_b), blocks, ff, False)
        part_down = parts[:, 2].reshape(blocks, PIECE, ff // PIECE, PIECE).transpose(0, 2, 1, 3)
        part_down = part_down.reshape(blocks, ff, PIECE // rows_dev, rows_dev)
        part_down = part_down.transpose(0, 2, 1, 3).reshape(ctx_count, ff, rows_dev)
        order = list(range(bits))
        grad_gate, grad_up, grad_down = [
            halved(x.reshape((ctx_count,) + shape), bits, order, ctx)[None]
            for x, shape in (
                (parts[:, 0], (rows_dev, ff)),
                (parts[:, 1], (rows_dev, ff)),
                (part_down, (ff, rows_dev)),
            )
        ]
    change_b = to_owners(after(change_b, layer_b[1:2]))
    layer_out = restore(where, ids_f, [layer_a, layer_b], experts, capacity)
    change_b = after(change_b, layer_out, grad_gate, grad_up, grad_down)
    grad_hidden = restore(where, ids_f, [change_a, change_b], experts, capacity)
    return (layer_out, grad_hidden, grad_gate, grad_up, grad_down)


def solution(mesh):
    in_specs = (
        P(None, "ctx", "exp"),
        P(None, "ctx", None),
        P(None, "ctx", None),
        P("exp", None),
        P(),
        P(("ctx", "exp"), None),
        P(("ctx", "exp"), None),
        P("exp", None, None),
        P("exp", None, None),
        P("exp", None, None),
        P(("ctx", "exp"), None),
    )
    out_specs = (
        P(("ctx", "exp"), None),
        P(("ctx", "exp"), None),
        P("exp", "ctx", None),
        P("exp", "ctx", None),
        P("exp", None, "ctx"),
    )
    return jax.shard_map(
        on_device, mesh=mesh, in_specs=in_specs, out_specs=out_specs, check_vma=False
    )
```

```python
import functools
import math

import jax
import jax.numpy as jnp
from jax import lax
from jax.experimental import pallas as pl
from jax.experimental.pallas import tpu as pltpu
from jax.sharding import PartitionSpec as P

LOCAL_QUERY_HEADS = 16
LOCAL_KEY_HEADS = 2
HEAD_SIZE = 128
PIECE = 256
PARTS = 2

epsilon = 1e-06
masked_score = -1e30
F32 = jnp.float32
BF16 = jnp.bfloat16
VMEM_LIMIT = 60 << 20


def dot(a, b, contract=((1,), (0,))):
    return lax.dot_general(a, b, (contract, ((), ())), preferred_element_type=F32)


def iota(shape, dim):
    return lax.broadcasted_iota(jnp.int32, shape, dim)


def slots_row(ids_row, capacity):
    n = ids_row.shape[1]
    names = iota((16, n), 0).astype(F32)
    chosen = names == ids_row
    before = (iota((n, n), 0) < iota((n, n), 1)).astype(F32).astype(BF16)
    earlier = dot(jnp.where(chosen, 1.0, 0.0).astype(BF16), before)
    return jnp.sum(jnp.where(chosen, earlier + names * capacity, 0.0), axis=0, keepdims=True)


def slots_column(ids_column, capacity):
    n = ids_column.shape[0]
    names = iota((n, 128), 1).astype(F32)
    chosen = names == ids_column
    before = (iota((n, n), 1) < iota((n, n), 0)).astype(F32).astype(BF16)
    earlier = dot(before, jnp.where(chosen, 1.0, 0.0).astype(BF16))
    return jnp.sum(jnp.where(chosen, earlier + names * capacity, 0.0), axis=1, keepdims=True)


def one_hot(matches):
    return jnp.where(matches, 1.0, 0.0).astype(BF16)


def shifted_slots(position, owner, experts, capacity):
    expert = jnp.bitwise_xor(position // capacity, owner)
    return (expert * capacity + lax.rem(position, capacity)).astype(F32)


def kernel_params():
    return pltpu.CompilerParams(vmem_limit_bytes=VMEM_LIMIT)


def brief():
    return pl.CostEstimate(flops=1000, bytes_accessed=1000, transcendentals=0)


def whole(*shape):
    return pl.BlockSpec(shape, lambda *_: (0,) * len(shape))


def smem():
    return pl.BlockSpec(memory_space=pltpu.SMEM)


def attend_kernel(experts, capacity, heads, n_ctx, where_ref, q_ref, ids_ref, *refs):
    count = n_ctx // 2 + 1
    *chips, cores = refs[:count]
    refs = refs[count:]
    blocks = []
    for j, chip in enumerate(chips):
        blocks += [chip, cores.at[j]]
    out_refs, refs = refs[: experts * PARTS], refs[experts * PARTS :]
    k_scr, v_scr, best_scr, acc_scr, att_scr = refs
    ctx, owner = where_ref[0], where_ref[1]
    seq = pl.program_id(0)
    block = q_ref.shape[1]
    tile = 2 * block
    factor = math.log2(math.e) / math.sqrt(HEAD_SIZE)

    @pl.when(seq == 0)
    def _():
        v_scr[:, :, HEAD_SIZE:] = jnp.ones((n_ctx, block, HEAD_SIZE), BF16)

    for m in range(n_ctx):
        index = jnp.bitwise_xor(ctx, m)
        k_scr[index] = blocks[m][0, :, :HEAD_SIZE]
        v_scr[index, :, :HEAD_SIZE] = blocks[m][0, :, HEAD_SIZE:]

    def fold(t, last):
        key_tile = k_scr[pl.ds(2 * t, 2)].reshape(tile, HEAD_SIZE)
        value_tile = v_scr[pl.ds(2 * t, 2)].reshape(tile, 2 * HEAD_SIZE)
        for h in range(heads):
            q = q_ref[0, :, h * HEAD_SIZE : (h + 1) * HEAD_SIZE]
            s = dot(q, key_tile, ((1,), (1,)))
            if last:
                key_pos = iota((block, tile), 1) + t * tile
                query_pos = iota((block, tile), 0) + ctx * block
                s = jnp.where(key_pos <= query_pos, s, masked_score)
            best = jnp.max(s, axis=1, keepdims=True)
            if not last:
                old = best_scr[h]
                best = jnp.maximum(old, best)
            p = jnp.exp2((s - best) * factor)
            blended = dot(p.astype(BF16), value_tile)
            if last:
                acc_scr[h] = blended
            else:
                acc_scr[h] = acc_scr[h] * jnp.exp2((old - best) * factor) + blended
            best_scr[h] = best

    fold(ctx // 2, True)

    @pl.loop(0, ctx // 2)
    def _(t):
        fold(t, False)

    for h in range(heads):
        acc = acc_scr[h]
        att = acc[:, :HEAD_SIZE] / acc[:, HEAD_SIZE:]
        att_scr[:, h * HEAD_SIZE : (h + 1) * HEAD_SIZE] = att.astype(BF16)

    n = ids_ref.shape[2]
    part = capacity // PARTS
    per_seq = block // n
    position = iota((experts * capacity, n), 0)
    slots = shifted_slots(position, owner, experts, capacity)
    for b in range(per_seq):
        source = seq * per_seq + b
        target = slots_row(ids_ref[source], capacity)
        picked = dot(one_hot(slots == target), att_scr[b * n : (b + 1) * n, :]).astype(BF16)
        for d in range(experts):
            rank = jnp.bitwise_xor(jnp.bitwise_xor(owner, d), source)
            for c in range(PARTS):
                first = d * capacity + c * part
                out_refs[c * experts + d][rank] = picked[first : first + part]


def attend(where, queries, key_values, ids, capacity):
    seqs, block, width = queries.shape
    n_ctx = 2 * (len(key_values) - 1)
    experts, _, n = ids.shape
    heads = width // HEAD_SIZE
    part = capacity // PARTS
    by_seq = pl.BlockSpec((1, block, 2 * HEAD_SIZE), lambda s: (s, 0, 0))
    outs = pl.pallas_call(
        functools.partial(attend_kernel, experts, capacity, heads, n_ctx),
        grid=(seqs,),
        in_specs=[
            smem(),
            pl.BlockSpec((1, block, width), lambda s: (s, 0, 0)),
            whole(experts, 1, n),
        ]
        + [by_seq] * (len(key_values) - 1)
        + [pl.BlockSpec((n_ctx // 2, 1, block, 2 * HEAD_SIZE), lambda s: (0, s, 0, 0))],
        out_specs=[whole(experts, part, width)] * (PARTS * experts),
        scratch_shapes=[
            pltpu.VMEM((n_ctx, block, HEAD_SIZE), BF16),
            pltpu.VMEM((n_ctx, block, 2 * HEAD_SIZE), BF16),
            pltpu.VMEM((heads, block, 1), F32),
            pltpu.VMEM((heads, block, 2 * HEAD_SIZE), F32),
            pltpu.VMEM((block, width), BF16),
        ],
        out_shape=[jax.ShapeDtypeStruct((experts, part, width), BF16)] * (PARTS * experts),
        compiler_params=kernel_params(),
        cost_estimate=brief(),
        name="attend",
    )(where, queries, ids, *key_values)
    return [outs[c * experts : (c + 1) * experts] for c in range(PARTS)]


def place_kernel(experts, capacity, where_ref, ids_ref, rows_ref, *refs):
    out_refs, pick_scr = refs[:-1], refs[-1]

    @pl.when(pl.program_id(0) == 0)
    def _():
        position = iota(pick_scr.shape, 0)
        slots = shifted_slots(position, where_ref[1], experts, capacity)
        pick_scr[...] = one_hot(slots == slots_row(ids_ref[...], capacity))

    picked = dot(pick_scr[...], rows_ref[...]).astype(BF16)
    for d, ref in enumerate(out_refs):
        ref[...] = picked[d * capacity : (d + 1) * capacity]


def place(where, ids_row, rows, experts, capacity):
    n, width = rows.shape
    cols = min(width, 1024)
    return pl.pallas_call(
        functools.partial(place_kernel, experts, capacity),
        grid=(width // cols,),
        in_specs=[smem(), whole(1, n), pl.BlockSpec((n, cols), lambda i: (0, i))],
        out_specs=[pl.BlockSpec((capacity, cols), lambda i: (0, i))] * experts,
        out_shape=[jax.ShapeDtypeStruct((capacity, width), BF16)] * experts,
        scratch_shapes=[pltpu.VMEM((experts * capacity, n), BF16)],
        compiler_params=kernel_params(),
        cost_estimate=brief(),
        name="place",
    )(where, ids_row, rows)


def restore_kernel(experts, capacity, tiles, where_ref, ids_ref, *refs):
    *parts, layer_ref, grad_ref, pick_scr = refs
    step = pl.program_id(0)

    @pl.when(step == 0)
    def _():
        slots = shifted_slots(iota(pick_scr.shape, 1), where_ref[1], experts, capacity)
        pick_scr[...] = one_hot(slots == slots_column(ids_ref[...], capacity))

    def rows(early, late):
        both = [ref[...] for pair in zip(early, late) for ref in pair]
        return dot(pick_scr[...], jnp.concatenate(both, axis=0)).astype(BF16)

    layer_a, change_a, now = [parts[i * experts : (i + 1) * experts] for i in range(3)]

    @pl.when(step < tiles)
    def _():
        layer_ref[...] = rows(layer_a, now)

    @pl.when(step >= tiles)
    def _():
        grad_ref[...] = rows(change_a, now)


def restore(where, ids_column, layer_a, change_a, packed, experts, capacity):
    n = ids_column.shape[0]
    part, width = layer_a[0].shape
    cols = min(width, 1024)
    tiles = width // cols
    first = lambda i: (0, jnp.minimum(i, tiles - 1))
    second = lambda i: (0, jnp.maximum(i - tiles, 0))
    block = lambda at: [pl.BlockSpec((part, cols), at)] * experts
    return pl.pallas_call(
        functools.partial(restore_kernel, experts, capacity, tiles),
        grid=(2 * tiles,),
        in_specs=[smem(), whole(n, 1)] + block(first) + block(second) + block(lambda i: (0, i)),
        out_specs=[pl.BlockSpec((n, cols), first), pl.BlockSpec((n, cols), second)],
        out_shape=[jax.ShapeDtypeStruct((n, width), BF16)] * 2,
        scratch_shapes=[pltpu.VMEM((n, experts * capacity), BF16)],
        compiler_params=kernel_params(),
        cost_estimate=brief(),
        name="restore",
    )(where, ids_column, *layer_a, *change_a, *packed)


def expert_kernel(experts, capacity, part_index, swap, where_ref, *refs):
    att_refs, refs = refs[:experts], refs[experts:]
    grad_refs, refs = refs[:experts], refs[experts:]
    width_of = grad_refs[0].shape[1]
    own_ref, same_hbm, other_hbm, gate_hbm, up_hbm, down_hbm = refs[:6]
    gain_ref, ids_ref, weight_ref, refs = refs[6], refs[7], refs[8], refs[9:]
    if part_index == 0:
        layer_refs, refs = refs[:experts], refs[experts:]
        change_refs, refs = refs[:experts], refs[experts:]
    else:
        packed_refs, refs = refs[:experts], refs[experts:]
        layer_refs = [ref.at[:, :width_of] for ref in packed_refs]
        change_refs = [ref.at[:, width_of:] for ref in packed_refs]
    saved_refs, refs = refs[: 1 + swap], refs[1 + swap :]
    w_scr, gate_scr, up_scr, down_scr, hidden_scr, normed_ref, back_ref, back_in_scr, sems = refs
    part, width = grad_refs[0].shape
    rows = experts * part
    att_cols = att_refs[0].shape[-1]
    pieces, _, _, piece = w_scr.shape
    ff = gate_scr.shape[1]
    ctx, owner = where_ref[0], where_ref[1]
    core = jnp.bitwise_and(ctx, 1)
    sources = [jnp.bitwise_xor(owner, d) for d in range(experts)]
    units_at, gate_at, up_at, normed_at = 0, ff, 2 * ff, 3 * ff

    copies = []
    for q in range(pieces // 2):
        for ref in (same_hbm, other_hbm):
            m = len(copies)
            copies.append(pltpu.make_async_copy(ref.at[q], w_scr.at[m], sems.at[m]))
    weight_copies = (
        pltpu.make_async_copy(gate_hbm.at[0], gate_scr, sems.at[pieces]),
        pltpu.make_async_copy(up_hbm.at[0], up_scr, sems.at[pieces + 1]),
        pltpu.make_async_copy(down_hbm.at[0], down_scr, sems.at[pieces + 2]),
    )
    for copy in copies:
        copy.start()
    for copy in weight_copies:
        copy.start()

    n = ids_ref.shape[2]
    weights = []
    for s, source in enumerate(sources):
        target = slots_row(ids_ref[source], capacity)
        slot = iota((part, n), 0) + (owner * capacity + part_index * part)
        weights.append(
            jnp.sum(
                jnp.where(slot.astype(F32) == target, weight_ref[source], 0.0),
                axis=1,
                keepdims=True,
            )
        )
        grads = grad_refs[s][...].astype(F32)
        back_ref[s * part : (s + 1) * part, :] = (weights[s] * grads).astype(BF16)

    for m in range(pieces):
        copies[m].wait()
        index = m + core if m % 2 == 0 else m - core
        column = pl.multiple_of(index * piece, piece)
        total = jnp.zeros((rows, piece), F32)
        for d in range(experts):
            block = own_ref[:, pl.ds(column, piece)] if d == 0 else w_scr[m, d - 1]
            total += dot(att_refs[d][...].reshape(rows, att_cols), block)
        hidden_scr[:, pl.ds(column, piece)] = total.astype(BF16)

    squares = jnp.zeros((rows, 1), F32)
    for t in range(0, width, PIECE):
        hidden = hidden_scr[:, t : t + PIECE].astype(F32)
        squares += jnp.sum(hidden * hidden, axis=1, keepdims=True)
    inv = lax.rsqrt(squares / width + epsilon)
    for t in range(0, width, PIECE):
        hidden = hidden_scr[:, t : t + PIECE].astype(F32)
        normed_ref[:, t : t + PIECE] = (hidden * inv * gain_ref[:, t : t + PIECE]).astype(BF16)

    for copy in weight_copies:
        copy.wait()
    for f in range(0, ff, 256):
        gate_act = dot(normed_ref[...], gate_scr[:, f : f + 256])
        up_act = dot(normed_ref[...], up_scr[:, f : f + 256])
        back_units = dot(back_ref[...], down_scr[f : f + 256, :], ((1,), (1,)))
        sigma = 1.0 / (1.0 + jnp.exp(-gate_act))
        gated = gate_act * sigma
        units = (gated * up_act).astype(BF16)
        back_gate = back_units * up_act * sigma * (1.0 + gate_act * (1.0 - sigma))
        back_gate = back_gate.astype(BF16)
        back_up = (back_units * gated).astype(BF16)
        for ref in saved_refs:
            ref[:, units_at + f : units_at + f + 256] = units
            ref[:, gate_at + f : gate_at + f + 256] = back_gate
            ref[:, up_at + f : up_at + f + 256] = back_up

    saved = saved_refs[0]
    half = width // len(saved_refs)
    for c, ref in enumerate(saved_refs):
        for t in range(half // PIECE):
            if swap:
                column = pl.multiple_of(jnp.bitwise_xor(ctx, 2 * t + c) * PIECE, PIECE)
            else:
                column = t * PIECE
            at = normed_at + t * PIECE
            ref[:, at : at + PIECE] = normed_ref[:, pl.ds(column, PIECE)]
            ref[:, at + half : at + half + PIECE] = back_ref[:, pl.ds(column, PIECE)]

    weight = jnp.concatenate(weights, axis=0)
    moment = jnp.zeros((rows, 1), F32)
    for t in range(0, width, PIECE):
        hidden = hidden_scr[:, t : t + PIECE].astype(F32)
        result = dot(saved[:, units_at:gate_at], down_scr[:, t : t + PIECE])
        layer = (hidden + weight * result.astype(BF16).astype(F32)).astype(BF16)
        for s in range(experts):
            layer_refs[s][:, t : t + PIECE] = layer[s * part : (s + 1) * part]
        back_in = dot(saved[:, gate_at:up_at], gate_scr[t : t + PIECE, :], ((1,), (1,)))
        back_in += dot(saved[:, up_at:normed_at], up_scr[t : t + PIECE, :], ((1,), (1,)))
        back_in = back_in.astype(BF16)
        back_in_scr[:, t : t + PIECE] = back_in
        scaled = back_in.astype(F32) * gain_ref[:, t : t + PIECE]
        moment += jnp.sum(scaled * (hidden * inv), axis=1, keepdims=True)
    moment = moment / width
    for t in range(0, width, PIECE):
        unit = hidden_scr[:, t : t + PIECE].astype(F32) * inv
        scaled = back_in_scr[:, t : t + PIECE].astype(F32) * gain_ref[:, t : t + PIECE]
        change = inv * (scaled - unit * moment)
        for s in range(experts):
            grads = grad_refs[s][:, t : t + PIECE].astype(F32)
            change_refs[s][:, t : t + PIECE] = (
                grads + change[s * part : (s + 1) * part]
            ).astype(BF16)


def expert_part(
    where, att, grads, own, same, other, gate, up, down, gain, ids, weights, capacity, swap, index
):
    experts, part, att_cols = att[0].shape
    pieces = 2 * same.shape[0]
    piece = same.shape[-1]
    width = grads[0].shape[1]
    ff = gate.shape[2]
    rows = experts * part
    n = ids.shape[2]
    half = width // 2 if swap else width
    out = lambda *shape: jax.ShapeDtypeStruct(shape, BF16)
    rows_out = [out(part, width)] * (2 * experts) if index == 0 else [out(part, 2 * width)] * experts
    in_hbm = pl.BlockSpec(memory_space=pl.ANY)
    outs = pl.pallas_call(
        functools.partial(expert_kernel, experts, capacity, index, swap),
        grid=(1,),
        in_specs=[smem()]
        + [whole(*x.shape) for x in att]
        + [pl.BlockSpec((part, width), lambda i: (index, 0))] * experts
        + [whole(*own.shape)]
        + [in_hbm] * 5
        + [whole(1, width), whole(experts, 1, n), whole(experts, 1, n)],
        out_specs=[whole(*x.shape) for x in rows_out]
        + [whole(rows, 3 * ff + 2 * half)] * (1 + swap),
        scratch_shapes=[
            pltpu.VMEM((pieces, experts - 1, att_cols, piece), BF16),
            pltpu.VMEM((width, ff), BF16),
            pltpu.VMEM((width, ff), BF16),
            pltpu.VMEM((ff, width), BF16),
            pltpu.VMEM((rows, width), BF16),
            pltpu.VMEM((rows, width), BF16),
            pltpu.VMEM((rows, width), BF16),
            pltpu.VMEM((rows, width), BF16),
            pltpu.SemaphoreType.DMA((pieces + 3,)),
        ],
        out_shape=rows_out
        + [out(rows, 3 * ff + 2 * half)] * (1 + swap),
        compiler_params=kernel_params(),
        cost_estimate=brief(),
        name="expert",
    )(where, *att, *grads, own, same, other, gate, up, down, gain, ids, weights)
    return outs[: len(rows_out)], outs[len(rows_out) :]


def weight_kernel(count, *refs):
    units, back_gate, back_up, normed, back = [refs[i * count : (i + 1) * count] for i in range(5)]
    outs = refs[5 * count :]
    first = ((0,), (0,))

    def total(left, right):
        return sum(dot(a[...], b[...], first) for a, b in zip(left, right)).astype(BF16)

    gate, up, down = total(normed, back_gate), total(normed, back_up), total(units, back)
    cols = down.shape[1]
    part = gate.shape[0] // len(outs)
    for c, ref in enumerate(outs):
        rows = slice(c * part, (c + 1) * part)
        ref[0, 0] = gate[rows]
        ref[0, 1] = up[rows]
        for t in range(0, down.shape[0], cols):
            ref[0, 2, :, t : t + cols] = down[t + c * part : t + (c + 1) * part]


def weight_blocks(saved, blocks, ff, split):
    count = len(saved)
    rows, total = saved[0].shape
    normed_at = 3 * ff // PIECE
    back_at = normed_at + blocks
    thin = lambda at: [pl.BlockSpec((rows, PIECE), lambda i: (0, at + i))] * count
    full = lambda at: [pl.BlockSpec((rows, ff), lambda i: (0, at))] * count
    part = PIECE // 2 if split else PIECE
    shuffled = lambda i: (i % 2 * (blocks // 2) + i // 2, 0, 0, 0)
    plain = lambda i: (i, 0, 0, 0)
    orders = [shuffled, plain] if split else [plain]
    return pl.pallas_call(
        functools.partial(weight_kernel, count),
        grid=(blocks,),
        in_specs=full(0) + full(1) + full(2) + thin(normed_at) + thin(back_at),
        out_specs=[pl.BlockSpec((1, 3, part, ff), order) for order in orders],
        out_shape=[jax.ShapeDtypeStruct((blocks, 3, part, ff), BF16) for _ in orders],
        compiler_params=kernel_params(),
        cost_estimate=brief(),
        name="weight_grads",
    )(*saved * 5)


def partner(value, mask):
    count = lax.axis_size("ctx")
    return lax.ppermute(value, "ctx", [(i, i ^ mask) for i in range(count)])


def to_owner(value, mask):
    count = lax.axis_size("exp")
    return lax.ppermute(value, "exp", [(i, i ^ mask) for i in range(count)])


def to_owners(values):
    return [values[0]] + [to_owner(values[d], d) for d in range(len(values) - 1, 0, -1)][::-1]


def chip_groups(count):
    return [
        list(range(first + core, first + count, 2))
        for first in range(0, lax.axis_size("ctx"), count)
        for core in range(2)
    ]


def after(value, *others):
    return lax.optimization_barrier((value, others))[0]


def halved(value, bits, order, ctx):
    shape = value.shape[1:]
    held = value.reshape((2,) * bits + shape)
    for place_in_order, bit in enumerate(order):
        axis = bits - 1 - bit
        mine = (ctx >> bit) & 1
        gone = lax.dynamic_slice_in_dim(held, 1 - mine, 1, axis)
        kept = lax.dynamic_slice_in_dim(held, mine, 1, axis)
        held = kept.astype(F32) + partner(gone, 1 << bit).astype(F32)
        if place_in_order < bits - 1:
            held = held.astype(BF16)
    return held.reshape(shape)


def on_device(
    queries,
    rotated_key_heads,
    value_head_rows,
    out_proj,
    norm_gain,
    expert_ids,
    gate_weights,
    expert_gate,
    expert_up,
    expert_down,
    grad_out,
):
    heads_dev = queries.shape[2] // HEAD_SIZE
    group = LOCAL_QUERY_HEADS // LOCAL_KEY_HEADS
    exp_count = lax.axis_size("exp")
    ctx_count = lax.axis_size("ctx")
    owner = lax.axis_index("exp")
    ctx = lax.axis_index("ctx")
    bits = ctx_count.bit_length() - 1
    n, _ = expert_ids.shape
    width = grad_out.shape[1]
    experts = exp_count
    capacity = min(n, 2 * n // experts)
    pieces = min(ctx_count, width // PIECE)
    piece = width // pieces
    piece_index = ctx % pieces
    where = jnp.stack([ctx, owner, piece_index]).astype(jnp.int32)

    ids_f = expert_ids.astype(F32)
    info = jnp.stack([ids_f[:, 0], gate_weights[:, 0]])
    info = jnp.broadcast_to(info[None], (exp_count,) + info.shape)
    info = lax.all_to_all(info, "exp", 0, 0, tiled=True)
    ids_all, weights_all = info[:, 0:1, :], info[:, 1:2, :]

    mine = lax.dynamic_slice_in_dim(out_proj, piece_index * piece, piece, 1)
    projection = to_owners([mine] * exp_count)[1:]

    first_column = (owner * heads_dev // group) * HEAD_SIZE
    keys = lax.dynamic_slice_in_dim(rotated_key_heads, first_column, HEAD_SIZE, 2)
    values = lax.dynamic_slice_in_dim(value_head_rows, first_column, HEAD_SIZE, 2)
    own = jnp.concatenate([keys, values], axis=2)
    chips = [own] + [partner(own, m) for m in range(2, ctx_count, 2)]
    key_values = chips + [partner(jnp.stack(chips), 1)]

    grads = place(where, ids_f.reshape(1, n), grad_out, experts, capacity)
    grads = to_owners(after(grads, projection))

    projection = after(jnp.stack(projection), chips)
    projection = jnp.broadcast_to(projection[None], (pieces // 2,) + projection.shape)
    same = lax.all_to_all(
        projection, "ctx", 0, 0, axis_index_groups=chip_groups(pieces), tiled=True
    )

    sent = attend(where, queries, key_values, ids_all, capacity)
    arrived = to_owners(after(sent[0], grads[2:]))
    later = after(sent[1], arrived, same)
    same = after(same, sent[0], grads[1:])
    other = partner(same, 1)

    rows_dev = width // ctx_count
    ff = expert_gate.shape[2]
    swap = rows_dev == PIECE

    def run(arrived, index):
        return expert_part(
            where,
            arrived,
            grads,
            out_proj,
            same,
            other,
            expert_gate,
            expert_up,
            expert_down,
            norm_gain.reshape(1, width),
            ids_all,
            weights_all,
            capacity,
            swap,
            index,
        )

    rows_a, saved_a = run(arrived, 0)
    layer_a = to_owners(rows_a[:experts])
    change_a = to_owners(after(rows_a[experts:], layer_a[1]))
    rows_b, saved_b = run(to_owners(later), 1)
    packed = to_owners(rows_b)
    if swap:
        saved = [saved_a[0], partner(saved_a[1], 1)]
        saved += [saved_b[0], partner(after(saved_b[1], layer_a), 1)]
        parts = weight_blocks(saved, ctx_count // 2, ff, True)
        parts = after(parts, change_a)
        half = ctx_count // 4
        masks = (2, 4), (4, 2)
        near = [partner(x[half:], m[0]) for x, m in zip(parts, masks)]
        sums = [x[:half].astype(F32) + y.astype(F32) for x, y in zip(parts, near)]
        gone = [x[1].astype(BF16) for x in sums]
        far = [partner(x, m[1]) for x, m in zip(gone, masks)]
        packed = after(packed, gone)
        total = [x[0] + y.astype(F32) for x, y in zip(sums, far)]
        total = jnp.concatenate(total, axis=1)
        grad_gate, grad_up = total[0][None], total[1][None]
        grad_down = total[2].reshape(PIECE, ff // PIECE, PIECE).transpose(1, 0, 2)
        grad_down = grad_down.reshape(1, ff, PIECE)
    else:
        blocks = width // PIECE
        (parts,) = weight_blocks(list(saved_a) + list(saved_b), blocks, ff, False)
        part_down = parts[:, 2].reshape(blocks, PIECE, ff // PIECE, PIECE).transpose(0, 2, 1, 3)
        part_down = part_down.reshape(blocks, ff, PIECE // rows_dev, rows_dev)
        part_down = part_down.transpose(0, 2, 1, 3).reshape(ctx_count, ff, rows_dev)
        order = list(range(bits))
        grad_gate, grad_up, grad_down = [
            halved(x.reshape((ctx_count,) + shape), bits, order, ctx)[None]
            for x, shape in (
                (parts[:, 0], (rows_dev, ff)),
                (parts[:, 1], (rows_dev, ff)),
                (part_down, (ff, rows_dev)),
            )
        ]
    layer_out, grad_hidden = restore(where, ids_f, layer_a, change_a, packed, experts, capacity)
    return (layer_out, grad_hidden, grad_gate, grad_up, grad_down)


def solution(mesh):
    in_specs = (
        P(None, "ctx", "exp"),
        P(None, "ctx", None),
        P(None, "ctx", None),
        P("exp", None),
        P(),
        P(("ctx", "exp"), None),
        P(("ctx", "exp"), None),
        P("exp", None, None),
        P("exp", None, None),
        P("exp", None, None),
        P(("ctx", "exp"), None),
    )
    out_specs = (
        P(("ctx", "exp"), None),
        P(("ctx", "exp"), None),
        P("exp", "ctx", None),
        P("exp", "ctx", None),
        P("exp", None, "ctx"),
    )
    return jax.shard_map(
        on_device, mesh=mesh, in_specs=in_specs, out_specs=out_specs, check_vma=False
    )
```

```python
import functools
import math

import jax
import jax.numpy as jnp
from jax import lax
from jax.experimental import pallas as pl
from jax.experimental.pallas import tpu as pltpu
from jax.sharding import PartitionSpec as P

LOCAL_QUERY_HEADS = 16
LOCAL_KEY_HEADS = 2
HEAD_SIZE = 128
PIECE = 256
PARTS = 2

epsilon = 1e-06
masked_score = -1e30
F32 = jnp.float32
BF16 = jnp.bfloat16
VMEM_LIMIT = 60 << 20


def dot(a, b, contract=((1,), (0,))):
    return lax.dot_general(a, b, (contract, ((), ())), preferred_element_type=F32)


def iota(shape, dim):
    return lax.broadcasted_iota(jnp.int32, shape, dim)


def slots_row(ids_row, capacity):
    n = ids_row.shape[1]
    names = iota((16, n), 0).astype(F32)
    chosen = names == ids_row
    before = (iota((n, n), 0) < iota((n, n), 1)).astype(F32).astype(BF16)
    earlier = dot(jnp.where(chosen, 1.0, 0.0).astype(BF16), before)
    return jnp.sum(jnp.where(chosen, earlier + names * capacity, 0.0), axis=0, keepdims=True)


def slots_column(ids_column, capacity):
    n = ids_column.shape[0]
    names = iota((n, 128), 1).astype(F32)
    chosen = names == ids_column
    before = (iota((n, n), 1) < iota((n, n), 0)).astype(F32).astype(BF16)
    earlier = dot(before, jnp.where(chosen, 1.0, 0.0).astype(BF16))
    return jnp.sum(jnp.where(chosen, earlier + names * capacity, 0.0), axis=1, keepdims=True)


def one_hot(matches):
    return jnp.where(matches, 1.0, 0.0).astype(BF16)


def shifted_slots(position, owner, experts, capacity):
    expert = jnp.bitwise_xor(position // capacity, owner)
    return (expert * capacity + lax.rem(position, capacity)).astype(F32)


def kernel_params():
    return pltpu.CompilerParams(vmem_limit_bytes=VMEM_LIMIT)


def brief():
    return pl.CostEstimate(flops=1000, bytes_accessed=1000, transcendentals=0)


def whole(*shape):
    return pl.BlockSpec(shape, lambda *_: (0,) * len(shape))


def smem():
    return pl.BlockSpec(memory_space=pltpu.SMEM)


def attend_kernel(experts, capacity, heads, n_ctx, where_ref, q_ref, ids_ref, *refs):
    count = n_ctx // 2 + 1
    *chips, cores = refs[:count]
    refs = refs[count:]
    blocks = []
    for j, chip in enumerate(chips):
        blocks += [chip, cores.at[j]]
    out_refs, refs = refs[: experts * PARTS], refs[experts * PARTS :]
    k_scr, v_scr, best_scr, acc_scr, att_scr = refs
    ctx, owner = where_ref[0], where_ref[1]
    seq = pl.program_id(0)
    block = q_ref.shape[1]
    tile = 2 * block
    factor = math.log2(math.e) / math.sqrt(HEAD_SIZE)

    @pl.when(seq == 0)
    def _():
        v_scr[:, :, HEAD_SIZE:] = jnp.ones((n_ctx, block, HEAD_SIZE), BF16)

    for m in range(n_ctx):
        index = jnp.bitwise_xor(ctx, m)
        k_scr[index] = blocks[m][0, :, :HEAD_SIZE]
        v_scr[index, :, :HEAD_SIZE] = blocks[m][0, :, HEAD_SIZE:]

    def fold(t, last):
        key_tile = k_scr[pl.ds(2 * t, 2)].reshape(tile, HEAD_SIZE)
        value_tile = v_scr[pl.ds(2 * t, 2)].reshape(tile, 2 * HEAD_SIZE)
        every = range(heads)
        s = [
            dot(q_ref[0, :, h * HEAD_SIZE : (h + 1) * HEAD_SIZE], key_tile, ((1,), (1,)))
            for h in every
        ]
        if last:
            key_pos = iota((block, tile), 1) + t * tile
            query_pos = iota((block, tile), 0) + ctx * block
            s = [jnp.where(key_pos <= query_pos, x, masked_score) for x in s]
        best = [jnp.max(x, axis=1, keepdims=True) for x in s]
        if not last:
            old = [best_scr[h] for h in every]
            best = [jnp.maximum(x, y) for x, y in zip(old, best)]
        p = [jnp.exp2((x - y) * factor).astype(BF16) for x, y in zip(s, best)]
        blended = [dot(x, value_tile) for x in p]
        for h in every:
            if last:
                acc_scr[h] = blended[h]
            else:
                acc_scr[h] = acc_scr[h] * jnp.exp2((old[h] - best[h]) * factor) + blended[h]
            best_scr[h] = best[h]

    fold(ctx // 2, True)

    @pl.loop(0, ctx // 2)
    def _(t):
        fold(t, False)

    for h in range(heads):
        acc = acc_scr[h]
        att = acc[:, :HEAD_SIZE] / acc[:, HEAD_SIZE:]
        att_scr[:, h * HEAD_SIZE : (h + 1) * HEAD_SIZE] = att.astype(BF16)

    n = ids_ref.shape[2]
    part = capacity // PARTS
    per_seq = block // n
    position = iota((experts * capacity, n), 0)
    slots = shifted_slots(position, owner, experts, capacity)
    for b in range(per_seq):
        source = seq * per_seq + b
        target = slots_row(ids_ref[source], capacity)
        picked = dot(one_hot(slots == target), att_scr[b * n : (b + 1) * n, :]).astype(BF16)
        for d in range(experts):
            rank = jnp.bitwise_xor(jnp.bitwise_xor(owner, d), source)
            for c in range(PARTS):
                first = d * capacity + c * part
                out_refs[c * experts + d][rank] = picked[first : first + part]


def attend(where, queries, key_values, ids, capacity):
    seqs, block, width = queries.shape
    n_ctx = 2 * (len(key_values) - 1)
    experts, _, n = ids.shape
    heads = width // HEAD_SIZE
    part = capacity // PARTS
    by_seq = pl.BlockSpec((1, block, 2 * HEAD_SIZE), lambda s: (s, 0, 0))
    outs = pl.pallas_call(
        functools.partial(attend_kernel, experts, capacity, heads, n_ctx),
        grid=(seqs,),
        in_specs=[
            smem(),
            pl.BlockSpec((1, block, width), lambda s: (s, 0, 0)),
            whole(experts, 1, n),
        ]
        + [by_seq] * (len(key_values) - 1)
        + [pl.BlockSpec((n_ctx // 2, 1, block, 2 * HEAD_SIZE), lambda s: (0, s, 0, 0))],
        out_specs=[whole(experts, part, width)] * (PARTS * experts),
        scratch_shapes=[
            pltpu.VMEM((n_ctx, block, HEAD_SIZE), BF16),
            pltpu.VMEM((n_ctx, block, 2 * HEAD_SIZE), BF16),
            pltpu.VMEM((heads, block, 1), F32),
            pltpu.VMEM((heads, block, 2 * HEAD_SIZE), F32),
            pltpu.VMEM((block, width), BF16),
        ],
        out_shape=[jax.ShapeDtypeStruct((experts, part, width), BF16)] * (PARTS * experts),
        compiler_params=kernel_params(),
        cost_estimate=brief(),
        name="attend",
    )(where, queries, ids, *key_values)
    return [outs[c * experts : (c + 1) * experts] for c in range(PARTS)]


def place_kernel(experts, capacity, where_ref, ids_ref, rows_ref, *refs):
    out_refs, pick_scr = refs[:-1], refs[-1]

    @pl.when(pl.program_id(0) == 0)
    def _():
        position = iota(pick_scr.shape, 0)
        slots = shifted_slots(position, where_ref[1], experts, capacity)
        pick_scr[...] = one_hot(slots == slots_row(ids_ref[...], capacity))

    picked = dot(pick_scr[...], rows_ref[...]).astype(BF16)
    for d, ref in enumerate(out_refs):
        ref[...] = picked[d * capacity : (d + 1) * capacity]


def place(where, ids_row, rows, experts, capacity):
    n, width = rows.shape
    cols = min(width, 1024)
    return pl.pallas_call(
        functools.partial(place_kernel, experts, capacity),
        grid=(width // cols,),
        in_specs=[smem(), whole(1, n), pl.BlockSpec((n, cols), lambda i: (0, i))],
        out_specs=[pl.BlockSpec((capacity, cols), lambda i: (0, i))] * experts,
        out_shape=[jax.ShapeDtypeStruct((capacity, width), BF16)] * experts,
        scratch_shapes=[pltpu.VMEM((experts * capacity, n), BF16)],
        compiler_params=kernel_params(),
        cost_estimate=brief(),
        name="place",
    )(where, ids_row, rows)


def restore_kernel(experts, capacity, tiles, where_ref, ids_ref, *refs):
    *parts, layer_ref, grad_ref, pick_scr = refs
    step = pl.program_id(0)

    @pl.when(step == 0)
    def _():
        slots = shifted_slots(iota(pick_scr.shape, 1), where_ref[1], experts, capacity)
        pick_scr[...] = one_hot(slots == slots_column(ids_ref[...], capacity))

    def rows(early, late):
        both = [ref[...] for pair in zip(early, late) for ref in pair]
        return dot(pick_scr[...], jnp.concatenate(both, axis=0)).astype(BF16)

    layer_a, change_a, now = [parts[i * experts : (i + 1) * experts] for i in range(3)]

    @pl.when(step < tiles)
    def _():
        layer_ref[...] = rows(layer_a, now)

    @pl.when(step >= tiles)
    def _():
        grad_ref[...] = rows(change_a, now)


def restore(where, ids_column, layer_a, change_a, packed, experts, capacity):
    n = ids_column.shape[0]
    part, width = layer_a[0].shape
    cols = min(width, 1024)
    tiles = width // cols
    first = lambda i: (0, jnp.minimum(i, tiles - 1))
    second = lambda i: (0, jnp.maximum(i - tiles, 0))
    block = lambda at: [pl.BlockSpec((part, cols), at)] * experts
    return pl.pallas_call(
        functools.partial(restore_kernel, experts, capacity, tiles),
        grid=(2 * tiles,),
        in_specs=[smem(), whole(n, 1)] + block(first) + block(second) + block(lambda i: (0, i)),
        out_specs=[pl.BlockSpec((n, cols), first), pl.BlockSpec((n, cols), second)],
        out_shape=[jax.ShapeDtypeStruct((n, width), BF16)] * 2,
        scratch_shapes=[pltpu.VMEM((n, experts * capacity), BF16)],
        compiler_params=kernel_params(),
        cost_estimate=brief(),
        name="restore",
    )(where, ids_column, *layer_a, *change_a, *packed)


def expert_kernel(experts, capacity, part_index, swap, where_ref, *refs):
    att_refs, refs = refs[:experts], refs[experts:]
    grad_refs, refs = refs[:experts], refs[experts:]
    width_of = grad_refs[0].shape[1]
    own_ref, same_hbm, other_hbm, gate_hbm, up_hbm, down_hbm = refs[:6]
    gain_ref, ids_ref, weight_ref, refs = refs[6], refs[7], refs[8], refs[9:]
    if part_index == 0:
        layer_refs, refs = refs[:experts], refs[experts:]
        change_refs, refs = refs[:experts], refs[experts:]
    else:
        packed_refs, refs = refs[:experts], refs[experts:]
        layer_refs = [ref.at[:, :width_of] for ref in packed_refs]
        change_refs = [ref.at[:, width_of:] for ref in packed_refs]
    saved_refs, refs = refs[: 1 + swap], refs[1 + swap :]
    w_scr, gate_scr, up_scr, down_scr, hidden_scr, normed_ref, back_ref, back_in_scr, sems = refs
    part, width = grad_refs[0].shape
    rows = experts * part
    att_cols = att_refs[0].shape[-1]
    pieces, _, _, piece = w_scr.shape
    ff = gate_scr.shape[1]
    ctx, owner = where_ref[0], where_ref[1]
    core = jnp.bitwise_and(ctx, 1)
    sources = [jnp.bitwise_xor(owner, d) for d in range(experts)]
    units_at, gate_at, up_at, normed_at = 0, ff, 2 * ff, 3 * ff

    copies = []
    for q in range(pieces // 2):
        for ref in (same_hbm, other_hbm):
            m = len(copies)
            copies.append(pltpu.make_async_copy(ref.at[q], w_scr.at[m], sems.at[m]))
    weight_copies = (
        pltpu.make_async_copy(gate_hbm.at[0], gate_scr, sems.at[pieces]),
        pltpu.make_async_copy(up_hbm.at[0], up_scr, sems.at[pieces + 1]),
        pltpu.make_async_copy(down_hbm.at[0], down_scr, sems.at[pieces + 2]),
    )
    for copy in copies:
        copy.start()
    for copy in weight_copies:
        copy.start()

    n = ids_ref.shape[2]
    weights = []
    for s, source in enumerate(sources):
        target = slots_row(ids_ref[source], capacity)
        slot = iota((part, n), 0) + (owner * capacity + part_index * part)
        weights.append(
            jnp.sum(
                jnp.where(slot.astype(F32) == target, weight_ref[source], 0.0),
                axis=1,
                keepdims=True,
            )
        )
        grads = grad_refs[s][...].astype(F32)
        back_ref[s * part : (s + 1) * part, :] = (weights[s] * grads).astype(BF16)

    for m in range(pieces):
        copies[m].wait()
        index = m + core if m % 2 == 0 else m - core
        column = pl.multiple_of(index * piece, piece)
        total = jnp.zeros((rows, piece), F32)
        for d in range(experts):
            block = own_ref[:, pl.ds(column, piece)] if d == 0 else w_scr[m, d - 1]
            total += dot(att_refs[d][...].reshape(rows, att_cols), block)
        hidden_scr[:, pl.ds(column, piece)] = total.astype(BF16)

    squares = jnp.zeros((rows, 1), F32)
    for t in range(0, width, PIECE):
        hidden = hidden_scr[:, t : t + PIECE].astype(F32)
        squares += jnp.sum(hidden * hidden, axis=1, keepdims=True)
    inv = lax.rsqrt(squares / width + epsilon)
    for t in range(0, width, PIECE):
        hidden = hidden_scr[:, t : t + PIECE].astype(F32)
        normed_ref[:, t : t + PIECE] = (hidden * inv * gain_ref[:, t : t + PIECE]).astype(BF16)

    for copy in weight_copies:
        copy.wait()
    for f in range(0, ff, 256):
        gate_act = dot(normed_ref[...], gate_scr[:, f : f + 256])
        up_act = dot(normed_ref[...], up_scr[:, f : f + 256])
        back_units = dot(back_ref[...], down_scr[f : f + 256, :], ((1,), (1,)))
        sigma = 1.0 / (1.0 + jnp.exp(-gate_act))
        gated = gate_act * sigma
        units = (gated * up_act).astype(BF16)
        back_gate = back_units * up_act * sigma * (1.0 + gate_act * (1.0 - sigma))
        back_gate = back_gate.astype(BF16)
        back_up = (back_units * gated).astype(BF16)
        for ref in saved_refs:
            ref[:, units_at + f : units_at + f + 256] = units
            ref[:, gate_at + f : gate_at + f + 256] = back_gate
            ref[:, up_at + f : up_at + f + 256] = back_up

    saved = saved_refs[0]
    half = width // len(saved_refs)
    for c, ref in enumerate(saved_refs):
        for t in range(half // PIECE):
            if swap:
                column = pl.multiple_of(jnp.bitwise_xor(ctx, 2 * t + c) * PIECE, PIECE)
            else:
                column = t * PIECE
            at = normed_at + t * PIECE
            ref[:, at : at + PIECE] = normed_ref[:, pl.ds(column, PIECE)]
            ref[:, at + half : at + half + PIECE] = back_ref[:, pl.ds(column, PIECE)]

    weight = jnp.concatenate(weights, axis=0)
    moment = jnp.zeros((rows, 1), F32)
    for t in range(0, width, PIECE):
        hidden = hidden_scr[:, t : t + PIECE].astype(F32)
        result = dot(saved[:, units_at:gate_at], down_scr[:, t : t + PIECE])
        layer = (hidden + weight * result.astype(BF16).astype(F32)).astype(BF16)
        for s in range(experts):
            layer_refs[s][:, t : t + PIECE] = layer[s * part : (s + 1) * part]
        back_in = dot(saved[:, gate_at:up_at], gate_scr[t : t + PIECE, :], ((1,), (1,)))
        back_in += dot(saved[:, up_at:normed_at], up_scr[t : t + PIECE, :], ((1,), (1,)))
        back_in = back_in.astype(BF16)
        back_in_scr[:, t : t + PIECE] = back_in
        scaled = back_in.astype(F32) * gain_ref[:, t : t + PIECE]
        moment += jnp.sum(scaled * (hidden * inv), axis=1, keepdims=True)
    moment = moment / width
    for t in range(0, width, PIECE):
        unit = hidden_scr[:, t : t + PIECE].astype(F32) * inv
        scaled = back_in_scr[:, t : t + PIECE].astype(F32) * gain_ref[:, t : t + PIECE]
        change = inv * (scaled - unit * moment)
        for s in range(experts):
            grads = grad_refs[s][:, t : t + PIECE].astype(F32)
            change_refs[s][:, t : t + PIECE] = (
                grads + change[s * part : (s + 1) * part]
            ).astype(BF16)


def expert_part(
    where, att, grads, own, same, other, gate, up, down, gain, ids, weights, capacity, swap, index
):
    experts, part, att_cols = att[0].shape
    pieces = 2 * same.shape[0]
    piece = same.shape[-1]
    width = grads[0].shape[1]
    ff = gate.shape[2]
    rows = experts * part
    n = ids.shape[2]
    half = width // 2 if swap else width
    out = lambda *shape: jax.ShapeDtypeStruct(shape, BF16)
    rows_out = [out(part, width)] * (2 * experts) if index == 0 else [out(part, 2 * width)] * experts
    in_hbm = pl.BlockSpec(memory_space=pl.ANY)
    outs = pl.pallas_call(
        functools.partial(expert_kernel, experts, capacity, index, swap),
        grid=(1,),
        in_specs=[smem()]
        + [whole(*x.shape) for x in att]
        + [pl.BlockSpec((part, width), lambda i: (index, 0))] * experts
        + [whole(*own.shape)]
        + [in_hbm] * 5
        + [whole(1, width), whole(experts, 1, n), whole(experts, 1, n)],
        out_specs=[whole(*x.shape) for x in rows_out]
        + [whole(rows, 3 * ff + 2 * half)] * (1 + swap),
        scratch_shapes=[
            pltpu.VMEM((pieces, experts - 1, att_cols, piece), BF16),
            pltpu.VMEM((width, ff), BF16),
            pltpu.VMEM((width, ff), BF16),
            pltpu.VMEM((ff, width), BF16),
            pltpu.VMEM((rows, width), BF16),
            pltpu.VMEM((rows, width), BF16),
            pltpu.VMEM((rows, width), BF16),
            pltpu.VMEM((rows, width), BF16),
            pltpu.SemaphoreType.DMA((pieces + 3,)),
        ],
        out_shape=rows_out
        + [out(rows, 3 * ff + 2 * half)] * (1 + swap),
        compiler_params=kernel_params(),
        cost_estimate=brief(),
        name="expert",
    )(where, *att, *grads, own, same, other, gate, up, down, gain, ids, weights)
    return outs[: len(rows_out)], outs[len(rows_out) :]


def weight_kernel(count, *refs):
    units, back_gate, back_up, normed, back = [refs[i * count : (i + 1) * count] for i in range(5)]
    outs = refs[5 * count :]
    first = ((0,), (0,))

    def total(left, right):
        return sum(dot(a[...], b[...], first) for a, b in zip(left, right)).astype(BF16)

    gate, up, down = total(normed, back_gate), total(normed, back_up), total(units, back)
    cols = down.shape[1]
    part = gate.shape[0] // len(outs)
    for c, ref in enumerate(outs):
        rows = slice(c * part, (c + 1) * part)
        ref[0, 0] = gate[rows]
        ref[0, 1] = up[rows]
        for t in range(0, down.shape[0], cols):
            ref[0, 2, :, t : t + cols] = down[t + c * part : t + (c + 1) * part]


def weight_blocks(saved, blocks, ff, split):
    count = len(saved)
    rows, total = saved[0].shape
    normed_at = 3 * ff // PIECE
    back_at = normed_at + blocks
    thin = lambda at: [pl.BlockSpec((rows, PIECE), lambda i: (0, at + i))] * count
    full = lambda at: [pl.BlockSpec((rows, ff), lambda i: (0, at))] * count
    part = PIECE // 2 if split else PIECE
    shuffled = lambda i: (i % 2 * (blocks // 2) + i // 2, 0, 0, 0)
    plain = lambda i: (i, 0, 0, 0)
    orders = [shuffled, plain] if split else [plain]
    return pl.pallas_call(
        functools.partial(weight_kernel, count),
        grid=(blocks,),
        in_specs=full(0) + full(1) + full(2) + thin(normed_at) + thin(back_at),
        out_specs=[pl.BlockSpec((1, 3, part, ff), order) for order in orders],
        out_shape=[jax.ShapeDtypeStruct((blocks, 3, part, ff), BF16) for _ in orders],
        compiler_params=kernel_params(),
        cost_estimate=brief(),
        name="weight_grads",
    )(*saved * 5)


def partner(value, mask):
    count = lax.axis_size("ctx")
    return lax.ppermute(value, "ctx", [(i, i ^ mask) for i in range(count)])


def to_owner(value, mask):
    count = lax.axis_size("exp")
    return lax.ppermute(value, "exp", [(i, i ^ mask) for i in range(count)])


def to_owners(values):
    return [values[0]] + [to_owner(values[d], d) for d in range(len(values) - 1, 0, -1)][::-1]


def in_two_hops(values):
    if len(values) != 4:
        return to_owners(values)
    near = to_owner(jnp.stack(values[1:3]), 1)
    far = to_owner(values[3], 3)
    return [values[0], near[0], to_owner(near[1], 3), far]


def chip_groups(count):
    return [
        list(range(first + core, first + count, 2))
        for first in range(0, lax.axis_size("ctx"), count)
        for core in range(2)
    ]


def after(value, *others):
    return lax.optimization_barrier((value, others))[0]


def halved(value, bits, order, ctx):
    shape = value.shape[1:]
    held = value.reshape((2,) * bits + shape)
    for place_in_order, bit in enumerate(order):
        axis = bits - 1 - bit
        mine = (ctx >> bit) & 1
        gone = lax.dynamic_slice_in_dim(held, 1 - mine, 1, axis)
        kept = lax.dynamic_slice_in_dim(held, mine, 1, axis)
        held = kept.astype(F32) + partner(gone, 1 << bit).astype(F32)
        if place_in_order < bits - 1:
            held = held.astype(BF16)
    return held.reshape(shape)


def on_device(
    queries,
    rotated_key_heads,
    value_head_rows,
    out_proj,
    norm_gain,
    expert_ids,
    gate_weights,
    expert_gate,
    expert_up,
    expert_down,
    grad_out,
):
    heads_dev = queries.shape[2] // HEAD_SIZE
    group = LOCAL_QUERY_HEADS // LOCAL_KEY_HEADS
    exp_count = lax.axis_size("exp")
    ctx_count = lax.axis_size("ctx")
    owner = lax.axis_index("exp")
    ctx = lax.axis_index("ctx")
    bits = ctx_count.bit_length() - 1
    n, _ = expert_ids.shape
    width = grad_out.shape[1]
    experts = exp_count
    capacity = min(n, 2 * n // experts)
    pieces = min(ctx_count, width // PIECE)
    piece = width // pieces
    piece_index = ctx % pieces
    where = jnp.stack([ctx, owner, piece_index]).astype(jnp.int32)

    ids_f = expert_ids.astype(F32)
    info = jnp.stack([ids_f[:, 0], gate_weights[:, 0]])
    info = jnp.broadcast_to(info[None], (exp_count,) + info.shape)
    info = lax.all_to_all(info, "exp", 0, 0, tiled=True)
    ids_all, weights_all = info[:, 0:1, :], info[:, 1:2, :]

    mine = lax.dynamic_slice_in_dim(out_proj, piece_index * piece, piece, 1)
    mine = lax.all_gather(mine, "exp")
    projection = [lax.dynamic_index_in_dim(mine, owner ^ d, 0, False) for d in range(1, exp_count)]

    first_column = (owner * heads_dev // group) * HEAD_SIZE
    keys = lax.dynamic_slice_in_dim(rotated_key_heads, first_column, HEAD_SIZE, 2)
    values = lax.dynamic_slice_in_dim(value_head_rows, first_column, HEAD_SIZE, 2)
    own = jnp.concatenate([keys, values], axis=2)
    chips = [own] + [partner(own, m) for m in range(2, ctx_count, 2)]
    key_values = chips + [partner(jnp.stack(chips), 1)]

    grads = place(where, ids_f.reshape(1, n), grad_out, experts, capacity)
    grads = to_owners(grads)

    projection = after(jnp.stack(projection), chips)
    projection = jnp.broadcast_to(projection[None], (pieces // 2,) + projection.shape)
    same = lax.all_to_all(
        projection, "ctx", 0, 0, axis_index_groups=chip_groups(pieces), tiled=True
    )

    sent = attend(where, after(queries, grads[1:]), key_values, ids_all, capacity)
    arrived = in_two_hops(sent[0])
    later = after(sent[1], arrived, same)
    same = after(same, sent[0])
    other = partner(same, 1)

    rows_dev = width // ctx_count
    ff = expert_gate.shape[2]
    swap = rows_dev == PIECE

    def run(arrived, index):
        return expert_part(
            where,
            arrived,
            grads,
            out_proj,
            same,
            other,
            expert_gate,
            expert_up,
            expert_down,
            norm_gain.reshape(1, width),
            ids_all,
            weights_all,
            capacity,
            swap,
            index,
        )

    rows_a, saved_a = run(arrived, 0)
    layer_a = to_owners(rows_a[:experts])
    change_a = in_two_hops(after(rows_a[experts:], layer_a[1]))
    rows_b, saved_b = run(to_owners(later), 1)
    packed = in_two_hops(rows_b)
    if swap:
        saved = [saved_a[0], partner(saved_a[1], 1)]
        saved += [saved_b[0], partner(after(saved_b[1], layer_a), 1)]
        parts = weight_blocks(saved, ctx_count // 2, ff, True)
        parts = after(parts, change_a)
        half = ctx_count // 4
        masks = (2, 4), (4, 2)
        near = [partner(x[half:], m[0]) for x, m in zip(parts, masks)]
        sums = [x[:half].astype(F32) + y.astype(F32) for x, y in zip(parts, near)]
        gone = [x[1].astype(BF16) for x in sums]
        far = [partner(x, m[1]) for x, m in zip(gone, masks)]
        packed = after(packed, gone)
        total = [x[0] + y.astype(F32) for x, y in zip(sums, far)]
        total = jnp.concatenate(total, axis=1)
        grad_gate, grad_up = total[0][None], total[1][None]
        grad_down = total[2].reshape(PIECE, ff // PIECE, PIECE).transpose(1, 0, 2)
        grad_down = grad_down.reshape(1, ff, PIECE)
    else:
        blocks = width // PIECE
        (parts,) = weight_blocks(list(saved_a) + list(saved_b), blocks, ff, False)
        part_down = parts[:, 2].reshape(blocks, PIECE, ff // PIECE, PIECE).transpose(0, 2, 1, 3)
        part_down = part_down.reshape(blocks, ff, PIECE // rows_dev, rows_dev)
        part_down = part_down.transpose(0, 2, 1, 3).reshape(ctx_count, ff, rows_dev)
        order = list(range(bits))
        grad_gate, grad_up, grad_down = [
            halved(x.reshape((ctx_count,) + shape), bits, order, ctx)[None]
            for x, shape in (
                (parts[:, 0], (rows_dev, ff)),
                (parts[:, 1], (rows_dev, ff)),
                (part_down, (ff, rows_dev)),
            )
        ]
    layer_out, grad_hidden = restore(where, ids_f, layer_a, change_a, packed, experts, capacity)
    return (layer_out, grad_hidden, grad_gate, grad_up, grad_down)


def solution(mesh):
    in_specs = (
        P(None, "ctx", "exp"),
        P(None, "ctx", None),
        P(None, "ctx", None),
        P("exp", None),
        P(),
        P(("ctx", "exp"), None),
        P(("ctx", "exp"), None),
        P("exp", None, None),
        P("exp", None, None),
        P("exp", None, None),
        P(("ctx", "exp"), None),
    )
    out_specs = (
        P(("ctx", "exp"), None),
        P(("ctx", "exp"), None),
        P("exp", "ctx", None),
        P("exp", "ctx", None),
        P("exp", None, "ctx"),
    )
    return jax.shard_map(
        on_device, mesh=mesh, in_specs=in_specs, out_specs=out_specs, check_vma=False
    )
```

```python
import functools
import math

import jax
import jax.numpy as jnp
from jax import lax
from jax.experimental import pallas as pl
from jax.experimental.pallas import tpu as pltpu
from jax.sharding import PartitionSpec as P

LOCAL_QUERY_HEADS = 16
LOCAL_KEY_HEADS = 2
HEAD_SIZE = 128
PIECE = 256
PARTS = 2

epsilon = 1e-06
masked_score = -1e30
F32 = jnp.float32
BF16 = jnp.bfloat16
VMEM_LIMIT = 60 << 20


def dot(a, b, contract=((1,), (0,))):
    return lax.dot_general(a, b, (contract, ((), ())), preferred_element_type=F32)


def iota(shape, dim):
    return lax.broadcasted_iota(jnp.int32, shape, dim)


def slots_row(ids_row, capacity):
    n = ids_row.shape[1]
    names = iota((16, n), 0).astype(F32)
    chosen = names == ids_row
    before = (iota((n, n), 0) < iota((n, n), 1)).astype(F32).astype(BF16)
    earlier = dot(jnp.where(chosen, 1.0, 0.0).astype(BF16), before)
    return jnp.sum(jnp.where(chosen, earlier + names * capacity, 0.0), axis=0, keepdims=True)


def slots_column(ids_column, capacity):
    n = ids_column.shape[0]
    names = iota((n, 128), 1).astype(F32)
    chosen = names == ids_column
    before = (iota((n, n), 1) < iota((n, n), 0)).astype(F32).astype(BF16)
    earlier = dot(before, jnp.where(chosen, 1.0, 0.0).astype(BF16))
    return jnp.sum(jnp.where(chosen, earlier + names * capacity, 0.0), axis=1, keepdims=True)


def one_hot(matches):
    return jnp.where(matches, 1.0, 0.0).astype(BF16)


def shifted_slots(position, owner, experts, capacity):
    expert = jnp.bitwise_xor(position // capacity, owner)
    return (expert * capacity + lax.rem(position, capacity)).astype(F32)


def kernel_params():
    return pltpu.CompilerParams(vmem_limit_bytes=VMEM_LIMIT)


def brief():
    return pl.CostEstimate(flops=1000, bytes_accessed=1000, transcendentals=0)


def whole(*shape):
    return pl.BlockSpec(shape, lambda *_: (0,) * len(shape))


def smem():
    return pl.BlockSpec(memory_space=pltpu.SMEM)


def attend_kernel(experts, capacity, heads, n_ctx, where_ref, q_ref, ids_ref, *refs):
    count = n_ctx // 2 + 1
    *chips, cores = refs[:count]
    refs = refs[count:]
    blocks = []
    for j, chip in enumerate(chips):
        blocks += [chip, cores.at[j]]
    out_refs, refs = refs[: experts * PARTS], refs[experts * PARTS :]
    k_scr, v_scr, best_scr, acc_scr, att_scr = refs
    ctx, owner = where_ref[0], where_ref[1]
    seq = pl.program_id(0)
    block = q_ref.shape[1]
    tile = 2 * block
    factor = math.log2(math.e) / math.sqrt(HEAD_SIZE)

    @pl.when(seq == 0)
    def _():
        v_scr[:, :, HEAD_SIZE:] = jnp.ones((n_ctx, block, HEAD_SIZE), BF16)

    for m in range(n_ctx):
        index = jnp.bitwise_xor(ctx, m)
        k_scr[index] = blocks[m][0, :, :HEAD_SIZE]
        v_scr[index, :, :HEAD_SIZE] = blocks[m][0, :, HEAD_SIZE:]

    def fold(t, last):
        key_tile = k_scr[pl.ds(2 * t, 2)].reshape(tile, HEAD_SIZE)
        value_tile = v_scr[pl.ds(2 * t, 2)].reshape(tile, 2 * HEAD_SIZE)
        for h in range(heads):
            q = q_ref[0, :, h * HEAD_SIZE : (h + 1) * HEAD_SIZE]
            s = dot(q, key_tile, ((1,), (1,)))
            if last:
                key_pos = iota((block, tile), 1) + t * tile
                query_pos = iota((block, tile), 0) + ctx * block
                s = jnp.where(key_pos <= query_pos, s, masked_score)
            best = jnp.max(s, axis=1, keepdims=True)
            if not last:
                old = best_scr[h]
                best = jnp.maximum(old, best)
            p = jnp.exp2((s - best) * factor)
            blended = dot(p.astype(BF16), value_tile)
            if last:
                acc_scr[h] = blended
            else:
                acc_scr[h] = acc_scr[h] * jnp.exp2((old - best) * factor) + blended
            best_scr[h] = best

    fold(ctx // 2, True)

    @pl.loop(0, ctx // 2)
    def _(t):
        fold(t, False)

    for h in range(heads):
        acc = acc_scr[h]
        att = acc[:, :HEAD_SIZE] / acc[:, HEAD_SIZE:]
        att_scr[:, h * HEAD_SIZE : (h + 1) * HEAD_SIZE] = att.astype(BF16)

    n = ids_ref.shape[2]
    part = capacity // PARTS
    per_seq = block // n
    position = iota((experts * capacity, n), 0)
    slots = shifted_slots(position, owner, experts, capacity)
    for b in range(per_seq):
        source = seq * per_seq + b
        target = slots_row(ids_ref[jnp.bitwise_xor(owner, source)], capacity)
        picked = dot(one_hot(slots == target), att_scr[b * n : (b + 1) * n, :]).astype(BF16)
        for d in range(experts):
            rank = jnp.bitwise_xor(jnp.bitwise_xor(owner, d), source)
            for c in range(PARTS):
                first = d * capacity + c * part
                out_refs[c * experts + d][rank] = picked[first : first + part]


def attend(where, queries, key_values, ids, capacity):
    seqs, block, width = queries.shape
    n_ctx = 2 * (len(key_values) - 1)
    experts, _, n = ids.shape
    heads = width // HEAD_SIZE
    part = capacity // PARTS
    by_seq = pl.BlockSpec((1, block, 2 * HEAD_SIZE), lambda s: (s, 0, 0))
    outs = pl.pallas_call(
        functools.partial(attend_kernel, experts, capacity, heads, n_ctx),
        grid=(seqs,),
        in_specs=[
            smem(),
            pl.BlockSpec((1, block, width), lambda s: (s, 0, 0)),
            whole(experts, 1, n),
        ]
        + [by_seq] * (len(key_values) - 1)
        + [pl.BlockSpec((n_ctx // 2, 1, block, 2 * HEAD_SIZE), lambda s: (0, s, 0, 0))],
        out_specs=[whole(experts, part, width)] * (PARTS * experts),
        scratch_shapes=[
            pltpu.VMEM((n_ctx, block, HEAD_SIZE), BF16),
            pltpu.VMEM((n_ctx, block, 2 * HEAD_SIZE), BF16),
            pltpu.VMEM((heads, block, 1), F32),
            pltpu.VMEM((heads, block, 2 * HEAD_SIZE), F32),
            pltpu.VMEM((block, width), BF16),
        ],
        out_shape=[jax.ShapeDtypeStruct((experts, part, width), BF16)] * (PARTS * experts),
        compiler_params=kernel_params(),
        cost_estimate=brief(),
        name="attend",
    )(where, queries, ids, *key_values)
    return [outs[c * experts : (c + 1) * experts] for c in range(PARTS)]


def place_kernel(capacity, ids_ref, rows_ref, out_ref, pick_scr):
    @pl.when(pl.program_id(0) == 0)
    def _():
        position = iota(pick_scr.shape, 0)
        pick_scr[...] = one_hot(position.astype(F32) == slots_row(ids_ref[...], capacity))

    out_ref[...] = dot(pick_scr[...], rows_ref[...]).astype(BF16).reshape(out_ref.shape)


def place(ids_row, rows, experts, capacity):
    n, width = rows.shape
    cols = min(width, 1024)
    return pl.pallas_call(
        functools.partial(place_kernel, capacity),
        grid=(width // cols,),
        in_specs=[whole(1, n), pl.BlockSpec((n, cols), lambda i: (0, i))],
        out_specs=pl.BlockSpec((experts, capacity, cols), lambda i: (0, 0, i)),
        out_shape=jax.ShapeDtypeStruct((experts, capacity, width), BF16),
        scratch_shapes=[pltpu.VMEM((experts * capacity, n), BF16)],
        compiler_params=kernel_params(),
        cost_estimate=brief(),
        name="place",
    )(ids_row, rows)


def restore_kernel(experts, capacity, tiles, where_ref, ids_ref, *refs):
    *parts, layer_ref, grad_ref, pick_scr = refs
    step = pl.program_id(0)

    @pl.when(step == 0)
    def _():
        slots = shifted_slots(iota(pick_scr.shape, 1), where_ref[1], experts, capacity)
        pick_scr[...] = one_hot(slots == slots_column(ids_ref[...], capacity))

    def rows(early, late):
        both = [ref[...] for pair in zip(early, late) for ref in pair]
        return dot(pick_scr[...], jnp.concatenate(both, axis=0)).astype(BF16)

    layer_a, change_a, now = [parts[i * experts : (i + 1) * experts] for i in range(3)]

    @pl.when(step < tiles)
    def _():
        layer_ref[...] = rows(layer_a, now)

    @pl.when(step >= tiles)
    def _():
        grad_ref[...] = rows(change_a, now)


def restore(where, ids_column, layer_a, change_a, packed, experts, capacity):
    n = ids_column.shape[0]
    part, width = layer_a[0].shape
    cols = min(width, 1024)
    tiles = width // cols
    first = lambda i: (0, jnp.minimum(i, tiles - 1))
    second = lambda i: (0, jnp.maximum(i - tiles, 0))
    block = lambda at: [pl.BlockSpec((part, cols), at)] * experts
    return pl.pallas_call(
        functools.partial(restore_kernel, experts, capacity, tiles),
        grid=(2 * tiles,),
        in_specs=[smem(), whole(n, 1)] + block(first) + block(second) + block(lambda i: (0, i)),
        out_specs=[pl.BlockSpec((n, cols), first), pl.BlockSpec((n, cols), second)],
        out_shape=[jax.ShapeDtypeStruct((n, width), BF16)] * 2,
        scratch_shapes=[pltpu.VMEM((n, experts * capacity), BF16)],
        compiler_params=kernel_params(),
        cost_estimate=brief(),
        name="restore",
    )(where, ids_column, *layer_a, *change_a, *packed)


def expert_kernel(pieces, experts, capacity, part_index, swap, where_ref, *refs):
    att_refs, refs = refs[:experts], refs[experts:]
    grad_ref, refs = refs[0], refs[1:]
    width_of = grad_ref.shape[2]
    own_ref, refs = refs[0], refs[1:]
    same_hbms, refs = refs[: pieces // 2], refs[pieces // 2 :]
    other_hbm, gate_hbm, up_hbm, down_hbm = refs[:4]
    gain_ref, ids_ref, weight_ref, refs = refs[4], refs[5], refs[6], refs[7:]
    if part_index == 0:
        layer_refs, refs = refs[:experts], refs[experts:]
        change_refs, refs = refs[:experts], refs[experts:]
    else:
        packed_refs, refs = refs[:experts], refs[experts:]
        layer_refs = [ref.at[:, :width_of] for ref in packed_refs]
        change_refs = [ref.at[:, width_of:] for ref in packed_refs]
    saved_refs, refs = refs[: 1 + swap], refs[1 + swap :]
    w_scr, gate_scr, up_scr, down_scr, hidden_scr, normed_ref, back_ref, back_in_scr, sems = refs
    _, part, width = grad_ref.shape
    rows = experts * part
    att_cols = att_refs[0].shape[-1]
    piece = w_scr.shape[3]
    ff = gate_scr.shape[1]
    ctx, owner = where_ref[0], where_ref[1]
    sources = [jnp.bitwise_xor(owner, d) for d in range(experts)]
    units_at, gate_at, up_at, normed_at = 0, ff, 2 * ff, 3 * ff

    copies = []
    for q in range(pieces // 2):
        for block in (same_hbms[q], other_hbm.at[q]):
            m = len(copies)
            copies.append(pltpu.make_async_copy(block, w_scr.at[m], sems.at[m]))
    weight_copies = (
        pltpu.make_async_copy(gate_hbm.at[0], gate_scr, sems.at[pieces]),
        pltpu.make_async_copy(up_hbm.at[0], up_scr, sems.at[pieces + 1]),
        pltpu.make_async_copy(down_hbm.at[0], down_scr, sems.at[pieces + 2]),
    )
    for copy in copies:
        copy.start()
    for copy in weight_copies:
        copy.start()

    n = ids_ref.shape[2]
    weights = []
    for s, source in enumerate(sources):
        target = slots_row(ids_ref[s], capacity)
        slot = iota((part, n), 0) + (owner * capacity + part_index * part)
        weights.append(
            jnp.sum(
                jnp.where(slot.astype(F32) == target, weight_ref[s], 0.0),
                axis=1,
                keepdims=True,
            )
        )
        grads = grad_ref[source].astype(F32)
        back_ref[s * part : (s + 1) * part, :] = (weights[s] * grads).astype(BF16)

    for m in range(pieces):
        copies[m].wait()
        column = pl.multiple_of(jnp.bitwise_xor(where_ref[2], m) * piece, piece)
        total = jnp.zeros((rows, piece), F32)
        for d in range(experts):
            block = own_ref[:, pl.ds(column, piece)] if d == 0 else w_scr[m, d - 1]
            total += dot(att_refs[d][...].reshape(rows, att_cols), block)
        hidden_scr[:, pl.ds(column, piece)] = total.astype(BF16)

    squares = jnp.zeros((rows, 1), F32)
    for t in range(0, width, PIECE):
        hidden = hidden_scr[:, t : t + PIECE].astype(F32)
        squares += jnp.sum(hidden * hidden, axis=1, keepdims=True)
    inv = lax.rsqrt(squares / width + epsilon)
    for t in range(0, width, PIECE):
        hidden = hidden_scr[:, t : t + PIECE].astype(F32)
        normed_ref[:, t : t + PIECE] = (hidden * inv * gain_ref[:, t : t + PIECE]).astype(BF16)

    for copy in weight_copies:
        copy.wait()
    for f in range(0, ff, 256):
        gate_act = dot(normed_ref[...], gate_scr[:, f : f + 256])
        up_act = dot(normed_ref[...], up_scr[:, f : f + 256])
        back_units = dot(back_ref[...], down_scr[f : f + 256, :], ((1,), (1,)))
        sigma = 1.0 / (1.0 + jnp.exp(-gate_act))
        gated = gate_act * sigma
        units = (gated * up_act).astype(BF16)
        back_gate = back_units * up_act * sigma * (1.0 + gate_act * (1.0 - sigma))
        back_gate = back_gate.astype(BF16)
        back_up = (back_units * gated).astype(BF16)
        for ref in saved_refs:
            ref[:, units_at + f : units_at + f + 256] = units
            ref[:, gate_at + f : gate_at + f + 256] = back_gate
            ref[:, up_at + f : up_at + f + 256] = back_up

    saved = saved_refs[0]
    half = width // len(saved_refs)
    for c, ref in enumerate(saved_refs):
        for t in range(half // PIECE):
            if swap:
                column = pl.multiple_of(jnp.bitwise_xor(ctx, 2 * t + c) * PIECE, PIECE)
            else:
                column = t * PIECE
            at = normed_at + t * PIECE
            ref[:, at : at + PIECE] = normed_ref[:, pl.ds(column, PIECE)]
            ref[:, at + half : at + half + PIECE] = back_ref[:, pl.ds(column, PIECE)]

    weight = jnp.concatenate(weights, axis=0)
    moment = jnp.zeros((rows, 1), F32)
    for t in range(0, width, PIECE):
        hidden = hidden_scr[:, t : t + PIECE].astype(F32)
        result = dot(saved[:, units_at:gate_at], down_scr[:, t : t + PIECE])
        layer = (hidden + weight * result.astype(BF16).astype(F32)).astype(BF16)
        for s in range(experts):
            layer_refs[s][:, t : t + PIECE] = layer[s * part : (s + 1) * part]
        back_in = dot(saved[:, gate_at:up_at], gate_scr[t : t + PIECE, :], ((1,), (1,)))
        back_in += dot(saved[:, up_at:normed_at], up_scr[t : t + PIECE, :], ((1,), (1,)))
        back_in = back_in.astype(BF16)
        back_in_scr[:, t : t + PIECE] = back_in
        scaled = back_in.astype(F32) * gain_ref[:, t : t + PIECE]
        moment += jnp.sum(scaled * (hidden * inv), axis=1, keepdims=True)
    moment = moment / width
    for t in range(0, width, PIECE):
        unit = hidden_scr[:, t : t + PIECE].astype(F32) * inv
        scaled = back_in_scr[:, t : t + PIECE].astype(F32) * gain_ref[:, t : t + PIECE]
        change = inv * (scaled - unit * moment)
        for s in range(experts):
            grads = grad_ref[sources[s], :, t : t + PIECE].astype(F32)
            change_refs[s][:, t : t + PIECE] = (
                grads + change[s * part : (s + 1) * part]
            ).astype(BF16)


def expert_part(
    where, att, grads, own, same, other, gate, up, down, gain, ids, weights, capacity, swap, index
):
    experts, part, att_cols = att[0].shape
    pieces = 2 * len(same)
    piece = same[0].shape[-1]
    width = grads.shape[2]
    ff = gate.shape[2]
    rows = experts * part
    n = ids.shape[2]
    half = width // 2 if swap else width
    out = lambda *shape: jax.ShapeDtypeStruct(shape, BF16)
    rows_out = [out(part, width)] * (2 * experts) if index == 0 else [out(part, 2 * width)] * experts
    in_hbm = pl.BlockSpec(memory_space=pl.ANY)
    outs = pl.pallas_call(
        functools.partial(expert_kernel, pieces, experts, capacity, index, swap),
        grid=(1,),
        in_specs=[smem()]
        + [whole(*x.shape) for x in att]
        + [pl.BlockSpec((experts, part, width), lambda i: (0, index, 0))]
        + [whole(*own.shape)]
        + [in_hbm] * (len(same) + 4)
        + [whole(1, width), whole(experts, 1, n), whole(experts, 1, n)],
        out_specs=[whole(*x.shape) for x in rows_out]
        + [whole(rows, 3 * ff + 2 * half)] * (1 + swap),
        scratch_shapes=[
            pltpu.VMEM((pieces, experts - 1, att_cols, piece), BF16),
            pltpu.VMEM((width, ff), BF16),
            pltpu.VMEM((width, ff), BF16),
            pltpu.VMEM((ff, width), BF16),
            pltpu.VMEM((rows, width), BF16),
            pltpu.VMEM((rows, width), BF16),
            pltpu.VMEM((rows, width), BF16),
            pltpu.VMEM((rows, width), BF16),
            pltpu.SemaphoreType.DMA((pieces + 3,)),
        ],
        out_shape=rows_out
        + [out(rows, 3 * ff + 2 * half)] * (1 + swap),
        compiler_params=kernel_params(),
        cost_estimate=brief(),
        name="expert",
    )(where, *att, grads, own, *same, other, gate, up, down, gain, ids, weights)
    return outs[: len(rows_out)], outs[len(rows_out) :]


def weight_kernel(count, *refs):
    units, back_gate, back_up, normed, back = [refs[i * count : (i + 1) * count] for i in range(5)]
    outs = refs[5 * count :]
    first = ((0,), (0,))

    def total(left, right):
        return sum(dot(a[...], b[...], first) for a, b in zip(left, right)).astype(BF16)

    gate, up, down = total(normed, back_gate), total(normed, back_up), total(units, back)
    cols = down.shape[1]
    part = gate.shape[0] // len(outs)
    for c, ref in enumerate(outs):
        rows = slice(c * part, (c + 1) * part)
        ref[0, 0] = gate[rows]
        ref[0, 1] = up[rows]
        for t in range(0, down.shape[0], cols):
            ref[0, 2, :, t : t + cols] = down[t + c * part : t + (c + 1) * part]


def weight_blocks(saved, blocks, ff, split):
    count = len(saved)
    rows, total = saved[0].shape
    normed_at = 3 * ff // PIECE
    back_at = normed_at + blocks
    thin = lambda at: [pl.BlockSpec((rows, PIECE), lambda i: (0, at + i))] * count
    full = lambda at: [pl.BlockSpec((rows, ff), lambda i: (0, at))] * count
    part = PIECE // 2 if split else PIECE
    shuffled = lambda i: (i % 2 * (blocks // 2) + i // 2, 0, 0, 0)
    plain = lambda i: (i, 0, 0, 0)
    orders = [shuffled, plain] if split else [plain]
    return pl.pallas_call(
        functools.partial(weight_kernel, count),
        grid=(blocks,),
        in_specs=full(0) + full(1) + full(2) + thin(normed_at) + thin(back_at),
        out_specs=[pl.BlockSpec((1, 3, part, ff), order) for order in orders],
        out_shape=[jax.ShapeDtypeStruct((blocks, 3, part, ff), BF16) for _ in orders],
        compiler_params=kernel_params(),
        cost_estimate=brief(),
        name="weight_grads",
    )(*saved * 5)


def partner(value, mask):
    count = lax.axis_size("ctx")
    return lax.ppermute(value, "ctx", [(i, i ^ mask) for i in range(count)])


def to_owner(value, mask):
    count = lax.axis_size("exp")
    return lax.ppermute(value, "exp", [(i, i ^ mask) for i in range(count)])


def to_owners(values):
    return [values[0]] + [to_owner(values[d], d) for d in range(len(values) - 1, 0, -1)][::-1]


def after(value, *others):
    return lax.optimization_barrier((value, others))[0]


def halved(value, bits, order, ctx):
    shape = value.shape[1:]
    held = value.reshape((2,) * bits + shape)
    for place_in_order, bit in enumerate(order):
        axis = bits - 1 - bit
        mine = (ctx >> bit) & 1
        gone = lax.dynamic_slice_in_dim(held, 1 - mine, 1, axis)
        kept = lax.dynamic_slice_in_dim(held, mine, 1, axis)
        held = kept.astype(F32) + partner(gone, 1 << bit).astype(F32)
        if place_in_order < bits - 1:
            held = held.astype(BF16)
    return held.reshape(shape)


def on_device(
    queries,
    rotated_key_heads,
    value_head_rows,
    out_proj,
    norm_gain,
    expert_ids,
    gate_weights,
    expert_gate,
    expert_up,
    expert_down,
    grad_out,
):
    heads_dev = queries.shape[2] // HEAD_SIZE
    group = LOCAL_QUERY_HEADS // LOCAL_KEY_HEADS
    exp_count = lax.axis_size("exp")
    ctx_count = lax.axis_size("ctx")
    owner = lax.axis_index("exp")
    ctx = lax.axis_index("ctx")
    bits = ctx_count.bit_length() - 1
    n, _ = expert_ids.shape
    width = grad_out.shape[1]
    experts = exp_count
    capacity = min(n, 2 * n // experts)
    pieces = min(ctx_count, width // PIECE)
    piece = width // pieces
    piece_index = ctx % pieces
    where = jnp.stack([ctx, owner, piece_index]).astype(jnp.int32)

    ids_f = expert_ids.astype(F32)
    gates = gate_weights[:, 0]
    high = lax.optimization_barrier(gates.astype(BF16))
    middle = lax.optimization_barrier((gates - high.astype(F32)).astype(BF16))
    low = (gates - high.astype(F32) - middle.astype(F32)).astype(BF16)
    info = jnp.stack([ids_f[:, 0].astype(BF16), high, middle, low])
    info = jnp.pad(info, ((0, 12), (0, piece - n)))
    mine = lax.dynamic_slice_in_dim(out_proj, piece_index * piece, piece, 1)
    depth = mine.shape[0]
    arrivals = to_owners([jnp.concatenate([mine, info])] * exp_count)
    projection = [x[:depth] for x in arrivals[1:]]
    info = jnp.stack([x[depth : depth + 4, :n] for x in arrivals]).astype(F32)
    ids_all, weights_all = info[:, 0:1], info[:, 1:2] + info[:, 2:3] + info[:, 3:4]

    first_column = (owner * heads_dev // group) * HEAD_SIZE
    keys = lax.dynamic_slice_in_dim(rotated_key_heads, first_column, HEAD_SIZE, 2)
    values = lax.dynamic_slice_in_dim(value_head_rows, first_column, HEAD_SIZE, 2)
    own = jnp.concatenate([keys, values], axis=2)
    chips = [own] + [partner(own, m) for m in range(2, ctx_count, 2)]
    key_values = chips + [partner(jnp.stack(chips), 1)]

    grads = place(ids_f.reshape(1, n), grad_out, experts, capacity)
    grads = lax.all_to_all(grads, "exp", 0, 0, tiled=True)

    projection = after(jnp.stack(projection), chips)
    same = [projection] + [partner(projection, m) for m in range(2, pieces, 2)]

    sent = attend(where, queries, key_values, ids_all, capacity)
    arrived = to_owners(after(sent[0], grads))
    later = after(sent[1], arrived, same)
    same = after(same, sent[0])
    other = partner(jnp.stack(same), 1)

    rows_dev = width // ctx_count
    ff = expert_gate.shape[2]
    swap = rows_dev == PIECE

    def run(arrived, index):
        return expert_part(
            where,
            arrived,
            grads,
            out_proj,
            same,
            other,
            expert_gate,
            expert_up,
            expert_down,
            norm_gain.reshape(1, width),
            ids_all,
            weights_all,
            capacity,
            swap,
            index,
        )

    rows_a, saved_a = run(arrived, 0)
    layer_a = to_owners(rows_a[:experts])
    change_a = to_owners(after(rows_a[experts:], layer_a[1]))
    rows_b, saved_b = run(to_owners(later), 1)
    packed = to_owners(rows_b)
    if swap:
        saved = [saved_a[0], partner(saved_a[1], 1)]
        saved += [saved_b[0], partner(after(saved_b[1], layer_a), 1)]
        parts = weight_blocks(saved, ctx_count // 2, ff, True)
        parts = after(parts, change_a)
        half = ctx_count // 4
        masks = (2, 4), (4, 2)
        near = [partner(x[half:], m[0]) for x, m in zip(parts, masks)]
        sums = [x[:half].astype(F32) + y.astype(F32) for x, y in zip(parts, near)]
        gone = [x[1].astype(BF16) for x in sums]
        far = [partner(x, m[1]) for x, m in zip(gone, masks)]
        packed = after(packed, gone)
        total = [x[0] + y.astype(F32) for x, y in zip(sums, far)]
        total = jnp.concatenate(total, axis=1)
        grad_gate, grad_up = total[0][None], total[1][None]
        grad_down = total[2].reshape(PIECE, ff // PIECE, PIECE).transpose(1, 0, 2)
        grad_down = grad_down.reshape(1, ff, PIECE)
    else:
        blocks = width // PIECE
        (parts,) = weight_blocks(list(saved_a) + list(saved_b), blocks, ff, False)
        part_down = parts[:, 2].reshape(blocks, PIECE, ff // PIECE, PIECE).transpose(0, 2, 1, 3)
        part_down = part_down.reshape(blocks, ff, PIECE // rows_dev, rows_dev)
        part_down = part_down.transpose(0, 2, 1, 3).reshape(ctx_count, ff, rows_dev)
        order = list(range(bits))
        grad_gate, grad_up, grad_down = [
            halved(x.reshape((ctx_count,) + shape), bits, order, ctx)[None]
            for x, shape in (
                (parts[:, 0], (rows_dev, ff)),
                (parts[:, 1], (rows_dev, ff)),
                (part_down, (ff, rows_dev)),
            )
        ]
    layer_out, grad_hidden = restore(where, ids_f, layer_a, change_a, packed, experts, capacity)
    return (layer_out, grad_hidden, grad_gate, grad_up, grad_down)


def solution(mesh):
    in_specs = (
        P(None, "ctx", "exp"),
        P(None, "ctx", None),
        P(None, "ctx", None),
        P("exp", None),
        P(),
        P(("ctx", "exp"), None),
        P(("ctx", "exp"), None),
        P("exp", None, None),
        P("exp", None, None),
        P("exp", None, None),
        P(("ctx", "exp"), None),
    )
    out_specs = (
        P(("ctx", "exp"), None),
        P(("ctx", "exp"), None),
        P("exp", "ctx", None),
        P("exp", "ctx", None),
        P("exp", None, "ctx"),
    )
    return jax.shard_map(
        on_device, mesh=mesh, in_specs=in_specs, out_specs=out_specs, check_vma=False
    )
```

```python
import functools
import math

import jax
import jax.numpy as jnp
from jax import lax
from jax.experimental import pallas as pl
from jax.experimental.pallas import tpu as pltpu
from jax.sharding import PartitionSpec as P

LOCAL_QUERY_HEADS = 16
LOCAL_KEY_HEADS = 2
HEAD_SIZE = 128
PIECE = 256
PARTS = 2

epsilon = 1e-06
masked_score = -1e30
F32 = jnp.float32
BF16 = jnp.bfloat16
VMEM_LIMIT = 60 << 20


def dot(a, b, contract=((1,), (0,))):
    return lax.dot_general(a, b, (contract, ((), ())), preferred_element_type=F32)


def iota(shape, dim):
    return lax.broadcasted_iota(jnp.int32, shape, dim)


def slots_row(ids_row, capacity):
    n = ids_row.shape[1]
    names = iota((16, n), 0).astype(F32)
    chosen = names == ids_row
    before = (iota((n, n), 0) < iota((n, n), 1)).astype(F32).astype(BF16)
    earlier = dot(jnp.where(chosen, 1.0, 0.0).astype(BF16), before)
    return jnp.sum(jnp.where(chosen, earlier + names * capacity, 0.0), axis=0, keepdims=True)


def slots_column(ids_column, capacity):
    n = ids_column.shape[0]
    names = iota((n, 128), 1).astype(F32)
    chosen = names == ids_column
    before = (iota((n, n), 1) < iota((n, n), 0)).astype(F32).astype(BF16)
    earlier = dot(before, jnp.where(chosen, 1.0, 0.0).astype(BF16))
    return jnp.sum(jnp.where(chosen, earlier + names * capacity, 0.0), axis=1, keepdims=True)


def one_hot(matches):
    return jnp.where(matches, 1.0, 0.0).astype(BF16)


def shifted_slots(position, owner, experts, capacity):
    expert = jnp.bitwise_xor(position // capacity, owner)
    return (expert * capacity + lax.rem(position, capacity)).astype(F32)


def kernel_params():
    return pltpu.CompilerParams(vmem_limit_bytes=VMEM_LIMIT)


def brief():
    return pl.CostEstimate(flops=1000, bytes_accessed=1000, transcendentals=0)


def whole(*shape):
    return pl.BlockSpec(shape, lambda *_: (0,) * len(shape))


def route_rows(route, n):
    last = route.shape[0] // 16 - 1
    return pl.BlockSpec((16, n), lambda *_: (last, 0))


def smem():
    return pl.BlockSpec(memory_space=pltpu.SMEM)


def attend_kernel(experts, capacity, heads, n_ctx, where_ref, q_ref, *refs):
    route_refs, refs = refs[:experts], refs[experts:]
    count = n_ctx // 2 + 1
    *chips, cores = refs[:count]
    refs = refs[count:]
    blocks = []
    for j, chip in enumerate(chips):
        blocks += [chip, cores.at[j]]
    out_refs, refs = refs[: experts * PARTS], refs[experts * PARTS :]
    k_scr, v_scr, best_scr, acc_scr, att_scr, ids_scr = refs
    ctx, owner = where_ref[0], where_ref[1]
    seq = pl.program_id(0)
    block = q_ref.shape[1]
    tile = 2 * block
    factor = math.log2(math.e) / math.sqrt(HEAD_SIZE)

    @pl.when(seq == 0)
    def _():
        v_scr[:, :, HEAD_SIZE:] = jnp.ones((n_ctx, block, HEAD_SIZE), BF16)
        for d, ref in enumerate(route_refs):
            ids_scr[d] = ref[...].astype(F32)[0:1]

    for m in range(n_ctx):
        index = jnp.bitwise_xor(ctx, m)
        k_scr[index] = blocks[m][0, :, :HEAD_SIZE]
        v_scr[index, :, :HEAD_SIZE] = blocks[m][0, :, HEAD_SIZE:]

    def fold(t, last):
        key_tile = k_scr[pl.ds(2 * t, 2)].reshape(tile, HEAD_SIZE)
        value_tile = v_scr[pl.ds(2 * t, 2)].reshape(tile, 2 * HEAD_SIZE)
        for h in range(heads):
            q = q_ref[0, :, h * HEAD_SIZE : (h + 1) * HEAD_SIZE]
            s = dot(q, key_tile, ((1,), (1,)))
            if last:
                key_pos = iota((block, tile), 1) + t * tile
                query_pos = iota((block, tile), 0) + ctx * block
                s = jnp.where(key_pos <= query_pos, s, masked_score)
            best = jnp.max(s, axis=1, keepdims=True)
            if not last:
                old = best_scr[h]
                best = jnp.maximum(old, best)
            p = jnp.exp2((s - best) * factor)
            blended = dot(p.astype(BF16), value_tile)
            if last:
                acc_scr[h] = blended
            else:
                acc_scr[h] = acc_scr[h] * jnp.exp2((old - best) * factor) + blended
            best_scr[h] = best

    fold(ctx // 2, True)

    @pl.loop(0, ctx // 2)
    def _(t):
        fold(t, False)

    for h in range(heads):
        acc = acc_scr[h]
        att = acc[:, :HEAD_SIZE] / acc[:, HEAD_SIZE:]
        att_scr[:, h * HEAD_SIZE : (h + 1) * HEAD_SIZE] = att.astype(BF16)

    n = ids_scr.shape[2]
    part = capacity // PARTS
    per_seq = block // n
    position = iota((experts * capacity, n), 0)
    slots = shifted_slots(position, owner, experts, capacity)
    for b in range(per_seq):
        source = seq * per_seq + b
        target = slots_row(ids_scr[jnp.bitwise_xor(owner, source)], capacity)
        picked = dot(one_hot(slots == target), att_scr[b * n : (b + 1) * n, :]).astype(BF16)
        for d in range(experts):
            rank = jnp.bitwise_xor(jnp.bitwise_xor(owner, d), source)
            for c in range(PARTS):
                first = d * capacity + c * part
                out_refs[c * experts + d][rank] = picked[first : first + part]


def attend(where, queries, key_values, routes, n, capacity):
    seqs, block, width = queries.shape
    n_ctx = 2 * (len(key_values) - 1)
    experts = len(routes)
    heads = width // HEAD_SIZE
    part = capacity // PARTS
    by_seq = pl.BlockSpec((1, block, 2 * HEAD_SIZE), lambda s: (s, 0, 0))
    outs = pl.pallas_call(
        functools.partial(attend_kernel, experts, capacity, heads, n_ctx),
        grid=(seqs,),
        in_specs=[
            smem(),
            pl.BlockSpec((1, block, width), lambda s: (s, 0, 0)),
        ]
        + [route_rows(x, n) for x in routes]
        + [by_seq] * (len(key_values) - 1)
        + [pl.BlockSpec((n_ctx // 2, 1, block, 2 * HEAD_SIZE), lambda s: (0, s, 0, 0))],
        out_specs=[whole(experts, part, width)] * (PARTS * experts),
        scratch_shapes=[
            pltpu.VMEM((n_ctx, block, HEAD_SIZE), BF16),
            pltpu.VMEM((n_ctx, block, 2 * HEAD_SIZE), BF16),
            pltpu.VMEM((heads, block, 1), F32),
            pltpu.VMEM((heads, block, 2 * HEAD_SIZE), F32),
            pltpu.VMEM((block, width), BF16),
            pltpu.VMEM((experts, 1, n), F32),
        ],
        out_shape=[jax.ShapeDtypeStruct((experts, part, width), BF16)] * (PARTS * experts),
        compiler_params=kernel_params(),
        cost_estimate=brief(),
        name="attend",
    )(where, queries, *routes, *key_values)
    return [outs[c * experts : (c + 1) * experts] for c in range(PARTS)]


def place_kernel(capacity, ids_ref, rows_ref, out_ref, pick_scr):
    @pl.when(pl.program_id(0) == 0)
    def _():
        position = iota(pick_scr.shape, 0)
        pick_scr[...] = one_hot(position.astype(F32) == slots_row(ids_ref[...], capacity))

    out_ref[...] = dot(pick_scr[...], rows_ref[...]).astype(BF16).reshape(out_ref.shape)


def place(ids_row, rows, experts, capacity):
    n, width = rows.shape
    cols = min(width, 1024)
    return pl.pallas_call(
        functools.partial(place_kernel, capacity),
        grid=(width // cols,),
        in_specs=[whole(1, n), pl.BlockSpec((n, cols), lambda i: (0, i))],
        out_specs=pl.BlockSpec((experts, capacity, cols), lambda i: (0, 0, i)),
        out_shape=jax.ShapeDtypeStruct((experts, capacity, width), BF16),
        scratch_shapes=[pltpu.VMEM((experts * capacity, n), BF16)],
        compiler_params=kernel_params(),
        cost_estimate=brief(),
        name="place",
    )(ids_row, rows)


def restore_kernel(experts, capacity, tiles, where_ref, ids_ref, *refs):
    *parts, layer_ref, grad_ref, pick_scr = refs
    step = pl.program_id(0)

    @pl.when(step == 0)
    def _():
        slots = shifted_slots(iota(pick_scr.shape, 1), where_ref[1], experts, capacity)
        pick_scr[...] = one_hot(slots == slots_column(ids_ref[...], capacity))

    def rows(early, late):
        both = [ref[...] for pair in zip(early, late) for ref in pair]
        return dot(pick_scr[...], jnp.concatenate(both, axis=0)).astype(BF16)

    layer_a, change_a, now = [parts[i * experts : (i + 1) * experts] for i in range(3)]

    @pl.when(step < tiles)
    def _():
        layer_ref[...] = rows(layer_a, now)

    @pl.when(step >= tiles)
    def _():
        grad_ref[...] = rows(change_a, now)


def restore(where, ids_column, layer_a, change_a, packed, experts, capacity):
    n = ids_column.shape[0]
    part, width = layer_a[0].shape
    cols = min(width, 1024)
    tiles = width // cols
    first = lambda i: (0, jnp.minimum(i, tiles - 1))
    second = lambda i: (0, jnp.maximum(i - tiles, 0))
    block = lambda at: [pl.BlockSpec((part, cols), at)] * experts
    return pl.pallas_call(
        functools.partial(restore_kernel, experts, capacity, tiles),
        grid=(2 * tiles,),
        in_specs=[smem(), whole(n, 1)] + block(first) + block(second) + block(lambda i: (0, i)),
        out_specs=[pl.BlockSpec((n, cols), first), pl.BlockSpec((n, cols), second)],
        out_shape=[jax.ShapeDtypeStruct((n, width), BF16)] * 2,
        scratch_shapes=[pltpu.VMEM((n, experts * capacity), BF16)],
        compiler_params=kernel_params(),
        cost_estimate=brief(),
        name="restore",
    )(where, ids_column, *layer_a, *change_a, *packed)


def expert_kernel(pieces, experts, capacity, part_index, swap, where_ref, *refs):
    att_refs, refs = refs[:experts], refs[experts:]
    grad_ref, refs = refs[0], refs[1:]
    width_of = grad_ref.shape[2]
    own_ref, refs = refs[0], refs[1:]
    same_hbms, refs = refs[: pieces // 2], refs[pieces // 2 :]
    other_hbm, gate_hbm, up_hbm, down_hbm, gain_ref = refs[:5]
    route_refs, refs = refs[5 : 5 + experts], refs[5 + experts :]
    if part_index == 0:
        layer_refs, refs = refs[:experts], refs[experts:]
        change_refs, refs = refs[:experts], refs[experts:]
    else:
        packed_refs, refs = refs[:experts], refs[experts:]
        layer_refs = [ref.at[:, :width_of] for ref in packed_refs]
        change_refs = [ref.at[:, width_of:] for ref in packed_refs]
    saved_refs, refs = refs[: 1 + swap], refs[1 + swap :]
    w_scr, gate_scr, up_scr, down_scr, hidden_scr, normed_ref, back_ref, back_in_scr, sems = refs
    _, part, width = grad_ref.shape
    rows = experts * part
    att_cols = att_refs[0].shape[-1]
    piece = w_scr.shape[3]
    ff = gate_scr.shape[1]
    ctx, owner = where_ref[0], where_ref[1]
    sources = [jnp.bitwise_xor(owner, d) for d in range(experts)]
    units_at, gate_at, up_at, normed_at = 0, ff, 2 * ff, 3 * ff

    copies = []
    for q in range(pieces // 2):
        for block in (same_hbms[q], other_hbm.at[q]):
            m = len(copies)
            copies.append(pltpu.make_async_copy(block, w_scr.at[m], sems.at[m]))
    weight_copies = (
        pltpu.make_async_copy(gate_hbm.at[0], gate_scr, sems.at[pieces]),
        pltpu.make_async_copy(up_hbm.at[0], up_scr, sems.at[pieces + 1]),
        pltpu.make_async_copy(down_hbm.at[0], down_scr, sems.at[pieces + 2]),
    )
    for copy in copies:
        copy.start()
    for copy in weight_copies:
        copy.start()

    n = route_refs[0].shape[1]
    weights = []
    for s, source in enumerate(sources):
        route = route_refs[s][...].astype(F32)
        target = slots_row(route[0:1], capacity)
        slot = iota((part, n), 0) + (owner * capacity + part_index * part)
        weights.append(
            jnp.sum(
                jnp.where(slot.astype(F32) == target, route[1:2] + route[2:3] + route[3:4], 0.0),
                axis=1,
                keepdims=True,
            )
        )
        grads = grad_ref[source].astype(F32)
        back_ref[s * part : (s + 1) * part, :] = (weights[s] * grads).astype(BF16)

    for m in range(pieces):
        copies[m].wait()
        column = pl.multiple_of(jnp.bitwise_xor(where_ref[2], m) * piece, piece)
        total = jnp.zeros((rows, piece), F32)
        for d in range(experts):
            block = own_ref[:, pl.ds(column, piece)] if d == 0 else w_scr[m, d - 1, :att_cols]
            total += dot(att_refs[d][...].reshape(rows, att_cols), block)
        hidden_scr[:, pl.ds(column, piece)] = total.astype(BF16)

    squares = jnp.zeros((rows, 1), F32)
    for t in range(0, width, PIECE):
        hidden = hidden_scr[:, t : t + PIECE].astype(F32)
        squares += jnp.sum(hidden * hidden, axis=1, keepdims=True)
    inv = lax.rsqrt(squares / width + epsilon)
    for t in range(0, width, PIECE):
        hidden = hidden_scr[:, t : t + PIECE].astype(F32)
        normed_ref[:, t : t + PIECE] = (hidden * inv * gain_ref[:, t : t + PIECE]).astype(BF16)

    for copy in weight_copies:
        copy.wait()
    for f in range(0, ff, 256):
        gate_act = dot(normed_ref[...], gate_scr[:, f : f + 256])
        up_act = dot(normed_ref[...], up_scr[:, f : f + 256])
        back_units = dot(back_ref[...], down_scr[f : f + 256, :], ((1,), (1,)))
        sigma = 1.0 / (1.0 + jnp.exp(-gate_act))
        gated = gate_act * sigma
        units = (gated * up_act).astype(BF16)
        back_gate = back_units * up_act * sigma * (1.0 + gate_act * (1.0 - sigma))
        back_gate = back_gate.astype(BF16)
        back_up = (back_units * gated).astype(BF16)
        for ref in saved_refs:
            ref[:, units_at + f : units_at + f + 256] = units
            ref[:, gate_at + f : gate_at + f + 256] = back_gate
            ref[:, up_at + f : up_at + f + 256] = back_up

    saved = saved_refs[0]
    half = width // len(saved_refs)
    for c, ref in enumerate(saved_refs):
        for t in range(half // PIECE):
            if swap:
                column = pl.multiple_of(jnp.bitwise_xor(ctx, 2 * t + c) * PIECE, PIECE)
            else:
                column = t * PIECE
            at = normed_at + t * PIECE
            ref[:, at : at + PIECE] = normed_ref[:, pl.ds(column, PIECE)]
            ref[:, at + half : at + half + PIECE] = back_ref[:, pl.ds(column, PIECE)]

    weight = jnp.concatenate(weights, axis=0)
    moment = jnp.zeros((rows, 1), F32)
    for t in range(0, width, PIECE):
        hidden = hidden_scr[:, t : t + PIECE].astype(F32)
        result = dot(saved[:, units_at:gate_at], down_scr[:, t : t + PIECE])
        layer = (hidden + weight * result.astype(BF16).astype(F32)).astype(BF16)
        for s in range(experts):
            layer_refs[s][:, t : t + PIECE] = layer[s * part : (s + 1) * part]
        back_in = dot(saved[:, gate_at:up_at], gate_scr[t : t + PIECE, :], ((1,), (1,)))
        back_in += dot(saved[:, up_at:normed_at], up_scr[t : t + PIECE, :], ((1,), (1,)))
        back_in = back_in.astype(BF16)
        back_in_scr[:, t : t + PIECE] = back_in
        scaled = back_in.astype(F32) * gain_ref[:, t : t + PIECE]
        moment += jnp.sum(scaled * (hidden * inv), axis=1, keepdims=True)
    moment = moment / width
    for t in range(0, width, PIECE):
        unit = hidden_scr[:, t : t + PIECE].astype(F32) * inv
        scaled = back_in_scr[:, t : t + PIECE].astype(F32) * gain_ref[:, t : t + PIECE]
        change = inv * (scaled - unit * moment)
        for s in range(experts):
            grads = grad_ref[sources[s], :, t : t + PIECE].astype(F32)
            change_refs[s][:, t : t + PIECE] = (
                grads + change[s * part : (s + 1) * part]
            ).astype(BF16)


def expert_part(
    where, att, grads, own, same, other, gate, up, down, gain, routes, n, capacity, swap, index
):
    experts, part, att_cols = att[0].shape
    pieces = 2 * len(same)
    piece = same[0].shape[-1]
    width = grads.shape[2]
    ff = gate.shape[2]
    rows = experts * part
    half = width // 2 if swap else width
    out = lambda *shape: jax.ShapeDtypeStruct(shape, BF16)
    rows_out = [out(part, width)] * (2 * experts) if index == 0 else [out(part, 2 * width)] * experts
    in_hbm = pl.BlockSpec(memory_space=pl.ANY)
    outs = pl.pallas_call(
        functools.partial(expert_kernel, pieces, experts, capacity, index, swap),
        grid=(1,),
        in_specs=[smem()]
        + [whole(*x.shape) for x in att]
        + [pl.BlockSpec((experts, part, width), lambda i: (0, index, 0))]
        + [whole(*own.shape)]
        + [in_hbm] * (len(same) + 4)
        + [whole(1, width)]
        + [route_rows(x, n) for x in routes],
        out_specs=[whole(*x.shape) for x in rows_out]
        + [whole(rows, 3 * ff + 2 * half)] * (1 + swap),
        scratch_shapes=[
            pltpu.VMEM((pieces,) + same[0].shape, BF16),
            pltpu.VMEM((width, ff), BF16),
            pltpu.VMEM((width, ff), BF16),
            pltpu.VMEM((ff, width), BF16),
            pltpu.VMEM((rows, width), BF16),
            pltpu.VMEM((rows, width), BF16),
            pltpu.VMEM((rows, width), BF16),
            pltpu.VMEM((rows, width), BF16),
            pltpu.SemaphoreType.DMA((pieces + 3,)),
        ],
        out_shape=rows_out
        + [out(rows, 3 * ff + 2 * half)] * (1 + swap),
        compiler_params=kernel_params(),
        cost_estimate=brief(),
        name="expert",
    )(where, *att, grads, own, *same, other, gate, up, down, gain, *routes)
    return outs[: len(rows_out)], outs[len(rows_out) :]


def weight_kernel(count, *refs):
    units, back_gate, back_up, normed, back = [refs[i * count : (i + 1) * count] for i in range(5)]
    outs = refs[5 * count :]
    first = ((0,), (0,))

    def total(left, right):
        return sum(dot(a[...], b[...], first) for a, b in zip(left, right)).astype(BF16)

    gate, up, down = total(normed, back_gate), total(normed, back_up), total(units, back)
    cols = down.shape[1]
    part = gate.shape[0] // len(outs)
    for c, ref in enumerate(outs):
        rows = slice(c * part, (c + 1) * part)
        ref[0, 0] = gate[rows]
        ref[0, 1] = up[rows]
        for t in range(0, down.shape[0], cols):
            ref[0, 2, :, t : t + cols] = down[t + c * part : t + (c + 1) * part]


def weight_blocks(saved, blocks, ff, split):
    count = len(saved)
    rows, total = saved[0].shape
    normed_at = 3 * ff // PIECE
    back_at = normed_at + blocks
    thin = lambda at: [pl.BlockSpec((rows, PIECE), lambda i: (0, at + i))] * count
    full = lambda at: [pl.BlockSpec((rows, ff), lambda i: (0, at))] * count
    part = PIECE // 2 if split else PIECE
    shuffled = lambda i: (i % 2 * (blocks // 2) + i // 2, 0, 0, 0)
    plain = lambda i: (i, 0, 0, 0)
    orders = [shuffled, plain] if split else [plain]
    return pl.pallas_call(
        functools.partial(weight_kernel, count),
        grid=(blocks,),
        in_specs=full(0) + full(1) + full(2) + thin(normed_at) + thin(back_at),
        out_specs=[pl.BlockSpec((1, 3, part, ff), order) for order in orders],
        out_shape=[jax.ShapeDtypeStruct((blocks, 3, part, ff), BF16) for _ in orders],
        compiler_params=kernel_params(),
        cost_estimate=brief(),
        name="weight_grads",
    )(*saved * 5)


def partner(value, mask):
    count = lax.axis_size("ctx")
    return lax.ppermute(value, "ctx", [(i, i ^ mask) for i in range(count)])


def to_owner(value, mask):
    count = lax.axis_size("exp")
    return lax.ppermute(value, "exp", [(i, i ^ mask) for i in range(count)])


def to_owners(values):
    return [values[0]] + [to_owner(values[d], d) for d in range(len(values) - 1, 0, -1)][::-1]


def after(value, *others):
    return lax.optimization_barrier((value, others))[0]


def halved(value, bits, order, ctx):
    shape = value.shape[1:]
    held = value.reshape((2,) * bits + shape)
    for place_in_order, bit in enumerate(order):
        axis = bits - 1 - bit
        mine = (ctx >> bit) & 1
        gone = lax.dynamic_slice_in_dim(held, 1 - mine, 1, axis)
        kept = lax.dynamic_slice_in_dim(held, mine, 1, axis)
        held = kept.astype(F32) + partner(gone, 1 << bit).astype(F32)
        if place_in_order < bits - 1:
            held = held.astype(BF16)
    return held.reshape(shape)


def on_device(
    queries,
    rotated_key_heads,
    value_head_rows,
    out_proj,
    norm_gain,
    expert_ids,
    gate_weights,
    expert_gate,
    expert_up,
    expert_down,
    grad_out,
):
    heads_dev = queries.shape[2] // HEAD_SIZE
    group = LOCAL_QUERY_HEADS // LOCAL_KEY_HEADS
    exp_count = lax.axis_size("exp")
    ctx_count = lax.axis_size("ctx")
    owner = lax.axis_index("exp")
    ctx = lax.axis_index("ctx")
    bits = ctx_count.bit_length() - 1
    n, _ = expert_ids.shape
    width = grad_out.shape[1]
    experts = exp_count
    capacity = min(n, 2 * n // experts)
    pieces = min(ctx_count, width // PIECE)
    piece = width // pieces
    piece_index = ctx % pieces
    where = jnp.stack([ctx, owner, piece_index]).astype(jnp.int32)

    ids_f = expert_ids.astype(F32)
    gates = gate_weights[:, 0]
    high = lax.optimization_barrier(gates.astype(BF16))
    middle = lax.optimization_barrier((gates - high.astype(F32)).astype(BF16))
    low = (gates - high.astype(F32) - middle.astype(F32)).astype(BF16)
    info = jnp.stack([ids_f[:, 0].astype(BF16), high, middle, low])
    info = jnp.pad(info, ((0, 12), (0, piece - n)))
    mine = lax.dynamic_slice_in_dim(out_proj, piece_index * piece, piece, 1)
    routes = to_owners([jnp.concatenate([mine, info])] * exp_count)

    first_column = (owner * heads_dev // group) * HEAD_SIZE
    keys = lax.dynamic_slice_in_dim(rotated_key_heads, first_column, HEAD_SIZE, 2)
    values = lax.dynamic_slice_in_dim(value_head_rows, first_column, HEAD_SIZE, 2)
    own = jnp.concatenate([keys, values], axis=2)
    chips = [own] + [partner(own, m) for m in range(2, ctx_count, 2)]

    grads = place(ids_f.reshape(1, n), grad_out, experts, capacity)
    key_values = chips + [partner(after(jnp.stack(chips), routes[1:], grads), 1)]
    grads = lax.all_to_all(grads, "exp", 0, 0, tiled=True)

    projection = after(jnp.stack(routes[1:]), chips)
    same = [projection] + [partner(projection, m) for m in range(2, pieces, 2)]

    sent = attend(where, queries, key_values, routes, n, capacity)
    arrived = to_owners(after(sent[0], grads))
    later = after(sent[1], arrived, same)
    same = after(same, sent[0])
    other = partner(jnp.stack(same), 1)

    rows_dev = width // ctx_count
    ff = expert_gate.shape[2]
    swap = rows_dev == PIECE

    def run(arrived, index):
        return expert_part(
            where,
            arrived,
            grads,
            out_proj,
            same,
            other,
            expert_gate,
            expert_up,
            expert_down,
            norm_gain.reshape(1, width),
            routes,
            n,
            capacity,
            swap,
            index,
        )

    rows_a, saved_a = run(arrived, 0)
    layer_a = to_owners(rows_a[:experts])
    change_a = to_owners(after(rows_a[experts:], layer_a[1]))
    rows_b, saved_b = run(to_owners(later), 1)
    packed = to_owners(rows_b)
    if swap:
        saved = [saved_a[0], partner(saved_a[1], 1)]
        saved += [saved_b[0], partner(after(saved_b[1], layer_a), 1)]
        parts = weight_blocks(saved, ctx_count // 2, ff, True)
        parts = after(parts, change_a)
        half = ctx_count // 4
        masks = (2, 4), (4, 2)
        near = [partner(x[half:], m[0]) for x, m in zip(parts, masks)]
        sums = [x[:half].astype(F32) + y.astype(F32) for x, y in zip(parts, near)]
        gone = [x[1].astype(BF16) for x in sums]
        far = [partner(x, m[1]) for x, m in zip(gone, masks)]
        packed = after(packed, gone)
        total = [x[0] + y.astype(F32) for x, y in zip(sums, far)]
        total = jnp.concatenate(total, axis=1)
        grad_gate, grad_up = total[0][None], total[1][None]
        grad_down = total[2].reshape(PIECE, ff // PIECE, PIECE).transpose(1, 0, 2)
        grad_down = grad_down.reshape(1, ff, PIECE)
    else:
        blocks = width // PIECE
        (parts,) = weight_blocks(list(saved_a) + list(saved_b), blocks, ff, False)
        part_down = parts[:, 2].reshape(blocks, PIECE, ff // PIECE, PIECE).transpose(0, 2, 1, 3)
        part_down = part_down.reshape(blocks, ff, PIECE // rows_dev, rows_dev)
        part_down = part_down.transpose(0, 2, 1, 3).reshape(ctx_count, ff, rows_dev)
        order = list(range(bits))
        grad_gate, grad_up, grad_down = [
            halved(x.reshape((ctx_count,) + shape), bits, order, ctx)[None]
            for x, shape in (
                (parts[:, 0], (rows_dev, ff)),
                (parts[:, 1], (rows_dev, ff)),
                (part_down, (ff, rows_dev)),
            )
        ]
    layer_out, grad_hidden = restore(where, after(ids_f, grad_gate, grad_up, grad_down), layer_a, change_a, packed, experts, capacity)
    return (layer_out, grad_hidden, grad_gate, grad_up, grad_down)


def solution(mesh):
    in_specs = (
        P(None, "ctx", "exp"),
        P(None, "ctx", None),
        P(None, "ctx", None),
        P("exp", None),
        P(),
        P(("ctx", "exp"), None),
        P(("ctx", "exp"), None),
        P("exp", None, None),
        P("exp", None, None),
        P("exp", None, None),
        P(("ctx", "exp"), None),
    )
    out_specs = (
        P(("ctx", "exp"), None),
        P(("ctx", "exp"), None),
        P("exp", "ctx", None),
        P("exp", "ctx", None),
        P("exp", None, "ctx"),
    )
    return jax.shard_map(
        on_device, mesh=mesh, in_specs=in_specs, out_specs=out_specs, check_vma=False
    )
```

```python
import functools
import math

import jax
import jax.numpy as jnp
from jax import lax
from jax.experimental import pallas as pl
from jax.experimental.pallas import tpu as pltpu
from jax.sharding import PartitionSpec as P

LOCAL_QUERY_HEADS = 16
LOCAL_KEY_HEADS = 2
HEAD_SIZE = 128
PIECE = 256
PARTS = 2

epsilon = 1e-06
masked_score = -1e30
F32 = jnp.float32
BF16 = jnp.bfloat16
VMEM_LIMIT = 60 << 20


def dot(a, b, contract=((1,), (0,))):
    return lax.dot_general(a, b, (contract, ((), ())), preferred_element_type=F32)


def iota(shape, dim):
    return lax.broadcasted_iota(jnp.int32, shape, dim)


def slots_row(ids_row, capacity):
    n = ids_row.shape[1]
    names = iota((16, n), 0).astype(F32)
    chosen = names == ids_row
    before = (iota((n, n), 0) < iota((n, n), 1)).astype(F32).astype(BF16)
    earlier = dot(jnp.where(chosen, 1.0, 0.0).astype(BF16), before)
    return jnp.sum(jnp.where(chosen, earlier + names * capacity, 0.0), axis=0, keepdims=True)


def slots_column(ids_column, capacity):
    n = ids_column.shape[0]
    names = iota((n, 128), 1).astype(F32)
    chosen = names == ids_column
    before = (iota((n, n), 1) < iota((n, n), 0)).astype(F32).astype(BF16)
    earlier = dot(before, jnp.where(chosen, 1.0, 0.0).astype(BF16))
    return jnp.sum(jnp.where(chosen, earlier + names * capacity, 0.0), axis=1, keepdims=True)


def one_hot(matches):
    return jnp.where(matches, 1.0, 0.0).astype(BF16)


def shifted_slots(position, owner, experts, capacity):
    expert = jnp.bitwise_xor(position // capacity, owner)
    return (expert * capacity + lax.rem(position, capacity)).astype(F32)


def kernel_params():
    return pltpu.CompilerParams(vmem_limit_bytes=VMEM_LIMIT)


def brief():
    return pl.CostEstimate(flops=1000, bytes_accessed=1000, transcendentals=0)


def whole(*shape):
    return pl.BlockSpec(shape, lambda *_: (0,) * len(shape))


def route_rows(route, n):
    last = route.shape[0] // 16 - 1
    return pl.BlockSpec((16, n), lambda *_: (last, 0))


def smem():
    return pl.BlockSpec(memory_space=pltpu.SMEM)


def attend_kernel(experts, capacity, heads, n_ctx, where_ref, q_ref, *refs):
    route_refs, refs = refs[:experts], refs[experts:]
    count = n_ctx // 2 + 1
    *chips, cores = refs[:count]
    refs = refs[count:]
    blocks = []
    for j, chip in enumerate(chips):
        blocks += [chip, cores.at[j]]
    out_refs, refs = refs[: experts * PARTS], refs[experts * PARTS :]
    k_scr, v_scr, best_scr, acc_scr, att_scr, ids_scr = refs
    ctx, owner = where_ref[0], where_ref[1]
    seq = pl.program_id(0)
    block = q_ref.shape[1]
    tile = 2 * block
    factor = math.log2(math.e) / math.sqrt(HEAD_SIZE)

    @pl.when(seq == 0)
    def _():
        v_scr[:, :, HEAD_SIZE:] = jnp.ones((n_ctx, block, HEAD_SIZE), BF16)
        for d, ref in enumerate(route_refs):
            ids_scr[d] = ref[...].astype(F32)[0:1]

    for m in range(n_ctx):
        index = jnp.bitwise_xor(ctx, m)
        k_scr[index] = blocks[m][0, :, :HEAD_SIZE]
        v_scr[index, :, :HEAD_SIZE] = blocks[m][0, :, HEAD_SIZE:]

    def fold(t, last):
        key_tile = k_scr[pl.ds(2 * t, 2)].reshape(tile, HEAD_SIZE)
        value_tile = v_scr[pl.ds(2 * t, 2)].reshape(tile, 2 * HEAD_SIZE)
        for h in range(heads):
            q = q_ref[0, :, h * HEAD_SIZE : (h + 1) * HEAD_SIZE]
            s = dot(q, key_tile, ((1,), (1,)))
            if last:
                key_pos = iota((block, tile), 1) + t * tile
                query_pos = iota((block, tile), 0) + ctx * block
                s = jnp.where(key_pos <= query_pos, s, masked_score)
            best = jnp.max(s, axis=1, keepdims=True)
            if not last:
                old = best_scr[h]
                best = jnp.maximum(old, best)
            p = jnp.exp2((s - best) * factor)
            blended = dot(p.astype(BF16), value_tile)
            if last:
                acc_scr[h] = blended
            else:
                acc_scr[h] = acc_scr[h] * jnp.exp2((old - best) * factor) + blended
            best_scr[h] = best

    fold(ctx // 2, True)

    @pl.loop(0, ctx // 2)
    def _(t):
        fold(t, False)

    for h in range(heads):
        acc = acc_scr[h]
        att = acc[:, :HEAD_SIZE] / acc[:, HEAD_SIZE:]
        att_scr[:, h * HEAD_SIZE : (h + 1) * HEAD_SIZE] = att.astype(BF16)

    n = ids_scr.shape[2]
    part = capacity // PARTS
    per_seq = block // n
    position = iota((experts * capacity, n), 0)
    slots = shifted_slots(position, owner, experts, capacity)
    for b in range(per_seq):
        source = seq * per_seq + b
        target = slots_row(ids_scr[jnp.bitwise_xor(owner, source)], capacity)
        picked = dot(one_hot(slots == target), att_scr[b * n : (b + 1) * n, :]).astype(BF16)
        for d in range(experts):
            rank = jnp.bitwise_xor(jnp.bitwise_xor(owner, d), source)
            for c in range(PARTS):
                first = d * capacity + c * part
                out_refs[c * experts + d][rank] = picked[first : first + part]


def attend(where, queries, key_values, routes, n, capacity):
    seqs, block, width = queries.shape
    n_ctx = 2 * (len(key_values) - 1)
    experts = len(routes)
    heads = width // HEAD_SIZE
    part = capacity // PARTS
    by_seq = pl.BlockSpec((1, block, 2 * HEAD_SIZE), lambda s: (s, 0, 0))
    outs = pl.pallas_call(
        functools.partial(attend_kernel, experts, capacity, heads, n_ctx),
        grid=(seqs,),
        in_specs=[
            smem(),
            pl.BlockSpec((1, block, width), lambda s: (s, 0, 0)),
        ]
        + [route_rows(x, n) for x in routes]
        + [by_seq] * (len(key_values) - 1)
        + [pl.BlockSpec((n_ctx // 2, 1, block, 2 * HEAD_SIZE), lambda s: (0, s, 0, 0))],
        out_specs=[whole(experts, part, width)] * (PARTS * experts),
        scratch_shapes=[
            pltpu.VMEM((n_ctx, block, HEAD_SIZE), BF16),
            pltpu.VMEM((n_ctx, block, 2 * HEAD_SIZE), BF16),
            pltpu.VMEM((heads, block, 1), F32),
            pltpu.VMEM((heads, block, 2 * HEAD_SIZE), F32),
            pltpu.VMEM((block, width), BF16),
            pltpu.VMEM((experts, 1, n), F32),
        ],
        out_shape=[jax.ShapeDtypeStruct((experts, part, width), BF16)] * (PARTS * experts),
        compiler_params=kernel_params(),
        cost_estimate=brief(),
        name="attend",
    )(where, queries, *routes, *key_values)
    return [outs[c * experts : (c + 1) * experts] for c in range(PARTS)]


def place_kernel(capacity, ids_ref, rows_ref, out_ref, pick_scr):
    @pl.when(pl.program_id(0) == 0)
    def _():
        position = iota(pick_scr.shape, 0)
        pick_scr[...] = one_hot(position.astype(F32) == slots_row(ids_ref[...], capacity))

    out_ref[...] = dot(pick_scr[...], rows_ref[...]).astype(BF16).reshape(out_ref.shape)


def place(ids_row, rows, experts, capacity):
    n, width = rows.shape
    cols = min(width, 1024)
    return pl.pallas_call(
        functools.partial(place_kernel, capacity),
        grid=(width // cols,),
        in_specs=[whole(1, n), pl.BlockSpec((n, cols), lambda i: (0, i))],
        out_specs=pl.BlockSpec((experts, capacity, cols), lambda i: (0, 0, i)),
        out_shape=jax.ShapeDtypeStruct((experts, capacity, width), BF16),
        scratch_shapes=[pltpu.VMEM((experts * capacity, n), BF16)],
        compiler_params=kernel_params(),
        cost_estimate=brief(),
        name="place",
    )(ids_row, rows)


def restore_kernel(experts, capacity, tiles, where_ref, ids_ref, *refs):
    *parts, layer_ref, grad_ref, pick_scr = refs
    step = pl.program_id(0)

    @pl.when(step == 0)
    def _():
        slots = shifted_slots(iota(pick_scr.shape, 1), where_ref[1], experts, capacity)
        pick_scr[...] = one_hot(slots == slots_column(ids_ref[...], capacity))

    def rows(early, late):
        both = [ref[...] for pair in zip(early, late) for ref in pair]
        return dot(pick_scr[...], jnp.concatenate(both, axis=0)).astype(BF16)

    layer_a, change_a, now = [parts[i * experts : (i + 1) * experts] for i in range(3)]

    @pl.when(step < tiles)
    def _():
        layer_ref[...] = rows(layer_a, now)

    @pl.when(step >= tiles)
    def _():
        grad_ref[...] = rows(change_a, now)


def restore(where, ids_column, layer_a, change_a, packed, experts, capacity):
    n = ids_column.shape[0]
    part, width = layer_a[0].shape
    cols = min(width, 1024)
    tiles = width // cols
    first = lambda i: (0, jnp.minimum(i, tiles - 1))
    second = lambda i: (0, jnp.maximum(i - tiles, 0))
    block = lambda at: [pl.BlockSpec((part, cols), at)] * experts
    return pl.pallas_call(
        functools.partial(restore_kernel, experts, capacity, tiles),
        grid=(2 * tiles,),
        in_specs=[smem(), whole(n, 1)] + block(first) + block(second) + block(lambda i: (0, i)),
        out_specs=[pl.BlockSpec((n, cols), first), pl.BlockSpec((n, cols), second)],
        out_shape=[jax.ShapeDtypeStruct((n, width), BF16)] * 2,
        scratch_shapes=[pltpu.VMEM((n, experts * capacity), BF16)],
        compiler_params=kernel_params(),
        cost_estimate=brief(),
        name="restore",
    )(where, ids_column, *layer_a, *change_a, *packed)


def expert_kernel(pieces, experts, capacity, part_index, swap, where_ref, *refs):
    att_refs, refs = refs[:experts], refs[experts:]
    grad_ref, refs = refs[0], refs[1:]
    width_of = grad_ref.shape[2]
    own_ref, refs = refs[0], refs[1:]
    same_hbms, refs = refs[: pieces // 2], refs[pieces // 2 :]
    other_hbm, gate_hbm, up_hbm, down_hbm, gain_ref = refs[:5]
    route_refs, refs = refs[5 : 5 + experts], refs[5 + experts :]
    if part_index == 0:
        layer_refs, refs = refs[:experts], refs[experts:]
        change_refs, refs = refs[:experts], refs[experts:]
    else:
        packed_refs, refs = refs[:experts], refs[experts:]
        layer_refs = [ref.at[:, :width_of] for ref in packed_refs]
        change_refs = [ref.at[:, width_of:] for ref in packed_refs]
    saved_refs, refs = refs[: 1 + swap], refs[1 + swap :]
    w_scr, gate_scr, up_scr, down_scr, hidden_scr, normed_ref, back_ref, back_in_scr, sems = refs
    _, part, width = grad_ref.shape
    rows = experts * part
    att_cols = att_refs[0].shape[-1]
    piece = w_scr.shape[3]
    ff = gate_scr.shape[1]
    ctx, owner = where_ref[0], where_ref[1]
    sources = [jnp.bitwise_xor(owner, d) for d in range(experts)]
    units_at, gate_at, up_at, normed_at = 0, ff, 2 * ff, 3 * ff

    copies = []
    for q in range(pieces // 2):
        for block in (same_hbms[q], other_hbm.at[q]):
            m = len(copies)
            copies.append(pltpu.make_async_copy(block, w_scr.at[m], sems.at[m]))
    weight_copies = (
        pltpu.make_async_copy(gate_hbm.at[0], gate_scr, sems.at[pieces]),
        pltpu.make_async_copy(up_hbm.at[0], up_scr, sems.at[pieces + 1]),
        pltpu.make_async_copy(down_hbm.at[0], down_scr, sems.at[pieces + 2]),
    )
    for copy in copies:
        copy.start()
    for copy in weight_copies:
        copy.start()

    n = route_refs[0].shape[1]
    weights = []
    for s, source in enumerate(sources):
        route = route_refs[s][...].astype(F32)
        target = slots_row(route[0:1], capacity)
        slot = iota((part, n), 0) + (owner * capacity + part_index * part)
        weights.append(
            jnp.sum(
                jnp.where(slot.astype(F32) == target, route[1:2] + route[2:3] + route[3:4], 0.0),
                axis=1,
                keepdims=True,
            )
        )
        grads = grad_ref[source].astype(F32)
        back_ref[s * part : (s + 1) * part, :] = (weights[s] * grads).astype(BF16)

    for m in range(pieces):
        copies[m].wait()
        column = pl.multiple_of(jnp.bitwise_xor(where_ref[2], m) * piece, piece)
        total = jnp.zeros((rows, piece), F32)
        for d in range(experts):
            block = own_ref[:, pl.ds(column, piece)] if d == 0 else w_scr[m, d - 1, :att_cols]
            total += dot(att_refs[d][...].reshape(rows, att_cols), block)
        hidden_scr[:, pl.ds(column, piece)] = total.astype(BF16)

    squares = jnp.zeros((rows, 1), F32)
    for t in range(0, width, PIECE):
        hidden = hidden_scr[:, t : t + PIECE].astype(F32)
        squares += jnp.sum(hidden * hidden, axis=1, keepdims=True)
    inv = lax.rsqrt(squares / width + epsilon)
    for t in range(0, width, PIECE):
        hidden = hidden_scr[:, t : t + PIECE].astype(F32)
        normed_ref[:, t : t + PIECE] = (hidden * inv * gain_ref[:, t : t + PIECE]).astype(BF16)

    for copy in weight_copies:
        copy.wait()
    for f in range(0, ff, 256):
        gate_act = dot(normed_ref[...], gate_scr[:, f : f + 256])
        up_act = dot(normed_ref[...], up_scr[:, f : f + 256])
        back_units = dot(back_ref[...], down_scr[f : f + 256, :], ((1,), (1,)))
        sigma = 1.0 / (1.0 + jnp.exp(-gate_act))
        gated = gate_act * sigma
        units = (gated * up_act).astype(BF16)
        back_gate = back_units * up_act * sigma * (1.0 + gate_act * (1.0 - sigma))
        back_gate = back_gate.astype(BF16)
        back_up = (back_units * gated).astype(BF16)
        for ref in saved_refs:
            ref[:, units_at + f : units_at + f + 256] = units
            ref[:, gate_at + f : gate_at + f + 256] = back_gate
            ref[:, up_at + f : up_at + f + 256] = back_up

    saved = saved_refs[0]
    half = width // len(saved_refs)
    for c, ref in enumerate(saved_refs):
        for t in range(half // PIECE):
            if swap:
                column = pl.multiple_of(jnp.bitwise_xor(ctx, 2 * t + c) * PIECE, PIECE)
            else:
                column = t * PIECE
            at = normed_at + t * PIECE
            ref[:, at : at + PIECE] = normed_ref[:, pl.ds(column, PIECE)]
            ref[:, at + half : at + half + PIECE] = back_ref[:, pl.ds(column, PIECE)]

    weight = jnp.concatenate(weights, axis=0)
    moment = jnp.zeros((rows, 1), F32)
    for t in range(0, width, PIECE):
        hidden = hidden_scr[:, t : t + PIECE].astype(F32)
        result = dot(saved[:, units_at:gate_at], down_scr[:, t : t + PIECE])
        layer = (hidden + weight * result.astype(BF16).astype(F32)).astype(BF16)
        for s in range(experts):
            layer_refs[s][:, t : t + PIECE] = layer[s * part : (s + 1) * part]
        back_in = dot(saved[:, gate_at:up_at], gate_scr[t : t + PIECE, :], ((1,), (1,)))
        back_in += dot(saved[:, up_at:normed_at], up_scr[t : t + PIECE, :], ((1,), (1,)))
        back_in = back_in.astype(BF16)
        back_in_scr[:, t : t + PIECE] = back_in
        scaled = back_in.astype(F32) * gain_ref[:, t : t + PIECE]
        moment += jnp.sum(scaled * (hidden * inv), axis=1, keepdims=True)
    moment = moment / width
    for t in range(0, width, PIECE):
        unit = hidden_scr[:, t : t + PIECE].astype(F32) * inv
        scaled = back_in_scr[:, t : t + PIECE].astype(F32) * gain_ref[:, t : t + PIECE]
        change = inv * (scaled - unit * moment)
        for s in range(experts):
            grads = grad_ref[sources[s], :, t : t + PIECE].astype(F32)
            change_refs[s][:, t : t + PIECE] = (
                grads + change[s * part : (s + 1) * part]
            ).astype(BF16)


def expert_part(
    where, att, grads, own, same, other, gate, up, down, gain, routes, n, capacity, swap, index
):
    experts, part, att_cols = att[0].shape
    pieces = 2 * len(same)
    piece = same[0].shape[-1]
    width = grads.shape[2]
    ff = gate.shape[2]
    rows = experts * part
    half = width // 2 if swap else width
    out = lambda *shape: jax.ShapeDtypeStruct(shape, BF16)
    rows_out = [out(part, width)] * (2 * experts) if index == 0 else [out(part, 2 * width)] * experts
    in_hbm = pl.BlockSpec(memory_space=pl.ANY)
    outs = pl.pallas_call(
        functools.partial(expert_kernel, pieces, experts, capacity, index, swap),
        grid=(1,),
        in_specs=[smem()]
        + [whole(*x.shape) for x in att]
        + [pl.BlockSpec((experts, part, width), lambda i: (0, index, 0))]
        + [whole(*own.shape)]
        + [in_hbm] * (len(same) + 4)
        + [whole(1, width)]
        + [route_rows(x, n) for x in routes],
        out_specs=[whole(*x.shape) for x in rows_out]
        + [whole(rows, 3 * ff + 2 * half)] * (1 + swap),
        scratch_shapes=[
            pltpu.VMEM((pieces,) + same[0].shape, BF16),
            pltpu.VMEM((width, ff), BF16),
            pltpu.VMEM((width, ff), BF16),
            pltpu.VMEM((ff, width), BF16),
            pltpu.VMEM((rows, width), BF16),
            pltpu.VMEM((rows, width), BF16),
            pltpu.VMEM((rows, width), BF16),
            pltpu.VMEM((rows, width), BF16),
            pltpu.SemaphoreType.DMA((pieces + 3,)),
        ],
        out_shape=rows_out
        + [out(rows, 3 * ff + 2 * half)] * (1 + swap),
        compiler_params=kernel_params(),
        cost_estimate=brief(),
        name="expert",
    )(where, *att, grads, own, *same, other, gate, up, down, gain, *routes)
    return outs[: len(rows_out)], outs[len(rows_out) :]


def weight_kernel(count, *refs):
    units, back_gate, back_up, normed, back = [refs[i * count : (i + 1) * count] for i in range(5)]
    outs = refs[5 * count :]
    first = ((0,), (0,))

    def total(left, right):
        return sum(dot(a[...], b[...], first) for a, b in zip(left, right)).astype(BF16)

    gate, up, down = total(normed, back_gate), total(normed, back_up), total(units, back)
    cols = down.shape[1]
    part = gate.shape[0] // len(outs)
    for c, ref in enumerate(outs):
        rows = slice(c * part, (c + 1) * part)
        ref[0, 0] = gate[rows]
        ref[0, 1] = up[rows]
        for t in range(0, down.shape[0], cols):
            ref[0, 2, :, t : t + cols] = down[t + c * part : t + (c + 1) * part]


def weight_blocks(saved, blocks, ff, split):
    count = len(saved)
    rows, total = saved[0].shape
    normed_at = 3 * ff // PIECE
    back_at = normed_at + blocks
    thin = lambda at: [pl.BlockSpec((rows, PIECE), lambda i: (0, at + i))] * count
    full = lambda at: [pl.BlockSpec((rows, ff), lambda i: (0, at))] * count
    part = PIECE // 2 if split else PIECE
    shuffled = lambda i: (i % 2 * (blocks // 2) + i // 2, 0, 0, 0)
    plain = lambda i: (i, 0, 0, 0)
    orders = [shuffled, plain] if split else [plain]
    return pl.pallas_call(
        functools.partial(weight_kernel, count),
        grid=(blocks,),
        in_specs=full(0) + full(1) + full(2) + thin(normed_at) + thin(back_at),
        out_specs=[pl.BlockSpec((1, 3, part, ff), order) for order in orders],
        out_shape=[jax.ShapeDtypeStruct((blocks, 3, part, ff), BF16) for _ in orders],
        compiler_params=kernel_params(),
        cost_estimate=brief(),
        name="weight_grads",
    )(*saved * 5)


def partner(value, mask):
    count = lax.axis_size("ctx")
    return lax.ppermute(value, "ctx", [(i, i ^ mask) for i in range(count)])


def to_owner(value, mask):
    count = lax.axis_size("exp")
    return lax.ppermute(value, "exp", [(i, i ^ mask) for i in range(count)])


def to_owners(values):
    return [values[0]] + [to_owner(values[d], d) for d in range(len(values) - 1, 0, -1)][::-1]


def after(value, *others):
    return lax.optimization_barrier((value, others))[0]


def halved(value, bits, order, ctx):
    shape = value.shape[1:]
    held = value.reshape((2,) * bits + shape)
    for place_in_order, bit in enumerate(order):
        axis = bits - 1 - bit
        mine = (ctx >> bit) & 1
        gone = lax.dynamic_slice_in_dim(held, 1 - mine, 1, axis)
        kept = lax.dynamic_slice_in_dim(held, mine, 1, axis)
        held = kept.astype(F32) + partner(gone, 1 << bit).astype(F32)
        if place_in_order < bits - 1:
            held = held.astype(BF16)
    return held.reshape(shape)


def on_device(
    queries,
    rotated_key_heads,
    value_head_rows,
    out_proj,
    norm_gain,
    expert_ids,
    gate_weights,
    expert_gate,
    expert_up,
    expert_down,
    grad_out,
):
    heads_dev = queries.shape[2] // HEAD_SIZE
    group = LOCAL_QUERY_HEADS // LOCAL_KEY_HEADS
    exp_count = lax.axis_size("exp")
    ctx_count = lax.axis_size("ctx")
    owner = lax.axis_index("exp")
    ctx = lax.axis_index("ctx")
    bits = ctx_count.bit_length() - 1
    n, _ = expert_ids.shape
    width = grad_out.shape[1]
    experts = exp_count
    capacity = min(n, 2 * n // experts)
    pieces = min(ctx_count, width // PIECE)
    piece = width // pieces
    piece_index = ctx % pieces
    where = jnp.stack([ctx, owner, piece_index]).astype(jnp.int32)

    ids_f = expert_ids.astype(F32)
    gates = gate_weights[:, 0]
    high = lax.optimization_barrier(gates.astype(BF16))
    middle = lax.optimization_barrier((gates - high.astype(F32)).astype(BF16))
    low = (gates - high.astype(F32) - middle.astype(F32)).astype(BF16)
    info = jnp.stack([ids_f[:, 0].astype(BF16), high, middle, low])
    info = jnp.pad(info, ((0, 12), (0, piece - n)))
    mine = lax.dynamic_slice_in_dim(out_proj, piece_index * piece, piece, 1)
    routes = to_owners([jnp.concatenate([mine, info])] * exp_count)

    first_column = (owner * heads_dev // group) * HEAD_SIZE
    keys = lax.dynamic_slice_in_dim(rotated_key_heads, first_column, HEAD_SIZE, 2)
    values = lax.dynamic_slice_in_dim(value_head_rows, first_column, HEAD_SIZE, 2)
    own = jnp.concatenate([keys, values], axis=2)
    chips = [own] + [partner(own, m) for m in range(2, ctx_count, 2)]

    grads = place(ids_f.reshape(1, n), grad_out, experts, capacity)
    key_values = chips + [partner(after(jnp.stack(chips), routes[1:], grads), 1)]
    grads = lax.all_to_all(grads, "exp", 0, 0, tiled=True)

    projection = after(jnp.stack(routes[1:]), chips)
    same = [projection] + [partner(projection, m) for m in range(2, pieces, 2)]

    sent = attend(where, queries, key_values, routes, n, capacity)
    arrived = to_owners(after(sent[0], grads))
    later = after(sent[1], arrived, same)
    same = after(same, sent[0], grads)
    other = partner(jnp.stack(same), 1)

    rows_dev = width // ctx_count
    ff = expert_gate.shape[2]
    swap = rows_dev == PIECE

    def run(arrived, index):
        return expert_part(
            where,
            arrived,
            grads,
            out_proj,
            same,
            other,
            expert_gate,
            expert_up,
            expert_down,
            norm_gain.reshape(1, width),
            routes,
            n,
            capacity,
            swap,
            index,
        )

    rows_a, saved_a = run(arrived, 0)
    layer_a = to_owners(rows_a[:experts])
    change_a = to_owners(after(rows_a[experts:], layer_a[1]))
    rows_b, saved_b = run(to_owners(later), 1)
    packed = to_owners(rows_b)
    if swap:
        saved = [saved_a[0], partner(saved_a[1], 1)]
        saved += [saved_b[0], partner(after(saved_b[1], layer_a), 1)]
        parts = weight_blocks(saved, ctx_count // 2, ff, True)
        parts = after(parts, change_a)
        half = ctx_count // 4
        masks = (2, 4), (4, 2)
        near = [partner(x[half:], m[0]) for x, m in zip(parts, masks)]
        sums = [x[:half].astype(F32) + y.astype(F32) for x, y in zip(parts, near)]
        gone = [x[1].astype(BF16) for x in sums]
        far = [partner(x, m[1]) for x, m in zip(gone, masks)]
        packed = after(packed, gone)
        total = [x[0] + y.astype(F32) for x, y in zip(sums, far)]
        total = jnp.concatenate(total, axis=1)
        grad_gate, grad_up = total[0][None], total[1][None]
        grad_down = total[2].reshape(PIECE, ff // PIECE, PIECE).transpose(1, 0, 2)
        grad_down = grad_down.reshape(1, ff, PIECE)
    else:
        blocks = width // PIECE
        (parts,) = weight_blocks(list(saved_a) + list(saved_b), blocks, ff, False)
        part_down = parts[:, 2].reshape(blocks, PIECE, ff // PIECE, PIECE).transpose(0, 2, 1, 3)
        part_down = part_down.reshape(blocks, ff, PIECE // rows_dev, rows_dev)
        part_down = part_down.transpose(0, 2, 1, 3).reshape(ctx_count, ff, rows_dev)
        order = list(range(bits))
        grad_gate, grad_up, grad_down = [
            halved(x.reshape((ctx_count,) + shape), bits, order, ctx)[None]
            for x, shape in (
                (parts[:, 0], (rows_dev, ff)),
                (parts[:, 1], (rows_dev, ff)),
                (part_down, (ff, rows_dev)),
            )
        ]
    layer_out, grad_hidden = restore(where, after(ids_f, grad_gate, grad_up, grad_down), layer_a, change_a, packed, experts, capacity)
    return (layer_out, grad_hidden, grad_gate, grad_up, grad_down)


def solution(mesh):
    in_specs = (
        P(None, "ctx", "exp"),
        P(None, "ctx", None),
        P(None, "ctx", None),
        P("exp", None),
        P(),
        P(("ctx", "exp"), None),
        P(("ctx", "exp"), None),
        P("exp", None, None),
        P("exp", None, None),
        P("exp", None, None),
        P(("ctx", "exp"), None),
    )
    out_specs = (
        P(("ctx", "exp"), None),
        P(("ctx", "exp"), None),
        P("exp", "ctx", None),
        P("exp", "ctx", None),
        P("exp", None, "ctx"),
    )
    return jax.shard_map(
        on_device, mesh=mesh, in_specs=in_specs, out_specs=out_specs, check_vma=False
    )
```
